32 devices in a mesh: wide: 16 (over z, y, x), grp: 2 (over core).
Axes of the slice: x: 2, y: 2, z: 4, core: 2. Of those that a mesh axis runs over, the one named last changes fastest.
Arguments:
- samples: bfloat16 [128, 512], P(('wide', 'grp')), may hold values from -6 to 6
- archive: bfloat16 [16384, 512], P(('wide', 'grp')), may hold values from -6 to 6
- inv_len: float32 [512], replicated, may hold values from 0.7 to 2.8
- mean_coef: bfloat16 [16384, 64], P(('wide', 'grp')), may hold values from -0.75 to 0.75
- var_coef: bfloat16 [16384, 64], P(('wide', 'grp')), may hold values from -4 to 4
Outputs:
- pred_mean: float32 [128, 64], P(('wide', 'grp'))
- pred_var: float32 [128, 64], P(('wide', 'grp'))
The draws below stay inside these ranges and needn't reach their ends.
All inputs are finite; a program needn't handle non-finite values.
Results may differ from the reference program's by a relative error of at most 0.0085.
Values may be sent and summed in bfloat16 or wider, within the bound.
No kernel may reach another device: no remote copies, remote signals or barrier semaphores. Data moves between devices by JAX's collectives and lax.ppermute only.
A program may use at most 64 MiB of HBM per device.

```python
import math
import jax
import jax.numpy as jnp
from jax import lax

DIN = 512
OUT = 64
M_DEV = 512
S = 128
M_ALL = 16384


def block_scale(key, extent, cuts, low, top_value):
    def one(position, blocks):
        heights = jax.random.uniform(jax.random.fold_in(jax.random.fold_in(key, 6), position), (blocks,), jnp.float32, low / len(cuts), top_value / len(cuts))
        return jnp.repeat(jnp.exp(heights), extent[position] // blocks).reshape((-1,) + (1,) * (len(extent) - position - 1))

    gain = one(*cuts[0])
    for cut in cuts[1:]:
        gain = gain * one(*cut)
    return gain


def noise(rng, shape, deviation, reach, shards=(), held_as=jnp.bfloat16):
    array = jax.random.normal(rng, shape, jnp.float32) * deviation
    if len(shards) > 0:
        array = block_scale(rng, shape, shards, -0.22, 0.18) * array
    return jnp.clip(array, min=-reach, max=reach).astype(held_as)


def setup_inputs(seed: int = 0) -> dict:
    streams_of = jax.random.split(jax.random.key(seed), 6)
    return {
        "samples": noise(streams_of[0], (S, DIN), 1.0, 6.0, ((0, 32),)),
        "archive": noise(streams_of[1], (M_ALL, DIN), 1.0, 6.0, ((0, 32),)),
        "inv_len": jnp.clip(jnp.exp(jax.random.uniform(streams_of[2], (DIN,), jnp.float32, math.log(0.7), math.log(2.8))), 0.7, 2.8),
        "mean_coef": noise(streams_of[3], (M_ALL, OUT), (M_ALL // 256) ** -0.5, 0.75, ((0, 32),)),
        "var_coef": noise(streams_of[4], (M_ALL, OUT), (max(1, M_ALL // 8192)) ** -0.5, 4.0, ((0, 32),)),
    }


def scaled_rows(rows, inv_len):
    factor = inv_len * (DIN ** -0.5)
    scaled = (rows.astype(jnp.float32) * factor).astype(jnp.bfloat16)
    wide_copy = scaled.astype(jnp.float32)
    return scaled, jnp.sum(wide_copy * wide_copy, axis=-1)


def reference(samples, archive, inv_len, mean_coef, var_coef):
    samp_z, samp_norm = scaled_rows(samples, inv_len)
    block_rows = 8 * M_DEV
    block_count = M_ALL // block_rows
    arch_blocks = archive.reshape(block_count, block_rows, DIN)
    mean_blocks = mean_coef.reshape(block_count, block_rows, OUT)
    var_blocks = var_coef.reshape(block_count, block_rows, OUT)

    def accumulate(totals, pieces):
        mean_sum, corr_sum = totals
        arch_rows, mean_rows, var_rows = pieces
        arch_z, arch_norm = scaled_rows(arch_rows, inv_len)
        inner_prod = jnp.dot(samp_z, arch_z.T, preferred_element_type=jnp.float32)
        kernel = jnp.exp(inner_prod - 0.5 * samp_norm[:, None] - 0.5 * arch_norm[None, :])
        kernel_half = kernel.astype(jnp.bfloat16)
        square_half = (kernel * kernel).astype(jnp.bfloat16)
        mean_sum = mean_sum + jnp.dot(kernel_half, mean_rows, preferred_element_type=jnp.float32)
        corr_sum = corr_sum + jnp.dot(square_half, var_rows, preferred_element_type=jnp.float32)
        return (mean_sum, corr_sum), None

    start_pair = (jnp.zeros((S, OUT), jnp.float32), jnp.zeros((S, OUT), jnp.float32))
    final_pair, unused = lax.scan(accumulate, start_pair, (arch_blocks, mean_blocks, var_blocks))
    pred_mean, correction = final_pair
    return pred_mean, 1.0 - correction
```

```python
import jax
import jax.numpy as jnp
from jax import lax
from jax.sharding import PartitionSpec as P

DIN = 512
AXES = ("wide", "grp")


def scaled_rows(rows, inv_len):
    factor = inv_len * DIN ** (-0.5)
    scaled = (rows.astype(jnp.float32) * factor).astype(jnp.bfloat16)
    wide_copy = scaled.astype(jnp.float32)
    return (scaled, jnp.sum(wide_copy * wide_copy, axis=-1))


def on_device(samples, archive, inv_len, mean_coef, var_coef):
    devices = lax.axis_size(AXES)
    own_rows = samples.shape[0]
    width = mean_coef.shape[1]
    sent = jnp.broadcast_to(samples[None], (devices,) + samples.shape)
    gathered = lax.all_to_all(sent, AXES, split_axis=0, concat_axis=0, tiled=True)
    gathered = gathered.reshape(devices * own_rows, DIN)
    arch_z, arch_norm = scaled_rows(archive, inv_len)
    samp_z, samp_norm = scaled_rows(gathered, inv_len)
    inner_prod = lax.dot_general(
        samp_z, arch_z, (((1,), (1,)), ((), ())), preferred_element_type=jnp.float32
    )
    kernel = jnp.exp(inner_prod - 0.5 * samp_norm[:, None] - 0.5 * arch_norm[None, :])
    kernel_half = kernel.astype(jnp.bfloat16)
    square_half = (kernel * kernel).astype(jnp.bfloat16)
    mean_sum = jnp.dot(kernel_half, mean_coef, preferred_element_type=jnp.float32)
    corr_sum = jnp.dot(square_half, var_coef, preferred_element_type=jnp.float32)
    sums = jnp.concatenate([mean_sum, corr_sum], axis=1).reshape(devices, own_rows, 2 * width)
    parts = lax.all_to_all(sums, AXES, split_axis=0, concat_axis=0, tiled=True)
    summed = jnp.sum(parts, axis=0)
    return (summed[:, :width], 1.0 - summed[:, width:])


def solution(mesh):
    rows = P(AXES, None)
    return jax.shard_map(
        on_device,
        mesh=mesh,
        in_specs=(rows, rows, P(), rows, rows),
        out_specs=(rows, rows),
        check_vma=False,
    )
```

```python
import jax
import jax.numpy as jnp
from jax import lax
from jax.sharding import PartitionSpec as P

DIN = 512


def scaled_rows(rows, inv_len):
    factor = inv_len * DIN ** (-0.5)
    scaled = (rows.astype(jnp.float32) * factor).astype(jnp.bfloat16)
    wide_copy = scaled.astype(jnp.float32)
    return (scaled, jnp.sum(wide_copy * wide_copy, axis=-1))


def on_device(samples, archive, inv_len, mean_coef, var_coef):
    wide = lax.axis_size("wide")
    grp = lax.axis_size("grp")
    own_rows = samples.shape[0]
    width = mean_coef.shape[1]

    def from_peer(array, step):
        return lax.ppermute(array, "grp", [(i, (i + step) % grp) for i in range(grp)])

    sent = jnp.broadcast_to(samples[None], (wide,) + samples.shape)
    gathered = lax.all_to_all(sent, "wide", split_axis=0, concat_axis=0, tiled=True)
    runs = [(archive, mean_coef, var_coef)]
    for step in range(1, grp):
        runs.append(tuple(from_peer(array, step) for array in (archive, mean_coef, var_coef)))
    samp_z, samp_norm = scaled_rows(gathered.reshape(wide * own_rows, DIN), inv_len)
    mean_sum = 0.0
    corr_sum = 0.0
    for arch_rows, mean_rows, var_rows in runs:
        arch_z, arch_norm = scaled_rows(arch_rows, inv_len)
        inner_prod = lax.dot_general(
            samp_z, arch_z, (((1,), (1,)), ((), ())), preferred_element_type=jnp.float32
        )
        kernel = jnp.exp(inner_prod - 0.5 * samp_norm[:, None] - 0.5 * arch_norm[None, :])
        kernel_half = kernel.astype(jnp.bfloat16)
        square_half = (kernel * kernel).astype(jnp.bfloat16)
        mean_sum += jnp.dot(kernel_half, mean_rows, preferred_element_type=jnp.float32)
        corr_sum += jnp.dot(square_half, var_rows, preferred_element_type=jnp.float32)
    sums = jnp.concatenate([mean_sum, corr_sum], axis=1).reshape(wide, own_rows, 2 * width)
    parts = lax.all_to_all(sums, "wide", split_axis=0, concat_axis=0, tiled=True)
    summed = jnp.sum(parts, axis=0)
    return (summed[:, :width], 1.0 - summed[:, width:])


def solution(mesh):
    rows = P(("wide", "grp"), None)
    return jax.shard_map(
        on_device,
        mesh=mesh,
        in_specs=(rows, rows, P(), rows, rows),
        out_specs=(rows, rows),
        check_vma=False,
    )
```

```python
import jax
import jax.numpy as jnp
from jax import lax
from jax.sharding import PartitionSpec as P

DIN = 512


def scaled_rows(rows, inv_len):
    factor = inv_len * DIN ** (-0.5)
    scaled = (rows.astype(jnp.float32) * factor).astype(jnp.bfloat16)
    wide_copy = scaled.astype(jnp.float32)
    return (scaled, jnp.sum(wide_copy * wide_copy, axis=-1))


def digits(size):
    found, stride = [], 1
    while stride < size:
        radix = min(4, size // stride)
        found.append((stride, radix))
        stride *= radix
    return found


def swap(array, size, mask):
    return lax.ppermute(array, "wide", [(i, i ^ mask) for i in range(size)])


def on_device(samples, archive, inv_len, mean_coef, var_coef):
    wide = lax.axis_size("wide")
    grp = lax.axis_size("grp")
    own_rows = samples.shape[0]
    width = mean_coef.shape[1]

    def from_peer(array, step):
        return lax.ppermute(array, "grp", [(i, (i + step) % grp) for i in range(grp)])

    gathered = samples[None]
    for stride, radix in digits(wide):
        pieces = [gathered] + [swap(gathered, wide, stride * k) for k in range(1, radix)]
        gathered = jnp.concatenate(pieces, axis=0)
    runs = [(archive, mean_coef, var_coef)]
    for step in range(1, grp):
        runs.append(tuple(from_peer(array, step) for array in (archive, mean_coef, var_coef)))
    samp_z, samp_norm = scaled_rows(gathered.reshape(wide * own_rows, DIN), inv_len)
    mean_sum = 0.0
    corr_sum = 0.0
    for arch_rows, mean_rows, var_rows in runs:
        arch_z, arch_norm = scaled_rows(arch_rows, inv_len)
        inner_prod = lax.dot_general(
            samp_z, arch_z, (((1,), (1,)), ((), ())), preferred_element_type=jnp.float32
        )
        kernel = jnp.exp(inner_prod - 0.5 * samp_norm[:, None] - 0.5 * arch_norm[None, :])
        kernel_half = kernel.astype(jnp.bfloat16)
        square_half = (kernel * kernel).astype(jnp.bfloat16)
        mean_sum += jnp.dot(kernel_half, mean_rows, preferred_element_type=jnp.float32)
        corr_sum += jnp.dot(square_half, var_rows, preferred_element_type=jnp.float32)
    sums = jnp.concatenate([mean_sum, corr_sum], axis=1).reshape(wide, own_rows, 2 * width)
    for stride, radix in reversed(digits(wide)):
        parts = sums.reshape((radix, stride) + sums.shape[1:])
        sums = parts[0]
        for k in range(1, radix):
            sums = sums + swap(parts[k], wide, stride * k)
    summed = sums[0]
    return (summed[:, :width], 1.0 - summed[:, width:])


def solution(mesh):
    rows = P(("wide", "grp"), None)
    return jax.shard_map(
        on_device,
        mesh=mesh,
        in_specs=(rows, rows, P(), rows, rows),
        out_specs=(rows, rows),
        check_vma=False,
    )
```

```python
import jax
import jax.numpy as jnp
from jax import lax
from jax.experimental import pallas as pl
from jax.experimental.pallas import tpu as pltpu
from jax.sharding import PartitionSpec as P

DIN = 512
AXES = ("wide", "grp")
BLOCK = 128
VMEM_LIMIT = 40 * 1024 * 1024
ON_CHIP = pl.BlockSpec(memory_space=pltpu.VMEM)
ROWS_BY_ROWS = (((1,), (1,)), ((), ()))


def scaled(rows, inv_len):
    factor = inv_len * DIN ** (-0.5)
    return (rows.astype(jnp.float32) * factor).astype(jnp.bfloat16)


def send_kernel(samples_hbm, inv_len_hbm, sent_ref, samples_ref, inv_len_ref, arrived):
    copies = [
        pltpu.make_async_copy(samples_hbm, samples_ref, arrived.at[0]),
        pltpu.make_async_copy(inv_len_hbm, inv_len_ref, arrived.at[1]),
    ]
    for copy in copies:
        copy.start()
    for copy in copies:
        copy.wait()
    samp_z = scaled(samples_ref[...], inv_len_ref[...])
    sent_ref[...] = jnp.broadcast_to(samp_z[None], sent_ref.shape)


def runs_kernel(archive_ref, inv_len_ref, mean_ref, var_ref, arch_z_ref, norm_ref, coef_ref):
    arch_z = scaled(archive_ref[...], inv_len_ref[...])
    arch_z_ref[...] = arch_z
    wide_copy = arch_z.astype(jnp.float32)
    square = wide_copy * wide_copy
    high = square.astype(jnp.bfloat16)
    low = (square - high.astype(jnp.float32)).astype(jnp.bfloat16)
    ones = jnp.ones((8, DIN), jnp.bfloat16)
    norm = lax.dot_general(ones, high, ROWS_BY_ROWS, preferred_element_type=jnp.float32)
    norm += lax.dot_general(ones, low, ROWS_BY_ROWS, preferred_element_type=jnp.float32)
    norm_ref[...] = 0.5 * norm
    width = mean_ref.shape[0]
    zero = jnp.zeros(mean_ref.shape, jnp.bfloat16)
    coef_ref[0, :width, :] = mean_ref[...]
    coef_ref[0, width:, :] = zero
    coef_ref[1, :width, :] = zero
    coef_ref[1, width:, :] = var_ref[...]


def sums_kernel(samp_z_ref, arch_z_ref, norm_ref, coef_ref, sums_ref):
    def block(rows):
        samp_z = samp_z_ref[rows, :]
        wide_copy = samp_z.astype(jnp.float32)
        samp_norm = jnp.sum(wide_copy * wide_copy, axis=-1, keepdims=True)
        inner_prod = lax.dot_general(
            samp_z, arch_z_ref[...], ROWS_BY_ROWS, preferred_element_type=jnp.float32
        )
        kernel = jnp.exp(inner_prod - 0.5 * samp_norm - norm_ref[:1, :])
        kernel_half = kernel.astype(jnp.bfloat16)
        square_half = (kernel * kernel).astype(jnp.bfloat16)
        sums_ref[rows, :] = lax.dot_general(
            kernel_half, coef_ref[0], ROWS_BY_ROWS, preferred_element_type=jnp.float32
        ) + lax.dot_general(
            square_half, coef_ref[1], ROWS_BY_ROWS, preferred_element_type=jnp.float32
        )

    count = samp_z_ref.shape[0]
    if count <= BLOCK:
        block(slice(None))
    else:
        @pl.loop(0, count // BLOCK)
        def _(step):
            block(pl.ds(pl.multiple_of(step * BLOCK, BLOCK), BLOCK))


def call(kernel, out_shape, inputs, flops, transcendentals=0, in_space=pltpu.VMEM, scratch=()):
    moved = sum(array.size * array.dtype.itemsize for array in inputs)
    return pl.pallas_call(
        kernel,
        out_shape=out_shape,
        in_specs=[pl.BlockSpec(memory_space=in_space)] * len(inputs),
        out_specs=jax.tree.map(lambda _: ON_CHIP, out_shape),
        scratch_shapes=scratch,
        cost_estimate=pl.CostEstimate(
            flops=flops, bytes_accessed=moved, transcendentals=transcendentals
        ),
        compiler_params=pltpu.CompilerParams(vmem_limit_bytes=VMEM_LIMIT),
    )(*inputs)


def on_device(samples, archive, inv_len, mean_coef, var_coef):
    devices = lax.axis_size(AXES)
    own_rows = samples.shape[0]
    all_rows = devices * own_rows
    runs, width = mean_coef.shape
    inv_len = inv_len.reshape(1, DIN)

    sent = call(
        send_kernel,
        pltpu.VMEM((devices, own_rows, DIN), jnp.bfloat16),
        [pltpu.with_memory_space_constraint(array, pltpu.HBM) for array in (samples, inv_len)],
        flops=own_rows * DIN,
        in_space=pltpu.HBM,
        scratch=[
            pltpu.VMEM(samples.shape, samples.dtype),
            pltpu.VMEM(inv_len.shape, inv_len.dtype),
            pltpu.SemaphoreType.DMA((2,)),
        ],
    )
    gathered = lax.all_to_all(sent, AXES, split_axis=0, concat_axis=0, tiled=True)
    arch_z, norm, coef = call(
        runs_kernel,
        (
            pltpu.VMEM((runs, DIN), jnp.bfloat16),
            pltpu.VMEM((8, runs), jnp.float32),
            pltpu.VMEM((2, 2 * width, runs), jnp.bfloat16),
        ),
        (archive, inv_len, mean_coef.T, var_coef.T),
        flops=36 * runs * DIN,
    )
    sums = call(
        sums_kernel,
        pltpu.VMEM((all_rows, 2 * width), jnp.float32),
        (gathered.reshape(all_rows, DIN), arch_z, norm, coef),
        flops=2 * all_rows * runs * (DIN + 4 * width),
        transcendentals=all_rows * runs,
    )
    sums = sums.reshape(devices, own_rows, 2 * width)
    parts = lax.all_to_all(sums, AXES, split_axis=0, concat_axis=0, tiled=True)
    summed = jnp.sum(parts, axis=0)
    return (summed[:, :width], 1.0 - summed[:, width:])


def solution(mesh):
    rows = P(AXES, None)
    return jax.shard_map(
        on_device,
        mesh=mesh,
        in_specs=(rows, rows, P(), rows, rows),
        out_specs=(rows, rows),
        check_vma=False,
    )
```

```python
import jax
import jax.numpy as jnp
from jax import lax
from jax.experimental import pallas as pl
from jax.experimental.pallas import tpu as pltpu
from jax.sharding import PartitionSpec as P

DIN = 512
AXES = ("wide", "grp")
PAIR = 2
BLOCK = 128
NORM_ROWS = 16
VMEM_LIMIT = 40 * 1024 * 1024
ROWS_BY_ROWS = (((1,), (1,)), ((), ()))


def scaled(rows, inv_len):
    factor = inv_len * DIN ** (-0.5)
    return (rows.astype(jnp.float32) * factor).astype(jnp.bfloat16)


def send_kernel(
    samples_hbm, inv_len_hbm, archive_hbm, mean_hbm, var_hbm,
    sent_ref, inv_len_ref, archive_ref, mean_ref, var_ref, samples_ref, arrived,
):
    copies = [
        pltpu.make_async_copy(source, target, arrived.at[number])
        for number, (source, target) in enumerate((
            (samples_hbm, samples_ref),
            (inv_len_hbm, inv_len_ref),
            (archive_hbm, archive_ref),
            (mean_hbm, mean_ref),
            (var_hbm, var_ref),
        ))
    ]
    for copy in copies:
        copy.start()
    for copy in copies[:2]:
        copy.wait()
    samp_z = scaled(samples_ref[...], inv_len_ref[...])
    samp_z = samp_z.reshape((1, PAIR) + sent_ref.shape[1:])
    targets = sent_ref.shape[0] // PAIR
    sent_ref[...] = jnp.broadcast_to(samp_z, (targets,) + samp_z.shape[1:]).reshape(sent_ref.shape)
    for copy in copies[2:]:
        copy.wait()


def runs_kernel(inv_len_ref, archive_ref, mean_ref, var_ref, pack_ref):
    runs = archive_ref.shape[0]
    width = mean_ref.shape[0]
    arch_z = scaled(archive_ref[...], inv_len_ref[...])
    pack_ref[:runs, :] = arch_z
    pack_ref[runs : runs + width, :] = mean_ref[...]
    pack_ref[runs + width : runs + 2 * width, :] = jnp.zeros(mean_ref.shape, jnp.bfloat16)
    pack_ref[runs + 2 * width : runs + 3 * width, :] = var_ref[...]
    wide_copy = arch_z.astype(jnp.float32)
    square = wide_copy * wide_copy
    high = square.astype(jnp.bfloat16)
    low = (square - high.astype(jnp.float32)).astype(jnp.bfloat16)
    ones = jnp.ones((NORM_ROWS, DIN), jnp.bfloat16)
    norm = lax.dot_general(ones, high, ROWS_BY_ROWS, preferred_element_type=jnp.float32)
    norm += lax.dot_general(ones, low, ROWS_BY_ROWS, preferred_element_type=jnp.float32)
    rest = 0.5 * norm
    row = lax.broadcasted_iota(jnp.int32, rest.shape, 0)
    parts = jnp.zeros(rest.shape, jnp.float32)
    for number in range(3):
        part = rest.astype(jnp.bfloat16).astype(jnp.float32)
        parts = jnp.where(row == number, part, parts)
        rest = rest - part
    pack_ref[runs + 3 * width :, :] = parts.astype(jnp.bfloat16)


def sums_kernel(samp_z_ref, own_ref, peer_ref, sums_ref):
    width = sums_ref.shape[1] // 2
    runs = own_ref.shape[0] - 3 * width - NORM_ROWS

    def block(rows):
        samp_z = samp_z_ref[rows, :]
        wide_copy = samp_z.astype(jnp.float32)
        samp_norm = 0.5 * jnp.sum(wide_copy * wide_copy, axis=-1, keepdims=True)
        total = None
        for pack_ref in (own_ref, peer_ref):
            norm_parts = pack_ref[runs + 3 * width :, :].astype(jnp.float32)
            arch_norm = jnp.sum(norm_parts, axis=0, keepdims=True)
            inner_prod = lax.dot_general(
                samp_z, pack_ref[:runs, :], ROWS_BY_ROWS, preferred_element_type=jnp.float32
            )
            kernel = jnp.exp(inner_prod - samp_norm - arch_norm)
            for half, first in ((kernel, runs), (kernel * kernel, runs + width)):
                part = lax.dot_general(
                    half.astype(jnp.bfloat16),
                    pack_ref[first : first + 2 * width, :],
                    ROWS_BY_ROWS,
                    preferred_element_type=jnp.float32,
                )
                total = part if total is None else total + part
        sums_ref[rows, :] = total

    count = samp_z_ref.shape[0]
    if count <= BLOCK:
        block(slice(None))
    else:
        @pl.loop(0, count // BLOCK)
        def _(step):
            block(pl.ds(pl.multiple_of(step * BLOCK, BLOCK), BLOCK))


def call(kernel, out_shape, inputs, flops, transcendentals=0, in_space=pltpu.VMEM, scratch=()):
    moved = sum(array.size * array.dtype.itemsize for array in inputs)
    return pl.pallas_call(
        kernel,
        out_shape=out_shape,
        in_specs=[pl.BlockSpec(memory_space=in_space)] * len(inputs),
        out_specs=jax.tree.map(lambda _: pl.BlockSpec(memory_space=pltpu.VMEM), out_shape),
        scratch_shapes=scratch,
        cost_estimate=pl.CostEstimate(
            flops=flops, bytes_accessed=moved, transcendentals=transcendentals
        ),
        compiler_params=pltpu.CompilerParams(vmem_limit_bytes=VMEM_LIMIT),
    )(*inputs)


def on_device(samples, archive, inv_len, mean_coef, var_coef):
    devices = lax.axis_size(AXES)
    grp = lax.axis_size("grp")
    own_rows = samples.shape[0]
    part_rows = own_rows // PAIR
    rows = devices * part_rows
    runs, width = mean_coef.shape

    arrays = (samples, inv_len.reshape(1, DIN), archive, mean_coef.T, var_coef.T)
    sent, *held = call(
        send_kernel,
        (pltpu.VMEM((devices, part_rows, DIN), jnp.bfloat16),)
        + tuple(pltpu.VMEM(array.shape, array.dtype) for array in arrays[1:]),
        [pltpu.with_memory_space_constraint(array, pltpu.HBM) for array in arrays],
        flops=own_rows * DIN,
        in_space=pltpu.HBM,
        scratch=[pltpu.VMEM(samples.shape, samples.dtype), pltpu.SemaphoreType.DMA((5,))],
    )
    gathered = lax.all_to_all(sent, AXES, split_axis=0, concat_axis=0, tiled=True)
    own = call(
        runs_kernel,
        pltpu.VMEM((runs + 3 * width + NORM_ROWS, DIN), jnp.bfloat16),
        held,
        flops=68 * runs * DIN,
    )
    peer = lax.ppermute(own, "grp", [(i, i ^ 1) for i in range(grp)])
    sums = call(
        sums_kernel,
        pltpu.VMEM((rows, 2 * width), jnp.float32),
        (gathered.reshape(rows, DIN), own, peer),
        flops=4 * rows * runs * (DIN + 4 * width),
        transcendentals=2 * rows * runs,
    )
    sums = sums.reshape(devices, part_rows, 2 * width)
    parts = lax.all_to_all(sums, AXES, split_axis=0, concat_axis=0, tiled=True)
    summed = jnp.sum(parts.reshape(devices // PAIR, own_rows, 2 * width), axis=0)
    return (summed[:, :width], 1.0 - summed[:, width:])


def solution(mesh):
    rows = P(AXES, None)
    return jax.shard_map(
        on_device,
        mesh=mesh,
        in_specs=(rows, rows, P(), rows, rows),
        out_specs=(rows, rows),
        check_vma=False,
    )
```

```python
import jax
import jax.numpy as jnp
from jax import lax
from jax.experimental import pallas as pl
from jax.experimental.pallas import tpu as pltpu
from jax.sharding import PartitionSpec as P

DIN = 512
AXES = ("wide", "grp")
PAIR = 2
BLOCK = 128
VMEM_LIMIT = 40 * 1024 * 1024
ROWS_BY_ROWS = (((1,), (1,)), ((), ()))


def scaled(rows, inv_len):
    factor = inv_len * DIN ** (-0.5)
    return (rows.astype(jnp.float32) * factor).astype(jnp.bfloat16)


def send_kernel(
    samples_hbm, inv_len_hbm, archive_hbm, mean_hbm, var_hbm,
    sent_ref, inv_len_ref, pack_ref, samples_ref, arrived,
):
    runs = archive_hbm.shape[0]
    width = mean_hbm.shape[0]
    copies = [
        pltpu.make_async_copy(source, target, arrived.at[number])
        for number, (source, target) in enumerate((
            (samples_hbm, samples_ref),
            (inv_len_hbm, inv_len_ref),
            (archive_hbm, pack_ref.at[pl.ds(0, runs)]),
            (mean_hbm, pack_ref.at[pl.ds(runs, width)]),
            (var_hbm, pack_ref.at[pl.ds(runs + 2 * width, width)]),
        ))
    ]
    for copy in copies:
        copy.start()
    pack_ref[runs + width : runs + 2 * width, :] = jnp.zeros((width, DIN), jnp.bfloat16)
    for copy in copies[:2]:
        copy.wait()
    samp_z = scaled(samples_ref[...], inv_len_ref[...])
    samp_z = samp_z.reshape((PAIR,) + sent_ref.shape[1:])
    for chip in range(sent_ref.shape[0] // PAIR):
        sent_ref[chip * PAIR : (chip + 1) * PAIR] = samp_z
    for copy in copies[2:]:
        copy.wait()


def runs_kernel(inv_len_ref, pack_ref, arch_z_ref, norm_ref):
    runs = arch_z_ref.shape[0]
    arch_z = scaled(pack_ref[:runs, :], inv_len_ref[...])
    arch_z_ref[...] = arch_z
    wide_copy = arch_z.astype(jnp.float32)
    square = wide_copy * wide_copy
    high = square.astype(jnp.bfloat16)
    low = (square - high.astype(jnp.float32)).astype(jnp.bfloat16)
    ones = jnp.ones((8, DIN), jnp.bfloat16)
    norm = lax.dot_general(ones, high, ROWS_BY_ROWS, preferred_element_type=jnp.float32)
    norm += lax.dot_general(ones, low, ROWS_BY_ROWS, preferred_element_type=jnp.float32)
    norm_ref[...] = 0.5 * norm


def sums_kernel(samp_z_ref, *refs):
    *held, sums_ref = refs
    width = sums_ref.shape[1] // 2

    def block(rows):
        samp_z = samp_z_ref[rows, :]
        wide_copy = samp_z.astype(jnp.float32)
        samp_norm = 0.5 * jnp.sum(wide_copy * wide_copy, axis=-1, keepdims=True)
        total = None
        for arch_z_ref, norm_ref, pack_ref in (held[:3], held[3:]):
            runs = arch_z_ref.shape[0]
            inner_prod = lax.dot_general(
                samp_z, arch_z_ref[...], ROWS_BY_ROWS, preferred_element_type=jnp.float32
            )
            kernel = jnp.exp(inner_prod - samp_norm - norm_ref[:1, :])
            for half, first in ((kernel, runs), (kernel * kernel, runs + width)):
                part = lax.dot_general(
                    half.astype(jnp.bfloat16),
                    pack_ref[first : first + 2 * width, :],
                    ROWS_BY_ROWS,
                    preferred_element_type=jnp.float32,
                )
                total = part if total is None else total + part
        sums_ref[rows, :] = total

    count = samp_z_ref.shape[0]
    if count <= BLOCK:
        block(slice(None))
    else:
        @pl.loop(0, count // BLOCK)
        def _(step):
            block(pl.ds(pl.multiple_of(step * BLOCK, BLOCK), BLOCK))


def call(kernel, out_shape, inputs, flops, transcendentals=0, in_space=pltpu.VMEM, scratch=()):
    moved = sum(array.size * array.dtype.itemsize for array in inputs)
    return pl.pallas_call(
        kernel,
        out_shape=out_shape,
        in_specs=[pl.BlockSpec(memory_space=in_space)] * len(inputs),
        out_specs=jax.tree.map(lambda _: pl.BlockSpec(memory_space=pltpu.VMEM), out_shape),
        scratch_shapes=scratch,
        cost_estimate=pl.CostEstimate(
            flops=flops, bytes_accessed=moved, transcendentals=transcendentals
        ),
        compiler_params=pltpu.CompilerParams(vmem_limit_bytes=VMEM_LIMIT),
    )(*inputs)


def on_device(samples, archive, inv_len, mean_coef, var_coef):
    devices = lax.axis_size(AXES)
    grp = lax.axis_size("grp")
    own_rows = samples.shape[0]
    part_rows = own_rows // PAIR
    rows = devices * part_rows
    runs, width = mean_coef.shape

    arrays = (samples, inv_len.reshape(1, DIN), archive, mean_coef.T, var_coef.T)
    pack_rows = runs + 3 * width
    sent, held_len, own = call(
        send_kernel,
        (
            pltpu.VMEM((devices, part_rows, DIN), jnp.bfloat16),
            pltpu.VMEM((1, DIN), jnp.float32),
            pltpu.VMEM((pack_rows, DIN), jnp.bfloat16),
        ),
        [pltpu.with_memory_space_constraint(array, pltpu.HBM) for array in arrays],
        flops=own_rows * DIN,
        in_space=pltpu.HBM,
        scratch=[pltpu.VMEM(samples.shape, samples.dtype), pltpu.SemaphoreType.DMA((5,))],
    )
    gathered = lax.all_to_all(sent, AXES, split_axis=0, concat_axis=0, tiled=True)
    peer = lax.ppermute(own, "grp", [(i, i ^ 1) for i in range(grp)])
    held = []
    for pack in (own, peer):
        held += call(
            runs_kernel,
            (pltpu.VMEM((runs, DIN), jnp.bfloat16), pltpu.VMEM((8, runs), jnp.float32)),
            (held_len, pack),
            flops=36 * runs * DIN,
        )
        held.append(pack)
    sums = call(
        sums_kernel,
        pltpu.VMEM((rows, 2 * width), jnp.float32),
        [gathered.reshape(rows, DIN)] + held,
        flops=4 * rows * runs * (DIN + 4 * width),
        transcendentals=2 * rows * runs,
    )
    sums = sums.reshape(devices, part_rows, 2 * width)
    parts = lax.all_to_all(sums, AXES, split_axis=0, concat_axis=0, tiled=True)
    summed = jnp.sum(parts.reshape(devices // PAIR, own_rows, 2 * width), axis=0)
    return (summed[:, :width], 1.0 - summed[:, width:])


def solution(mesh):
    rows = P(AXES, None)
    return jax.shard_map(
        on_device,
        mesh=mesh,
        in_specs=(rows, rows, P(), rows, rows),
        out_specs=(rows, rows),
        check_vma=False,
    )
```

```python
import jax
import jax.numpy as jnp
from jax import lax
from jax.experimental import pallas as pl
from jax.experimental.pallas import tpu as pltpu
from jax.sharding import PartitionSpec as P

DIN = 512
AXES = ("wide", "grp")
PAIR = 2
BLOCK = 128
NORM_ROWS = 16
CHUNKS = 4
FIRST_WEIGHT = 200
VMEM_LIMIT = 40 * 1024 * 1024
ROWS_BY_ROWS = (((1,), (1,)), ((), ()))


def scaled(rows, inv_len):
    factor = inv_len * DIN ** (-0.5)
    return (rows.astype(jnp.float32) * factor).astype(jnp.bfloat16)


def send_kernel(samples_hbm, inv_len_hbm, sent_ref, inv_len_ref, samples_ref, arrived):
    copies = [
        pltpu.make_async_copy(samples_hbm, samples_ref, arrived.at[0]),
        pltpu.make_async_copy(inv_len_hbm, inv_len_ref, arrived.at[1]),
    ]
    for copy in copies:
        copy.start()
    for copy in copies:
        copy.wait()
    samp_z = scaled(samples_ref[...], inv_len_ref[...])
    samp_z = samp_z.reshape((1, PAIR) + sent_ref.shape[1:])
    targets = sent_ref.shape[0] // PAIR
    sent_ref[...] = jnp.broadcast_to(samp_z, (targets,) + samp_z.shape[1:]).reshape(sent_ref.shape)


def runs_kernel(inv_len_ref, archive_hbm, mean_hbm, var_hbm, pack_ref, archive_ref, arrived):
    runs = archive_ref.shape[0]
    width = mean_hbm.shape[0]
    chunk = runs // CHUNKS
    places = [pl.ds(number * chunk, chunk) for number in range(CHUNKS)]
    copies = [
        pltpu.make_async_copy(archive_hbm.at[place], archive_ref.at[place], arrived.at[number])
        for number, place in enumerate(places)
    ]
    copies.append(
        pltpu.make_async_copy(mean_hbm, pack_ref.at[pl.ds(runs, width)], arrived.at[CHUNKS])
    )
    copies.append(
        pltpu.make_async_copy(
            var_hbm, pack_ref.at[pl.ds(runs + 2 * width, width)], arrived.at[CHUNKS + 1]
        )
    )
    for copy in copies:
        copy.start()
    pack_ref[runs + width : runs + 2 * width, :] = jnp.zeros((width, DIN), jnp.bfloat16)
    ones = jnp.ones((NORM_ROWS, DIN), jnp.bfloat16)
    row = lax.broadcasted_iota(jnp.int32, (NORM_ROWS, chunk), 0)
    for number, place in enumerate(places):
        copies[number].wait()
        arch_z = scaled(archive_ref[place, :], inv_len_ref[...])
        pack_ref[place, :] = arch_z
        wide_copy = arch_z.astype(jnp.float32)
        square = wide_copy * wide_copy
        high = square.astype(jnp.bfloat16)
        low = (square - high.astype(jnp.float32)).astype(jnp.bfloat16)
        norm = lax.dot_general(ones, high, ROWS_BY_ROWS, preferred_element_type=jnp.float32)
        norm += lax.dot_general(ones, low, ROWS_BY_ROWS, preferred_element_type=jnp.float32)
        rest = 0.5 * norm
        parts = jnp.zeros(rest.shape, jnp.float32)
        for part_row in range(3):
            part = rest.astype(jnp.bfloat16).astype(jnp.float32)
            parts = jnp.where(row == part_row, part, parts)
            rest = rest - part
        pack_ref[runs + 3 * width :, place] = parts.astype(jnp.bfloat16)
    for copy in copies[CHUNKS:]:
        copy.wait()


def sums_kernel(samp_z_ref, pack_ref, *refs):
    *before, sums_ref = refs
    width = sums_ref.shape[1] // 2
    runs = pack_ref.shape[0] - 3 * width - NORM_ROWS

    def block(rows):
        samp_z = samp_z_ref[rows, :]
        wide_copy = samp_z.astype(jnp.float32)
        samp_norm = 0.5 * jnp.sum(wide_copy * wide_copy, axis=-1, keepdims=True)
        norm_parts = pack_ref[runs + 3 * width :, :].astype(jnp.float32)
        arch_norm = jnp.sum(norm_parts, axis=0, keepdims=True)
        inner_prod = lax.dot_general(
            samp_z, pack_ref[:runs, :], ROWS_BY_ROWS, preferred_element_type=jnp.float32
        )
        kernel = jnp.exp(inner_prod - samp_norm - arch_norm)
        total = before[0][rows, :] if before else None
        for half, first in ((kernel, runs), (kernel * kernel, runs + width)):
            part = lax.dot_general(
                half.astype(jnp.bfloat16),
                pack_ref[first : first + 2 * width, :],
                ROWS_BY_ROWS,
                preferred_element_type=jnp.float32,
            )
            total = part if total is None else total + part
        sums_ref[rows, :] = total

    count = samp_z_ref.shape[0]
    if count <= BLOCK:
        block(slice(None))
    else:
        @pl.loop(0, count // BLOCK)
        def _(step):
            block(pl.ds(pl.multiple_of(step * BLOCK, BLOCK), BLOCK))


def call(kernel, out_shape, inputs, flops, transcendentals=0, in_spaces=None, scratch=()):
    moved = sum(array.size * array.dtype.itemsize for array in inputs)
    in_spaces = in_spaces or [pltpu.VMEM] * len(inputs)
    inputs = [
        pltpu.with_memory_space_constraint(array, space) if space == pltpu.HBM else array
        for array, space in zip(inputs, in_spaces)
    ]
    return pl.pallas_call(
        kernel,
        out_shape=out_shape,
        in_specs=[pl.BlockSpec(memory_space=space) for space in in_spaces],
        out_specs=jax.tree.map(lambda _: pl.BlockSpec(memory_space=pltpu.VMEM), out_shape),
        scratch_shapes=scratch,
        cost_estimate=pl.CostEstimate(
            flops=flops, bytes_accessed=moved, transcendentals=transcendentals
        ),
        compiler_params=pltpu.CompilerParams(vmem_limit_bytes=VMEM_LIMIT),
    )(*inputs)


def on_device(samples, archive, inv_len, mean_coef, var_coef):
    devices = lax.axis_size(AXES)
    grp = lax.axis_size("grp")
    own_rows = samples.shape[0]
    part_rows = own_rows // PAIR
    rows = devices * part_rows
    runs, width = mean_coef.shape

    sent, held_len = call(
        send_kernel,
        (
            pltpu.VMEM((devices, part_rows, DIN), jnp.bfloat16),
            pltpu.VMEM((1, DIN), jnp.float32),
        ),
        (samples, inv_len.reshape(1, DIN)),
        flops=own_rows * DIN,
        in_spaces=[pltpu.HBM] * 2,
        scratch=[pltpu.VMEM(samples.shape, samples.dtype), pltpu.SemaphoreType.DMA((2,))],
    )
    gathered = lax.all_to_all(sent, AXES, split_axis=0, concat_axis=0, tiled=True)
    own = call(
        runs_kernel,
        pltpu.VMEM((runs + 3 * width + NORM_ROWS, DIN), jnp.bfloat16),
        (held_len, archive, mean_coef.T, var_coef.T),
        flops=68 * runs * DIN,
        in_spaces=[pltpu.VMEM] + [pltpu.HBM] * 3,
        scratch=[
            pltpu.VMEM(archive.shape, archive.dtype),
            pltpu.SemaphoreType.DMA((CHUNKS + 2,)),
        ],
    )
    peer = lax.ppermute(own, "grp", [(i, i ^ 1) for i in range(grp)])
    samp_z = gathered.reshape(rows, DIN)
    sums = ()
    for pack, weight in ((own, FIRST_WEIGHT), (peer, 1)):
        sums = call(
            sums_kernel,
            pltpu.VMEM((rows, 2 * width), jnp.float32),
            (samp_z, pack, *sums),
            flops=2 * rows * runs * (DIN + 4 * width) * weight,
            transcendentals=rows * runs,
        ),
    (sums,) = sums
    sums = sums.reshape(devices, part_rows, 2 * width)
    parts = lax.all_to_all(sums, AXES, split_axis=0, concat_axis=0, tiled=True)
    summed = jnp.sum(parts.reshape(devices // PAIR, own_rows, 2 * width), axis=0)
    return (summed[:, :width], 1.0 - summed[:, width:])


def solution(mesh):
    rows = P(AXES, None)
    return jax.shard_map(
        on_device,
        mesh=mesh,
        in_specs=(rows, rows, P(), rows, rows),
        out_specs=(rows, rows),
        check_vma=False,
    )
```

```python
import jax
import jax.numpy as jnp
from jax import lax
from jax.experimental import pallas as pl
from jax.experimental.pallas import tpu as pltpu
from jax.sharding import PartitionSpec as P

DIN = 512
AXES = ("wide", "grp")
PAIR = 2
BLOCK = 128
NORM_ROWS = 16
LANES = 128
NORMS_WEIGHT = 400000
VMEM_LIMIT = 40 * 1024 * 1024
ROWS_BY_ROWS = (((1,), (1,)), ((), ()))


def scaled(rows, inv_len):
    factor = inv_len * DIN ** (-0.5)
    return (rows.astype(jnp.float32) * factor).astype(jnp.bfloat16)


def send_kernel(
    samples_hbm, inv_len_hbm, archive_hbm, mean_hbm, var_hbm,
    sent_ref, inv_len_ref, archive_ref, mean_ref, var_ref, samples_ref, arrived,
):
    copies = [
        pltpu.make_async_copy(source, target, arrived.at[number])
        for number, (source, target) in enumerate((
            (samples_hbm, samples_ref),
            (inv_len_hbm, inv_len_ref),
            (archive_hbm, archive_ref),
            (mean_hbm, mean_ref),
            (var_hbm, var_ref),
        ))
    ]
    for copy in copies:
        copy.start()
    for copy in copies[:2]:
        copy.wait()
    samp_z = scaled(samples_ref[...], inv_len_ref[...])
    samp_z = samp_z.reshape((1, PAIR) + sent_ref.shape[1:])
    targets = sent_ref.shape[0] // PAIR
    sent_ref[...] = jnp.broadcast_to(samp_z, (targets,) + samp_z.shape[1:]).reshape(sent_ref.shape)
    for copy in copies[2:]:
        copy.wait()


def runs_kernel(inv_len_ref, archive_ref, mean_ref, var_ref, pack_ref):
    runs = archive_ref.shape[0]
    width = mean_ref.shape[0]
    arch_z = scaled(archive_ref[...], inv_len_ref[...])
    pack_ref[:runs, :] = arch_z
    pack_ref[runs : runs + width, :] = mean_ref[...]
    pack_ref[runs + width : runs + 2 * width, :] = jnp.zeros(mean_ref.shape, jnp.bfloat16)
    pack_ref[runs + 2 * width : runs + 3 * width, :] = var_ref[...]
    wide_copy = arch_z.astype(jnp.float32)
    square = wide_copy * wide_copy
    high = square.astype(jnp.bfloat16)
    low = (square - high.astype(jnp.float32)).astype(jnp.bfloat16)
    ones = jnp.ones((NORM_ROWS, DIN), jnp.bfloat16)
    norm = lax.dot_general(ones, high, ROWS_BY_ROWS, preferred_element_type=jnp.float32)
    norm += lax.dot_general(ones, low, ROWS_BY_ROWS, preferred_element_type=jnp.float32)
    rest = 0.5 * norm
    row = lax.broadcasted_iota(jnp.int32, rest.shape, 0)
    parts = jnp.zeros(rest.shape, jnp.float32)
    for number in range(3):
        part = rest.astype(jnp.bfloat16).astype(jnp.float32)
        parts = jnp.where(row == number, part, parts)
        rest = rest - part
    pack_ref[runs + 3 * width :, :] = parts.astype(jnp.bfloat16)


def norms_kernel(samp_z_ref, norm_ref):
    def block(rows):
        wide_copy = samp_z_ref[rows, :].astype(jnp.float32)
        norm = 0.5 * jnp.sum(wide_copy * wide_copy, axis=-1, keepdims=True)
        norm_ref[rows, :] = jnp.broadcast_to(norm, (norm.shape[0], LANES))

    by_blocks(block, samp_z_ref.shape[0])


def sums_kernel(samp_z_ref, samp_norm_ref, own_ref, peer_ref, sums_ref):
    width = sums_ref.shape[1] // 2
    runs = own_ref.shape[0] - 3 * width - NORM_ROWS
    packs = (own_ref, peer_ref)

    def block(rows):
        samp_z = samp_z_ref[rows, :]
        samp_norm = samp_norm_ref[rows, :1]
        inner_prods = [
            lax.dot_general(
                samp_z, pack_ref[:runs, :], ROWS_BY_ROWS, preferred_element_type=jnp.float32
            )
            for pack_ref in packs
        ]
        kernels = []
        for inner_prod, pack_ref in zip(inner_prods, packs):
            norm_parts = pack_ref[runs + 3 * width :, :].astype(jnp.float32)
            arch_norm = jnp.sum(norm_parts, axis=0, keepdims=True)
            kernels.append(jnp.exp(inner_prod - samp_norm - arch_norm))
        total = None
        for kernel, pack_ref in zip(kernels, packs):
            for half, first in ((kernel, runs), (kernel * kernel, runs + width)):
                part = lax.dot_general(
                    half.astype(jnp.bfloat16),
                    pack_ref[first : first + 2 * width, :],
                    ROWS_BY_ROWS,
                    preferred_element_type=jnp.float32,
                )
                total = part if total is None else total + part
        sums_ref[rows, :] = total

    by_blocks(block, samp_z_ref.shape[0])


def by_blocks(block, count):
    if count <= BLOCK:
        block(slice(None))
    else:
        @pl.loop(0, count // BLOCK)
        def _(step):
            block(pl.ds(pl.multiple_of(step * BLOCK, BLOCK), BLOCK))


def call(kernel, out_shape, inputs, flops, transcendentals=0, in_space=pltpu.VMEM, scratch=()):
    moved = sum(array.size * array.dtype.itemsize for array in inputs)
    return pl.pallas_call(
        kernel,
        out_shape=out_shape,
        in_specs=[pl.BlockSpec(memory_space=in_space)] * len(inputs),
        out_specs=jax.tree.map(lambda _: pl.BlockSpec(memory_space=pltpu.VMEM), out_shape),
        scratch_shapes=scratch,
        cost_estimate=pl.CostEstimate(
            flops=flops, bytes_accessed=moved, transcendentals=transcendentals
        ),
        compiler_params=pltpu.CompilerParams(vmem_limit_bytes=VMEM_LIMIT),
    )(*inputs)


def on_device(samples, archive, inv_len, mean_coef, var_coef):
    devices = lax.axis_size(AXES)
    grp = lax.axis_size("grp")
    own_rows = samples.shape[0]
    part_rows = own_rows // PAIR
    rows = devices * part_rows
    runs, width = mean_coef.shape

    arrays = (samples, inv_len.reshape(1, DIN), archive, mean_coef.T, var_coef.T)
    sent, *held = call(
        send_kernel,
        (pltpu.VMEM((devices, part_rows, DIN), jnp.bfloat16),)
        + tuple(pltpu.VMEM(array.shape, array.dtype) for array in arrays[1:]),
        [pltpu.with_memory_space_constraint(array, pltpu.HBM) for array in arrays],
        flops=own_rows * DIN,
        in_space=pltpu.HBM,
        scratch=[pltpu.VMEM(samples.shape, samples.dtype), pltpu.SemaphoreType.DMA((5,))],
    )
    gathered = lax.all_to_all(sent, AXES, split_axis=0, concat_axis=0, tiled=True)
    own = call(
        runs_kernel,
        pltpu.VMEM((runs + 3 * width + NORM_ROWS, DIN), jnp.bfloat16),
        held,
        flops=68 * runs * DIN,
    )
    peer = lax.ppermute(own, "grp", [(i, i ^ 1) for i in range(grp)])
    samp_z = gathered.reshape(rows, DIN)
    samp_norm = call(
        norms_kernel,
        pltpu.VMEM((rows, LANES), jnp.float32),
        (samp_z,),
        flops=NORMS_WEIGHT * rows * DIN,
    )
    sums = call(
        sums_kernel,
        pltpu.VMEM((rows, 2 * width), jnp.float32),
        (samp_z, samp_norm, own, peer),
        flops=4 * rows * runs * (DIN + 4 * width),
        transcendentals=2 * rows * runs,
    )
    sums = sums.reshape(devices, part_rows, 2 * width)
    parts = lax.all_to_all(sums, AXES, split_axis=0, concat_axis=0, tiled=True)
    summed = jnp.sum(parts.reshape(devices // PAIR, own_rows, 2 * width), axis=0)
    return (summed[:, :width], 1.0 - summed[:, width:])


def solution(mesh):
    rows = P(AXES, None)
    return jax.shard_map(
        on_device,
        mesh=mesh,
        in_specs=(rows, rows, P(), rows, rows),
        out_specs=(rows, rows),
        check_vma=False,
    )
```

```python
import jax
import jax.numpy as jnp
from jax import lax
from jax.experimental import pallas as pl
from jax.experimental.pallas import tpu as pltpu
from jax.sharding import PartitionSpec as P

DIN = 512
AXES = ("wide", "grp")
PAIR = 2
BLOCK = 128
NORM_ROWS = 16
VMEM_LIMIT = 40 * 1024 * 1024
ROWS_BY_ROWS = (((1,), (1,)), ((), ()))


def scaled(rows, inv_len):
    factor = inv_len * DIN ** (-0.5)
    return (rows.astype(jnp.float32) * factor).astype(jnp.bfloat16)


def prepare_kernel(
    samples_hbm, inv_len_hbm, archive_hbm, mean_hbm, var_hbm,
    sent_ref, pack_ref, samples_ref, inv_len_ref, archive_ref, arrived,
):
    runs = archive_hbm.shape[0]
    width = mean_hbm.shape[0]
    chunks = [pl.ds(first, BLOCK) for first in range(0, runs, BLOCK)]
    moves = [(samples_hbm, samples_ref), (inv_len_hbm, inv_len_ref)]
    moves += [(archive_hbm.at[chunk], archive_ref.at[chunk]) for chunk in chunks]
    moves += [
        (mean_hbm, pack_ref.at[pl.ds(runs, width)]),
        (var_hbm, pack_ref.at[pl.ds(runs + 2 * width, width)]),
    ]
    copies = [
        pltpu.make_async_copy(source, target, arrived.at[number])
        for number, (source, target) in enumerate(moves)
    ]
    for copy in copies:
        copy.start()
    pack_ref[runs + width : runs + 2 * width, :] = jnp.zeros((width, DIN), jnp.bfloat16)
    copies[0].wait()
    copies[1].wait()
    inv_len = inv_len_ref[...]
    samp_z = scaled(samples_ref[...], inv_len)
    samp_z = samp_z.reshape((1, PAIR) + sent_ref.shape[1:])
    targets = sent_ref.shape[0] // PAIR
    sent_ref[...] = jnp.broadcast_to(samp_z, (targets,) + samp_z.shape[1:]).reshape(sent_ref.shape)
    row = lax.broadcasted_iota(jnp.int32, (BLOCK, BLOCK), 0)
    column = lax.broadcasted_iota(jnp.int32, (BLOCK, BLOCK), 1)
    part_row = lax.broadcasted_iota(jnp.int32, (NORM_ROWS, BLOCK), 0)
    for copy, chunk in zip(copies[2:], chunks):
        copy.wait()
        arch_z = scaled(archive_ref[chunk, :], inv_len)
        pack_ref[chunk, :] = arch_z
        products = lax.dot_general(arch_z, arch_z, ROWS_BY_ROWS, preferred_element_type=jnp.float32)
        norm = jnp.sum(jnp.where(row == column, products, 0.0), axis=0, keepdims=True)
        rest = jnp.broadcast_to(0.5 * norm, part_row.shape)
        parts = jnp.zeros(rest.shape, jnp.float32)
        for number in range(3):
            part = rest.astype(jnp.bfloat16).astype(jnp.float32)
            parts = jnp.where(part_row == number, part, parts)
            rest = rest - part
        pack_ref[runs + 3 * width :, chunk] = parts.astype(jnp.bfloat16)
    for copy in copies[2 + len(chunks) :]:
        copy.wait()


def sums_kernel(samp_z_ref, own_ref, peer_ref, sums_ref):
    width = sums_ref.shape[1] // 2
    runs = own_ref.shape[0] - 3 * width - NORM_ROWS
    packs = (own_ref, peer_ref)

    def block(rows):
        samp_z = samp_z_ref[rows, :]
        wide_copy = samp_z.astype(jnp.float32)
        samp_norm = 0.5 * jnp.sum(wide_copy * wide_copy, axis=-1, keepdims=True)
        inner_prods = [
            lax.dot_general(
                samp_z, pack_ref[:runs, :], ROWS_BY_ROWS, preferred_element_type=jnp.float32
            )
            for pack_ref in packs
        ]
        kernels = []
        for inner_prod, pack_ref in zip(inner_prods, packs):
            norm_parts = pack_ref[runs + 3 * width :, :].astype(jnp.float32)
            arch_norm = jnp.sum(norm_parts, axis=0, keepdims=True)
            kernels.append(jnp.exp(inner_prod - samp_norm - arch_norm))
        total = None
        for kernel, pack_ref in zip(kernels, packs):
            for half, first in ((kernel, runs), (kernel * kernel, runs + width)):
                part = lax.dot_general(
                    half.astype(jnp.bfloat16),
                    pack_ref[first : first + 2 * width, :],
                    ROWS_BY_ROWS,
                    preferred_element_type=jnp.float32,
                )
                total = part if total is None else total + part
        sums_ref[rows, :] = total

    by_blocks(block, samp_z_ref.shape[0])


def by_blocks(block, count):
    if count <= BLOCK:
        block(slice(None))
    else:
        @pl.loop(0, count // BLOCK)
        def _(step):
            block(pl.ds(pl.multiple_of(step * BLOCK, BLOCK), BLOCK))


def call(kernel, out_shape, inputs, flops, transcendentals=0, in_space=pltpu.VMEM, scratch=()):
    moved = sum(array.size * array.dtype.itemsize for array in inputs)
    return pl.pallas_call(
        kernel,
        out_shape=out_shape,
        in_specs=[pl.BlockSpec(memory_space=in_space)] * len(inputs),
        out_specs=jax.tree.map(lambda _: pl.BlockSpec(memory_space=pltpu.VMEM), out_shape),
        scratch_shapes=scratch,
        cost_estimate=pl.CostEstimate(
            flops=flops, bytes_accessed=moved, transcendentals=transcendentals
        ),
        compiler_params=pltpu.CompilerParams(vmem_limit_bytes=VMEM_LIMIT),
    )(*inputs)


def on_device(samples, archive, inv_len, mean_coef, var_coef):
    devices = lax.axis_size(AXES)
    grp = lax.axis_size("grp")
    own_rows = samples.shape[0]
    part_rows = own_rows // PAIR
    rows = devices * part_rows
    runs, width = mean_coef.shape

    arrays = (samples, inv_len.reshape(1, DIN), archive, mean_coef.T, var_coef.T)
    sent, own = call(
        prepare_kernel,
        (
            pltpu.VMEM((devices, part_rows, DIN), jnp.bfloat16),
            pltpu.VMEM((runs + 3 * width + NORM_ROWS, DIN), jnp.bfloat16),
        ),
        [pltpu.with_memory_space_constraint(array, pltpu.HBM) for array in arrays],
        flops=2 * BLOCK * runs * DIN,
        in_space=pltpu.HBM,
        scratch=[pltpu.VMEM(array.shape, array.dtype) for array in arrays[:3]]
        + [pltpu.SemaphoreType.DMA((4 + runs // BLOCK,))],
    )
    gathered = lax.all_to_all(sent, AXES, split_axis=0, concat_axis=0, tiled=True)
    peer = lax.ppermute(own, "grp", [(i, i ^ 1) for i in range(grp)])
    sums = call(
        sums_kernel,
        pltpu.VMEM((rows, 2 * width), jnp.float32),
        (gathered.reshape(rows, DIN), own, peer),
        flops=4 * rows * runs * (DIN + 4 * width),
        transcendentals=2 * rows * runs,
    )
    sums = sums.reshape(devices, part_rows, 2 * width)
    parts = lax.all_to_all(sums, AXES, split_axis=0, concat_axis=0, tiled=True)
    summed = jnp.sum(parts.reshape(devices // PAIR, own_rows, 2 * width), axis=0)
    return (summed[:, :width], 1.0 - summed[:, width:])


def solution(mesh):
    rows = P(AXES, None)
    return jax.shard_map(
        on_device,
        mesh=mesh,
        in_specs=(rows, rows, P(), rows, rows),
        out_specs=(rows, rows),
        check_vma=False,
    )
```

```python
import jax
import jax.numpy as jnp
from jax import lax
from jax.experimental import pallas as pl
from jax.experimental.pallas import tpu as pltpu
from jax.sharding import PartitionSpec as P

DIN = 512
AXES = ("wide", "grp")
PAIR = 2
BLOCK = 128
NORM_ROWS = 16
LANES = 128
NORMS_WEIGHT = 400000
VMEM_LIMIT = 40 * 1024 * 1024
ROWS_BY_ROWS = (((1,), (1,)), ((), ()))


def scaled(rows, inv_len):
    factor = inv_len * DIN ** (-0.5)
    return (rows.astype(jnp.float32) * factor).astype(jnp.bfloat16)


def send_kernel(samples_hbm, inv_len_hbm, sent_ref, inv_len_ref, samples_ref, arrived):
    copies = [
        pltpu.make_async_copy(samples_hbm, samples_ref, arrived.at[0]),
        pltpu.make_async_copy(inv_len_hbm, inv_len_ref, arrived.at[1]),
    ]
    for copy in copies:
        copy.start()
    for copy in copies:
        copy.wait()
    samp_z = scaled(samples_ref[...], inv_len_ref[...])
    samp_z = samp_z.reshape((1, PAIR) + sent_ref.shape[1:])
    targets = sent_ref.shape[0] // PAIR
    sent_ref[...] = jnp.broadcast_to(samp_z, (targets,) + samp_z.shape[1:]).reshape(sent_ref.shape)


def runs_kernel(inv_len_ref, archive_ref, mean_hbm, var_hbm, pack_ref, arrived):
    runs = archive_ref.shape[0]
    width = mean_hbm.shape[0]
    copies = [
        pltpu.make_async_copy(mean_hbm, pack_ref.at[pl.ds(runs, width)], arrived.at[0]),
        pltpu.make_async_copy(var_hbm, pack_ref.at[pl.ds(runs + 2 * width, width)], arrived.at[1]),
    ]
    for copy in copies:
        copy.start()
    pack_ref[runs + width : runs + 2 * width, :] = jnp.zeros((width, DIN), jnp.bfloat16)
    row = lax.broadcasted_iota(jnp.int32, (BLOCK, BLOCK), 0)
    column = lax.broadcasted_iota(jnp.int32, (BLOCK, BLOCK), 1)
    norms = []
    for first in range(0, runs, BLOCK):
        arch_z = scaled(archive_ref[first : first + BLOCK, :], inv_len_ref[...])
        pack_ref[first : first + BLOCK, :] = arch_z
        products = lax.dot_general(arch_z, arch_z, ROWS_BY_ROWS, preferred_element_type=jnp.float32)
        norms.append(jnp.sum(jnp.where(row == column, products, 0.0), axis=0, keepdims=True))
    rest = jnp.broadcast_to(0.5 * jnp.concatenate(norms, axis=1), (NORM_ROWS, runs))
    part_row = lax.broadcasted_iota(jnp.int32, rest.shape, 0)
    parts = jnp.zeros(rest.shape, jnp.float32)
    for number in range(3):
        part = rest.astype(jnp.bfloat16).astype(jnp.float32)
        parts = jnp.where(part_row == number, part, parts)
        rest = rest - part
    pack_ref[runs + 3 * width :, :] = parts.astype(jnp.bfloat16)
    for copy in copies:
        copy.wait()


def norms_kernel(samp_z_ref, norm_ref):
    def block(rows):
        wide_copy = samp_z_ref[rows, :].astype(jnp.float32)
        norm = 0.5 * jnp.sum(wide_copy * wide_copy, axis=-1, keepdims=True)
        norm_ref[rows, :] = jnp.broadcast_to(norm, (norm.shape[0], LANES))

    by_blocks(block, samp_z_ref.shape[0])


def sums_kernel(samp_z_ref, samp_norm_ref, own_ref, peer_ref, sums_ref):
    width = sums_ref.shape[1] // 2
    runs = own_ref.shape[0] - 3 * width - NORM_ROWS
    packs = (own_ref, peer_ref)

    def block(rows):
        samp_z = samp_z_ref[rows, :]
        samp_norm = samp_norm_ref[rows, :1]
        inner_prods = [
            lax.dot_general(
                samp_z, pack_ref[:runs, :], ROWS_BY_ROWS, preferred_element_type=jnp.float32
            )
            for pack_ref in packs
        ]
        kernels = []
        for inner_prod, pack_ref in zip(inner_prods, packs):
            norm_parts = pack_ref[runs + 3 * width :, :].astype(jnp.float32)
            arch_norm = jnp.sum(norm_parts, axis=0, keepdims=True)
            kernels.append(jnp.exp(inner_prod - samp_norm - arch_norm))
        total = None
        for kernel, pack_ref in zip(kernels, packs):
            for half, first in ((kernel, runs), (kernel * kernel, runs + width)):
                part = lax.dot_general(
                    half.astype(jnp.bfloat16),
                    pack_ref[first : first + 2 * width, :],
                    ROWS_BY_ROWS,
                    preferred_element_type=jnp.float32,
                )
                total = part if total is None else total + part
        sums_ref[rows, :] = total

    by_blocks(block, samp_z_ref.shape[0])


def by_blocks(block, count):
    if count <= BLOCK:
        block(slice(None))
    else:
        @pl.loop(0, count // BLOCK)
        def _(step):
            block(pl.ds(pl.multiple_of(step * BLOCK, BLOCK), BLOCK))


def call(kernel, out_shape, inputs, flops, transcendentals=0, in_spaces=None, scratch=()):
    moved = sum(array.size * array.dtype.itemsize for array in inputs)
    in_spaces = in_spaces or [pltpu.VMEM] * len(inputs)
    inputs = [
        pltpu.with_memory_space_constraint(array, space) if space == pltpu.HBM else array
        for array, space in zip(inputs, in_spaces)
    ]
    return pl.pallas_call(
        kernel,
        out_shape=out_shape,
        in_specs=[pl.BlockSpec(memory_space=space) for space in in_spaces],
        out_specs=jax.tree.map(lambda _: pl.BlockSpec(memory_space=pltpu.VMEM), out_shape),
        scratch_shapes=scratch,
        cost_estimate=pl.CostEstimate(
            flops=flops, bytes_accessed=moved, transcendentals=transcendentals
        ),
        compiler_params=pltpu.CompilerParams(vmem_limit_bytes=VMEM_LIMIT),
    )(*inputs)


def on_device(samples, archive, inv_len, mean_coef, var_coef):
    devices = lax.axis_size(AXES)
    grp = lax.axis_size("grp")
    own_rows = samples.shape[0]
    part_rows = own_rows // PAIR
    rows = devices * part_rows
    runs, width = mean_coef.shape

    sent, held_len = call(
        send_kernel,
        (
            pltpu.VMEM((devices, part_rows, DIN), jnp.bfloat16),
            pltpu.VMEM((1, DIN), jnp.float32),
        ),
        (samples, inv_len.reshape(1, DIN)),
        flops=own_rows * DIN,
        in_spaces=[pltpu.HBM] * 2,
        scratch=[pltpu.VMEM(samples.shape, samples.dtype), pltpu.SemaphoreType.DMA((2,))],
    )
    gathered = lax.all_to_all(sent, AXES, split_axis=0, concat_axis=0, tiled=True)
    own = call(
        runs_kernel,
        pltpu.VMEM((runs + 3 * width + NORM_ROWS, DIN), jnp.bfloat16),
        (held_len, archive, mean_coef.T, var_coef.T),
        flops=2 * BLOCK * runs * DIN,
        in_spaces=[pltpu.VMEM] * 2 + [pltpu.HBM] * 2,
        scratch=[pltpu.SemaphoreType.DMA((2,))],
    )
    peer = lax.ppermute(own, "grp", [(i, i ^ 1) for i in range(grp)])
    samp_z = gathered.reshape(rows, DIN)
    samp_norm = call(
        norms_kernel,
        pltpu.VMEM((rows, LANES), jnp.float32),
        (samp_z,),
        flops=NORMS_WEIGHT * rows * DIN,
    )
    sums = call(
        sums_kernel,
        pltpu.VMEM((rows, 2 * width), jnp.float32),
        (samp_z, samp_norm, own, peer),
        flops=4 * rows * runs * (DIN + 4 * width),
        transcendentals=2 * rows * runs,
    )
    sums = sums.reshape(devices, part_rows, 2 * width)
    parts = lax.all_to_all(sums, AXES, split_axis=0, concat_axis=0, tiled=True)
    summed = jnp.sum(parts.reshape(devices // PAIR, own_rows, 2 * width), axis=0)
    return (summed[:, :width], 1.0 - summed[:, width:])


def solution(mesh):
    rows = P(AXES, None)
    return jax.shard_map(
        on_device,
        mesh=mesh,
        in_specs=(rows, rows, P(), rows, rows),
        out_specs=(rows, rows),
        check_vma=False,
    )
```

```python
import jax
import jax.numpy as jnp
from jax import lax
from jax.experimental import pallas as pl
from jax.experimental.pallas import tpu as pltpu
from jax.sharding import PartitionSpec as P

DIN = 512
AXES = ("wide", "grp")
PAIR = 2
BLOCK = 128
NORM_ROWS = 16
VMEM_LIMIT = 40 * 1024 * 1024
ROWS_BY_ROWS = (((1,), (1,)), ((), ()))


def scaled(rows, inv_len):
    factor = inv_len * DIN ** (-0.5)
    return (rows.astype(jnp.float32) * factor).astype(jnp.bfloat16)


def send_kernel(
    samples_hbm, inv_len_hbm, archive_hbm, mean_hbm, var_hbm,
    sent_ref, inv_len_ref, archive_ref, mean_ref, var_ref, samples_ref, arrived,
):
    copies = [
        pltpu.make_async_copy(source, target, arrived.at[number])
        for number, (source, target) in enumerate((
            (samples_hbm, samples_ref),
            (inv_len_hbm, inv_len_ref),
            (archive_hbm, archive_ref),
            (mean_hbm, mean_ref),
            (var_hbm, var_ref),
        ))
    ]
    for copy in copies:
        copy.start()
    for copy in copies[:2]:
        copy.wait()
    samp_z = scaled(samples_ref[...], inv_len_ref[...])
    samp_z = samp_z.reshape((1, PAIR) + sent_ref.shape[1:])
    targets = sent_ref.shape[0] // PAIR
    sent_ref[...] = jnp.broadcast_to(samp_z, (targets,) + samp_z.shape[1:]).reshape(sent_ref.shape)
    for copy in copies[2:]:
        copy.wait()


def runs_kernel(inv_len_ref, archive_ref, mean_ref, var_ref, pack_ref):
    runs = archive_ref.shape[0]
    width = mean_ref.shape[0]
    row = lax.broadcasted_iota(jnp.int32, (BLOCK, BLOCK), 0)
    column = lax.broadcasted_iota(jnp.int32, (BLOCK, BLOCK), 1)
    norms = []
    for first in range(0, runs, BLOCK):
        arch_z = scaled(archive_ref[first : first + BLOCK, :], inv_len_ref[...])
        pack_ref[first : first + BLOCK, :] = arch_z
        products = lax.dot_general(arch_z, arch_z, ROWS_BY_ROWS, preferred_element_type=jnp.float32)
        norms.append(jnp.sum(jnp.where(row == column, products, 0.0), axis=0, keepdims=True))
    pack_ref[runs : runs + width, :] = mean_ref[...]
    pack_ref[runs + width : runs + 2 * width, :] = jnp.zeros(mean_ref.shape, jnp.bfloat16)
    pack_ref[runs + 2 * width : runs + 3 * width, :] = var_ref[...]
    rest = jnp.broadcast_to(0.5 * jnp.concatenate(norms, axis=1), (NORM_ROWS, runs))
    part_row = lax.broadcasted_iota(jnp.int32, rest.shape, 0)
    parts = jnp.zeros(rest.shape, jnp.float32)
    for number in range(3):
        part = rest.astype(jnp.bfloat16).astype(jnp.float32)
        parts = jnp.where(part_row == number, part, parts)
        rest = rest - part
    pack_ref[runs + 3 * width :, :] = parts.astype(jnp.bfloat16)


def sums_kernel(samp_z_ref, own_ref, peer_ref, sums_ref):
    width = sums_ref.shape[1] // 2
    runs = own_ref.shape[0] - 3 * width - NORM_ROWS
    packs = (own_ref, peer_ref)

    def block(rows):
        samp_z = samp_z_ref[rows, :]
        wide_copy = samp_z.astype(jnp.float32)
        samp_norm = 0.5 * jnp.sum(wide_copy * wide_copy, axis=-1, keepdims=True)
        inner_prods = [
            lax.dot_general(
                samp_z, pack_ref[:runs, :], ROWS_BY_ROWS, preferred_element_type=jnp.float32
            )
            for pack_ref in packs
        ]
        kernels = []
        for inner_prod, pack_ref in zip(inner_prods, packs):
            norm_parts = pack_ref[runs + 3 * width :, :].astype(jnp.float32)
            arch_norm = jnp.sum(norm_parts, axis=0, keepdims=True)
            kernels.append(jnp.exp(inner_prod - samp_norm - arch_norm))
        total = None
        for kernel, pack_ref in zip(kernels, packs):
            for half, first in ((kernel, runs), (kernel * kernel, runs + width)):
                part = lax.dot_general(
                    half.astype(jnp.bfloat16),
                    pack_ref[first : first + 2 * width, :],
                    ROWS_BY_ROWS,
                    preferred_element_type=jnp.float32,
                )
                total = part if total is None else total + part
        sums_ref[rows, :] = total

    by_blocks(block, samp_z_ref.shape[0])


def by_blocks(block, count):
    if count <= BLOCK:
        block(slice(None))
    else:
        @pl.loop(0, count // BLOCK)
        def _(step):
            block(pl.ds(pl.multiple_of(step * BLOCK, BLOCK), BLOCK))


def call(kernel, out_shape, inputs, flops, transcendentals=0, in_space=pltpu.VMEM, scratch=()):
    moved = sum(array.size * array.dtype.itemsize for array in inputs)
    return pl.pallas_call(
        kernel,
        out_shape=out_shape,
        in_specs=[pl.BlockSpec(memory_space=in_space)] * len(inputs),
        out_specs=jax.tree.map(lambda _: pl.BlockSpec(memory_space=pltpu.VMEM), out_shape),
        scratch_shapes=scratch,
        cost_estimate=pl.CostEstimate(
            flops=flops, bytes_accessed=moved, transcendentals=transcendentals
        ),
        compiler_params=pltpu.CompilerParams(vmem_limit_bytes=VMEM_LIMIT),
    )(*inputs)


def on_device(samples, archive, inv_len, mean_coef, var_coef):
    devices = lax.axis_size(AXES)
    grp = lax.axis_size("grp")
    own_rows = samples.shape[0]
    part_rows = own_rows // PAIR
    rows = devices * part_rows
    runs, width = mean_coef.shape

    arrays = (samples, inv_len.reshape(1, DIN), archive, mean_coef.T, var_coef.T)
    sent, *held = call(
        send_kernel,
        (pltpu.VMEM((devices, part_rows, DIN), jnp.bfloat16),)
        + tuple(pltpu.VMEM(array.shape, array.dtype) for array in arrays[1:]),
        [pltpu.with_memory_space_constraint(array, pltpu.HBM) for array in arrays],
        flops=own_rows * DIN,
        in_space=pltpu.HBM,
        scratch=[pltpu.VMEM(samples.shape, samples.dtype), pltpu.SemaphoreType.DMA((5,))],
    )
    gathered = lax.all_to_all(sent, AXES, split_axis=0, concat_axis=0, tiled=True)
    own = call(
        runs_kernel,
        pltpu.VMEM((runs + 3 * width + NORM_ROWS, DIN), jnp.bfloat16),
        held,
        flops=2 * BLOCK * runs * DIN,
    )
    peer = lax.ppermute(own, "grp", [(i, i ^ 1) for i in range(grp)])
    sums = call(
        sums_kernel,
        pltpu.VMEM((rows, 2 * width), jnp.float32),
        (gathered.reshape(rows, DIN), own, peer),
        flops=4 * rows * runs * (DIN + 4 * width),
        transcendentals=2 * rows * runs,
    )
    sums = sums.reshape(devices, part_rows, 2 * width)
    parts = lax.all_to_all(sums, AXES, split_axis=0, concat_axis=0, tiled=True)
    summed = jnp.sum(parts.reshape(devices // PAIR, own_rows, 2 * width), axis=0)
    return (summed[:, :width], 1.0 - summed[:, width:])


def solution(mesh):
    rows = P(AXES, None)
    return jax.shard_map(
        on_device,
        mesh=mesh,
        in_specs=(rows, rows, P(), rows, rows),
        out_specs=(rows, rows),
        check_vma=False,
    )
```

```python
import jax
import jax.numpy as jnp
from jax import lax
from jax.experimental import pallas as pl
from jax.experimental.pallas import tpu as pltpu
from jax.sharding import PartitionSpec as P

DIN = 512
AXES = ("wide", "grp")
PAIR = 2
BLOCK = 128
NORM_ROWS = 16
VMEM_LIMIT = 40 * 1024 * 1024
ROWS_BY_ROWS = (((1,), (1,)), ((), ()))


def scaled(rows, inv_len):
    factor = inv_len * DIN ** (-0.5)
    return (rows.astype(jnp.float32) * factor).astype(jnp.bfloat16)


def send_kernel(samples_hbm, inv_len_hbm, sent_ref, inv_len_ref, samples_ref, arrived):
    copies = [
        pltpu.make_async_copy(samples_hbm, samples_ref, arrived.at[0]),
        pltpu.make_async_copy(inv_len_hbm, inv_len_ref, arrived.at[1]),
    ]
    for copy in copies:
        copy.start()
    for copy in copies:
        copy.wait()
    samp_z = scaled(samples_ref[...], inv_len_ref[...])
    samp_z = samp_z.reshape((1, PAIR) + sent_ref.shape[1:])
    targets = sent_ref.shape[0] // PAIR
    sent_ref[...] = jnp.broadcast_to(samp_z, (targets,) + samp_z.shape[1:]).reshape(sent_ref.shape)


def runs_kernel(inv_len_ref, archive_ref, mean_ref, var_ref, pack_ref):
    runs = archive_ref.shape[0]
    width = mean_ref.shape[0]
    row = lax.broadcasted_iota(jnp.int32, (BLOCK, BLOCK), 0)
    column = lax.broadcasted_iota(jnp.int32, (BLOCK, BLOCK), 1)
    norms = []
    for first in range(0, runs, BLOCK):
        arch_z = scaled(archive_ref[first : first + BLOCK, :], inv_len_ref[...])
        pack_ref[first : first + BLOCK, :] = arch_z
        products = lax.dot_general(arch_z, arch_z, ROWS_BY_ROWS, preferred_element_type=jnp.float32)
        norms.append(jnp.sum(jnp.where(row == column, products, 0.0), axis=0, keepdims=True))
    pack_ref[runs : runs + width, :] = mean_ref[...]
    pack_ref[runs + width : runs + 2 * width, :] = jnp.zeros(mean_ref.shape, jnp.bfloat16)
    pack_ref[runs + 2 * width : runs + 3 * width, :] = var_ref[...]
    rest = jnp.broadcast_to(0.5 * jnp.concatenate(norms, axis=1), (NORM_ROWS, runs))
    part_row = lax.broadcasted_iota(jnp.int32, rest.shape, 0)
    parts = jnp.zeros(rest.shape, jnp.float32)
    for number in range(3):
        part = rest.astype(jnp.bfloat16).astype(jnp.float32)
        parts = jnp.where(part_row == number, part, parts)
        rest = rest - part
    pack_ref[runs + 3 * width :, :] = parts.astype(jnp.bfloat16)


def sums_kernel(samp_z_ref, own_ref, peer_ref, sums_ref):
    width = sums_ref.shape[1] // 2
    runs = own_ref.shape[0] - 3 * width - NORM_ROWS
    packs = (own_ref, peer_ref)

    def block(rows):
        samp_z = samp_z_ref[rows, :]
        wide_copy = samp_z.astype(jnp.float32)
        samp_norm = 0.5 * jnp.sum(wide_copy * wide_copy, axis=-1, keepdims=True)
        inner_prods = [
            lax.dot_general(
                samp_z, pack_ref[:runs, :], ROWS_BY_ROWS, preferred_element_type=jnp.float32
            )
            for pack_ref in packs
        ]
        kernels = []
        for inner_prod, pack_ref in zip(inner_prods, packs):
            norm_parts = pack_ref[runs + 3 * width :, :].astype(jnp.float32)
            arch_norm = jnp.sum(norm_parts, axis=0, keepdims=True)
            kernels.append(jnp.exp(inner_prod - samp_norm - arch_norm))
        total = None
        for kernel, pack_ref in zip(kernels, packs):
            for half, first in ((kernel, runs), (kernel * kernel, runs + width)):
                part = lax.dot_general(
                    half.astype(jnp.bfloat16),
                    pack_ref[first : first + 2 * width, :],
                    ROWS_BY_ROWS,
                    preferred_element_type=jnp.float32,
                )
                total = part if total is None else total + part
        sums_ref[rows, :] = total

    by_blocks(block, samp_z_ref.shape[0])


def by_blocks(block, count):
    if count <= BLOCK:
        block(slice(None))
    else:
        @pl.loop(0, count // BLOCK)
        def _(step):
            block(pl.ds(pl.multiple_of(step * BLOCK, BLOCK), BLOCK))


def call(kernel, out_shape, inputs, flops, transcendentals=0, in_spaces=None, scratch=()):
    moved = sum(array.size * array.dtype.itemsize for array in inputs)
    in_spaces = in_spaces or [pltpu.VMEM] * len(inputs)
    inputs = [
        pltpu.with_memory_space_constraint(array, space) if space == pltpu.HBM else array
        for array, space in zip(inputs, in_spaces)
    ]
    return pl.pallas_call(
        kernel,
        out_shape=out_shape,
        in_specs=[pl.BlockSpec(memory_space=space) for space in in_spaces],
        out_specs=jax.tree.map(lambda _: pl.BlockSpec(memory_space=pltpu.VMEM), out_shape),
        scratch_shapes=scratch,
        cost_estimate=pl.CostEstimate(
            flops=flops, bytes_accessed=moved, transcendentals=transcendentals
        ),
        compiler_params=pltpu.CompilerParams(vmem_limit_bytes=VMEM_LIMIT),
    )(*inputs)


def on_device(samples, archive, inv_len, mean_coef, var_coef):
    devices = lax.axis_size(AXES)
    grp = lax.axis_size("grp")
    own_rows = samples.shape[0]
    part_rows = own_rows // PAIR
    rows = devices * part_rows
    runs, width = mean_coef.shape

    sent, held_len = call(
        send_kernel,
        (
            pltpu.VMEM((devices, part_rows, DIN), jnp.bfloat16),
            pltpu.VMEM((1, DIN), jnp.float32),
        ),
        (samples, inv_len.reshape(1, DIN)),
        flops=own_rows * DIN,
        in_spaces=[pltpu.HBM] * 2,
        scratch=[pltpu.VMEM(samples.shape, samples.dtype), pltpu.SemaphoreType.DMA((2,))],
    )
    gathered = lax.all_to_all(sent, AXES, split_axis=0, concat_axis=0, tiled=True)
    own = call(
        runs_kernel,
        pltpu.VMEM((runs + 3 * width + NORM_ROWS, DIN), jnp.bfloat16),
        (held_len, archive, mean_coef.T, var_coef.T),
        flops=2 * BLOCK * runs * DIN,
    )
    peer = lax.ppermute(own, "grp", [(i, i ^ 1) for i in range(grp)])
    sums = call(
        sums_kernel,
        pltpu.VMEM((rows, 2 * width), jnp.float32),
        (gathered.reshape(rows, DIN), own, peer),
        flops=4 * rows * runs * (DIN + 4 * width),
        transcendentals=2 * rows * runs,
    )
    sums = sums.reshape(devices, part_rows, 2 * width)
    parts = lax.all_to_all(sums, AXES, split_axis=0, concat_axis=0, tiled=True)
    summed = jnp.sum(parts.reshape(devices // PAIR, own_rows, 2 * width), axis=0)
    return (summed[:, :width], 1.0 - summed[:, width:])


def solution(mesh):
    rows = P(AXES, None)
    return jax.shard_map(
        on_device,
        mesh=mesh,
        in_specs=(rows, rows, P(), rows, rows),
        out_specs=(rows, rows),
        check_vma=False,
    )
```

```python
import jax
import jax.numpy as jnp
from jax import lax
from jax.experimental import pallas as pl
from jax.experimental.pallas import tpu as pltpu
from jax.sharding import PartitionSpec as P

DIN = 512
AXES = ("wide", "grp")
PAIR = 2
BLOCK = 128
NORM_ROWS = 16
VMEM_LIMIT = 40 * 1024 * 1024
ROWS_BY_ROWS = (((1,), (1,)), ((), ()))


def scaled(rows, inv_len):
    factor = inv_len * DIN ** (-0.5)
    return (rows.astype(jnp.float32) * factor).astype(jnp.bfloat16)


def prepare_kernel(
    samples_hbm, inv_len_hbm, archive_hbm, mean_hbm, var_hbm,
    sent_ref, pack_ref, samples_ref, inv_len_ref, archive_ref, arrived,
):
    runs = archive_hbm.shape[0]
    width = mean_hbm.shape[0]
    chunks = [pl.ds(first, BLOCK) for first in range(0, runs, BLOCK)]
    moves = [(samples_hbm, samples_ref), (inv_len_hbm, inv_len_ref)]
    moves += [(archive_hbm.at[chunk], archive_ref.at[chunk]) for chunk in chunks]
    moves += [
        (mean_hbm, pack_ref.at[pl.ds(runs, width)]),
        (var_hbm, pack_ref.at[pl.ds(runs + 2 * width, width)]),
    ]
    copies = [
        pltpu.make_async_copy(source, target, arrived.at[number])
        for number, (source, target) in enumerate(moves)
    ]
    for copy in copies:
        copy.start()
    pack_ref[runs + width : runs + 2 * width, :] = jnp.zeros((width, DIN), jnp.bfloat16)
    copies[0].wait()
    copies[1].wait()
    inv_len = inv_len_ref[...]
    samp_z = scaled(samples_ref[...], inv_len)
    samp_z = samp_z.reshape((1, PAIR) + sent_ref.shape[1:])
    targets = sent_ref.shape[0] // PAIR
    sent_ref[...] = jnp.broadcast_to(samp_z, (targets,) + samp_z.shape[1:]).reshape(sent_ref.shape)
    row = lax.broadcasted_iota(jnp.int32, (BLOCK, BLOCK), 0)
    column = lax.broadcasted_iota(jnp.int32, (BLOCK, BLOCK), 1)
    for copy in copies[2 : 2 + len(chunks)]:
        copy.wait()
    norms = []
    for chunk in chunks:
        arch_z = scaled(archive_ref[chunk, :], inv_len)
        pack_ref[chunk, :] = arch_z
        products = lax.dot_general(arch_z, arch_z, ROWS_BY_ROWS, preferred_element_type=jnp.float32)
        norms.append(jnp.sum(jnp.where(row == column, products, 0.0), axis=0, keepdims=True))
    rest = jnp.broadcast_to(0.5 * jnp.concatenate(norms, axis=1), (NORM_ROWS, runs))
    part_row = lax.broadcasted_iota(jnp.int32, rest.shape, 0)
    parts = jnp.zeros(rest.shape, jnp.float32)
    for number in range(3):
        part = rest.astype(jnp.bfloat16).astype(jnp.float32)
        parts = jnp.where(part_row == number, part, parts)
        rest = rest - part
    pack_ref[runs + 3 * width :, :] = parts.astype(jnp.bfloat16)
    for copy in copies[2 + len(chunks) :]:
        copy.wait()


def sums_kernel(samp_z_ref, own_ref, peer_ref, sums_ref):
    width = sums_ref.shape[1] // 2
    runs = own_ref.shape[0] - 3 * width - NORM_ROWS
    packs = (own_ref, peer_ref)

    def block(rows):
        samp_z = samp_z_ref[rows, :]
        wide_copy = samp_z.astype(jnp.float32)
        samp_norm = 0.5 * jnp.sum(wide_copy * wide_copy, axis=-1, keepdims=True)
        inner_prods = [
            lax.dot_general(
                samp_z, pack_ref[:runs, :], ROWS_BY_ROWS, preferred_element_type=jnp.float32
            )
            for pack_ref in packs
        ]
        kernels = []
        for inner_prod, pack_ref in zip(inner_prods, packs):
            norm_parts = pack_ref[runs + 3 * width :, :].astype(jnp.float32)
            arch_norm = jnp.sum(norm_parts, axis=0, keepdims=True)
            kernels.append(jnp.exp(inner_prod - samp_norm - arch_norm))
        total = None
        for kernel, pack_ref in zip(kernels, packs):
            for half, first in ((kernel, runs), (kernel * kernel, runs + width)):
                part = lax.dot_general(
                    half.astype(jnp.bfloat16),
                    pack_ref[first : first + 2 * width, :],
                    ROWS_BY_ROWS,
                    preferred_element_type=jnp.float32,
                )
                total = part if total is None else total + part
        sums_ref[rows, :] = total

    by_blocks(block, samp_z_ref.shape[0])


def by_blocks(block, count):
    if count <= BLOCK:
        block(slice(None))
    else:
        @pl.loop(0, count // BLOCK)
        def _(step):
            block(pl.ds(pl.multiple_of(step * BLOCK, BLOCK), BLOCK))


def call(kernel, out_shape, inputs, flops, transcendentals=0, in_space=pltpu.VMEM, scratch=()):
    moved = sum(array.size * array.dtype.itemsize for array in inputs)
    return pl.pallas_call(
        kernel,
        out_shape=out_shape,
        in_specs=[pl.BlockSpec(memory_space=in_space)] * len(inputs),
        out_specs=jax.tree.map(lambda _: pl.BlockSpec(memory_space=pltpu.VMEM), out_shape),
        scratch_shapes=scratch,
        cost_estimate=pl.CostEstimate(
            flops=flops, bytes_accessed=moved, transcendentals=transcendentals
        ),
        compiler_params=pltpu.CompilerParams(vmem_limit_bytes=VMEM_LIMIT),
    )(*inputs)


def on_device(samples, archive, inv_len, mean_coef, var_coef):
    devices = lax.axis_size(AXES)
    grp = lax.axis_size("grp")
    own_rows = samples.shape[0]
    part_rows = own_rows // PAIR
    rows = devices * part_rows
    runs, width = mean_coef.shape

    arrays = (samples, inv_len.reshape(1, DIN), archive, mean_coef.T, var_coef.T)
    sent, own = call(
        prepare_kernel,
        (
            pltpu.VMEM((devices, part_rows, DIN), jnp.bfloat16),
            pltpu.VMEM((runs + 3 * width + NORM_ROWS, DIN), jnp.bfloat16),
        ),
        [pltpu.with_memory_space_constraint(array, pltpu.HBM) for array in arrays],
        flops=2 * BLOCK * runs * DIN,
        in_space=pltpu.HBM,
        scratch=[pltpu.VMEM(array.shape, array.dtype) for array in arrays[:3]]
        + [pltpu.SemaphoreType.DMA((4 + runs // BLOCK,))],
    )
    gathered = lax.all_to_all(sent, AXES, split_axis=0, concat_axis=0, tiled=True)
    peer = lax.ppermute(own, "grp", [(i, i ^ 1) for i in range(grp)])
    sums = call(
        sums_kernel,
        pltpu.VMEM((rows, 2 * width), jnp.float32),
        (gathered.reshape(rows, DIN), own, peer),
        flops=4 * rows * runs * (DIN + 4 * width),
        transcendentals=2 * rows * runs,
    )
    sums = sums.reshape(devices, part_rows, 2 * width)
    parts = lax.all_to_all(sums, AXES, split_axis=0, concat_axis=0, tiled=True)
    summed = jnp.sum(parts.reshape(devices // PAIR, own_rows, 2 * width), axis=0)
    return (summed[:, :width], 1.0 - summed[:, width:])


def solution(mesh):
    rows = P(AXES, None)
    return jax.shard_map(
        on_device,
        mesh=mesh,
        in_specs=(rows, rows, P(), rows, rows),
        out_specs=(rows, rows),
        check_vma=False,
    )
```

```python
import jax
import jax.numpy as jnp
from jax import lax
from jax.experimental import pallas as pl
from jax.experimental.pallas import tpu as pltpu
from jax.sharding import PartitionSpec as P

DIN = 512
AXES = ("wide", "grp")
PAIR = 2
BLOCK = 128
NORM_ROWS = 16
LANES = 128
NORMS_WEIGHT = 400000
VMEM_LIMIT = 40 * 1024 * 1024
ROWS_BY_ROWS = (((1,), (1,)), ((), ()))


def scaled(rows, inv_len):
    factor = inv_len * DIN ** (-0.5)
    return (rows.astype(jnp.float32) * factor).astype(jnp.bfloat16)


def send_kernel(
    samples_hbm, inv_len_hbm, archive_hbm, mean_hbm, var_hbm,
    sent_hbm, inv_len_ref, archive_ref, mean_ref, var_ref, samples_ref, sent_ref, arrived,
):
    copies = [
        pltpu.make_async_copy(source, target, arrived.at[number])
        for number, (source, target) in enumerate((
            (samples_hbm, samples_ref),
            (inv_len_hbm, inv_len_ref),
            (archive_hbm, archive_ref),
            (mean_hbm, mean_ref),
            (var_hbm, var_ref),
            (sent_ref, sent_hbm),
        ))
    ]
    for copy in copies[:5]:
        copy.start()
    for copy in copies[:2]:
        copy.wait()
    samp_z = scaled(samples_ref[...], inv_len_ref[...])
    samp_z = samp_z.reshape((1, PAIR) + sent_ref.shape[1:])
    targets = sent_ref.shape[0] // PAIR
    sent_ref[...] = jnp.broadcast_to(samp_z, (targets,) + samp_z.shape[1:]).reshape(sent_ref.shape)
    copies[5].start()
    for copy in copies[2:]:
        copy.wait()


def runs_kernel(inv_len_ref, archive_ref, mean_ref, var_ref, pack_ref):
    runs = archive_ref.shape[0]
    width = mean_ref.shape[0]
    row = lax.broadcasted_iota(jnp.int32, (BLOCK, BLOCK), 0)
    column = lax.broadcasted_iota(jnp.int32, (BLOCK, BLOCK), 1)
    norms = []
    for first in range(0, runs, BLOCK):
        arch_z = scaled(archive_ref[first : first + BLOCK, :], inv_len_ref[...])
        pack_ref[first : first + BLOCK, :] = arch_z
        products = lax.dot_general(arch_z, arch_z, ROWS_BY_ROWS, preferred_element_type=jnp.float32)
        norms.append(jnp.sum(jnp.where(row == column, products, 0.0), axis=0, keepdims=True))
    pack_ref[runs : runs + width, :] = mean_ref[...]
    pack_ref[runs + width : runs + 2 * width, :] = jnp.zeros(mean_ref.shape, jnp.bfloat16)
    pack_ref[runs + 2 * width : runs + 3 * width, :] = var_ref[...]
    rest = jnp.broadcast_to(0.5 * jnp.concatenate(norms, axis=1), (NORM_ROWS, runs))
    part_row = lax.broadcasted_iota(jnp.int32, rest.shape, 0)
    parts = jnp.zeros(rest.shape, jnp.float32)
    for number in range(3):
        part = rest.astype(jnp.bfloat16).astype(jnp.float32)
        parts = jnp.where(part_row == number, part, parts)
        rest = rest - part
    pack_ref[runs + 3 * width :, :] = parts.astype(jnp.bfloat16)


def norms_kernel(samp_z_ref, norm_ref):
    def block(rows):
        wide_copy = samp_z_ref[rows, :].astype(jnp.float32)
        norm = 0.5 * jnp.sum(wide_copy * wide_copy, axis=-1, keepdims=True)
        norm_ref[rows, :] = jnp.broadcast_to(norm, (norm.shape[0], LANES))

    by_blocks(block, samp_z_ref.shape[0])


def sums_kernel(samp_z_ref, samp_norm_ref, own_ref, peer_ref, sums_ref):
    width = sums_ref.shape[1] // 2
    runs = own_ref.shape[0] - 3 * width - NORM_ROWS
    packs = (own_ref, peer_ref)

    def block(rows):
        samp_z = samp_z_ref[rows, :]
        samp_norm = samp_norm_ref[rows, :1]
        inner_prods = [
            lax.dot_general(
                samp_z, pack_ref[:runs, :], ROWS_BY_ROWS, preferred_element_type=jnp.float32
            )
            for pack_ref in packs
        ]
        kernels = []
        for inner_prod, pack_ref in zip(inner_prods, packs):
            norm_parts = pack_ref[runs + 3 * width :, :].astype(jnp.float32)
            arch_norm = jnp.sum(norm_parts, axis=0, keepdims=True)
            kernels.append(jnp.exp(inner_prod - samp_norm - arch_norm))
        total = None
        for kernel, pack_ref in zip(kernels, packs):
            for half, first in ((kernel, runs), (kernel * kernel, runs + width)):
                part = lax.dot_general(
                    half.astype(jnp.bfloat16),
                    pack_ref[first : first + 2 * width, :],
                    ROWS_BY_ROWS,
                    preferred_element_type=jnp.float32,
                )
                total = part if total is None else total + part
        sums_ref[rows, :] = total

    by_blocks(block, samp_z_ref.shape[0])


def by_blocks(block, count):
    if count <= BLOCK:
        block(slice(None))
    else:
        @pl.loop(0, count // BLOCK)
        def _(step):
            block(pl.ds(pl.multiple_of(step * BLOCK, BLOCK), BLOCK))


def call(kernel, out_shape, inputs, flops, transcendentals=0, in_space=pltpu.VMEM, scratch=()):
    moved = sum(array.size * array.dtype.itemsize for array in inputs)
    return pl.pallas_call(
        kernel,
        out_shape=out_shape,
        in_specs=[pl.BlockSpec(memory_space=in_space)] * len(inputs),
        out_specs=jax.tree.map(lambda out: pl.BlockSpec(memory_space=out.memory_space), out_shape),
        scratch_shapes=scratch,
        cost_estimate=pl.CostEstimate(
            flops=flops, bytes_accessed=moved, transcendentals=transcendentals
        ),
        compiler_params=pltpu.CompilerParams(vmem_limit_bytes=VMEM_LIMIT),
    )(*inputs)


def on_device(samples, archive, inv_len, mean_coef, var_coef):
    devices = lax.axis_size(AXES)
    grp = lax.axis_size("grp")
    own_rows = samples.shape[0]
    part_rows = own_rows // PAIR
    rows = devices * part_rows
    runs, width = mean_coef.shape

    arrays = (samples, inv_len.reshape(1, DIN), archive, mean_coef.T, var_coef.T)
    sent, *held = call(
        send_kernel,
        (pltpu.HBM((devices, part_rows, DIN), jnp.bfloat16),)
        + tuple(pltpu.VMEM(array.shape, array.dtype) for array in arrays[1:]),
        [pltpu.with_memory_space_constraint(array, pltpu.HBM) for array in arrays],
        flops=own_rows * DIN,
        in_space=pltpu.HBM,
        scratch=[
            pltpu.VMEM(samples.shape, samples.dtype),
            pltpu.VMEM((devices, part_rows, DIN), jnp.bfloat16),
            pltpu.SemaphoreType.DMA((6,)),
        ],
    )
    gathered = lax.all_to_all(sent, AXES, split_axis=0, concat_axis=0, tiled=True)
    own = call(
        runs_kernel,
        pltpu.VMEM((runs + 3 * width + NORM_ROWS, DIN), jnp.bfloat16),
        held,
        flops=2 * BLOCK * runs * DIN,
    )
    peer = lax.ppermute(own, "grp", [(i, i ^ 1) for i in range(grp)])
    samp_z = gathered.reshape(rows, DIN)
    samp_norm = call(
        norms_kernel,
        pltpu.VMEM((rows, LANES), jnp.float32),
        (samp_z,),
        flops=NORMS_WEIGHT * rows * DIN,
    )
    sums = call(
        sums_kernel,
        pltpu.VMEM((rows, 2 * width), jnp.float32),
        (samp_z, samp_norm, own, peer),
        flops=4 * rows * runs * (DIN + 4 * width),
        transcendentals=2 * rows * runs,
    )
    sums = sums.reshape(devices, part_rows, 2 * width)
    parts = lax.all_to_all(sums, AXES, split_axis=0, concat_axis=0, tiled=True)
    summed = jnp.sum(parts.reshape(devices // PAIR, own_rows, 2 * width), axis=0)
    return (summed[:, :width], 1.0 - summed[:, width:])


def solution(mesh):
    rows = P(AXES, None)
    return jax.shard_map(
        on_device,
        mesh=mesh,
        in_specs=(rows, rows, P(), rows, rows),
        out_specs=(rows, rows),
        check_vma=False,
    )
```

```python
import jax
import jax.numpy as jnp
from jax import lax
from jax.experimental import pallas as pl
from jax.experimental.pallas import tpu as pltpu
from jax.sharding import PartitionSpec as P

DIN = 512
AXES = ("wide", "grp")
PAIR = 2
BLOCK = 128
NORM_ROWS = 16
VMEM_LIMIT = 40 * 1024 * 1024
ROWS_BY_ROWS = (((1,), (1,)), ((), ()))


def scaled(rows, inv_len):
    factor = inv_len * DIN ** (-0.5)
    return (rows.astype(jnp.float32) * factor).astype(jnp.bfloat16)


def send_kernel(
    samples_hbm, inv_len_hbm, archive_hbm, mean_hbm, var_hbm,
    sent_ref, inv_len_ref, archive_ref, mean_ref, var_ref, samples_ref, arrived,
):
    copies = [
        pltpu.make_async_copy(source, target, arrived.at[number])
        for number, (source, target) in enumerate((
            (samples_hbm, samples_ref),
            (inv_len_hbm, inv_len_ref),
            (archive_hbm, archive_ref),
            (mean_hbm, mean_ref),
            (var_hbm, var_ref),
        ))
    ]
    for copy in copies:
        copy.start()
    for copy in copies[:2]:
        copy.wait()
    samp_z = scaled(samples_ref[...], inv_len_ref[...])
    samp_z = samp_z.reshape((1, PAIR) + sent_ref.shape[1:])
    targets = sent_ref.shape[0] // PAIR
    sent_ref[...] = jnp.broadcast_to(samp_z, (targets,) + samp_z.shape[1:]).reshape(sent_ref.shape)
    for copy in copies[2:]:
        copy.wait()


def runs_kernel(inv_len_ref, archive_ref, mean_ref, var_ref, pack_ref):
    runs = archive_ref.shape[0]
    width = mean_ref.shape[0]
    row = lax.broadcasted_iota(jnp.int32, (BLOCK, BLOCK), 0)
    column = lax.broadcasted_iota(jnp.int32, (BLOCK, BLOCK), 1)
    norms = []
    for first in range(0, runs, BLOCK):
        arch_z = scaled(archive_ref[first : first + BLOCK, :], inv_len_ref[...])
        pack_ref[first : first + BLOCK, :] = arch_z
        products = lax.dot_general(arch_z, arch_z, ROWS_BY_ROWS, preferred_element_type=jnp.float32)
        norms.append(jnp.sum(jnp.where(row == column, products, 0.0), axis=0, keepdims=True))
    pack_ref[runs : runs + width, :] = mean_ref[...]
    pack_ref[runs + width : runs + 2 * width, :] = jnp.zeros(mean_ref.shape, jnp.bfloat16)
    pack_ref[runs + 2 * width : runs + 3 * width, :] = var_ref[...]
    rest = jnp.broadcast_to(0.5 * jnp.concatenate(norms, axis=1), (NORM_ROWS, runs))
    part_row = lax.broadcasted_iota(jnp.int32, rest.shape, 0)
    parts = jnp.zeros(rest.shape, jnp.float32)
    for number in range(3):
        part = rest.astype(jnp.bfloat16).astype(jnp.float32)
        parts = jnp.where(part_row == number, part, parts)
        rest = rest - part
    pack_ref[runs + 3 * width :, :] = parts.astype(jnp.bfloat16)


def sums_kernel(samp_z_ref, own_ref, peer_ref, sums_ref):
    width = sums_ref.shape[1] // 2
    runs = own_ref.shape[0] - 3 * width - NORM_ROWS
    packs = (own_ref, peer_ref)

    def block(rows):
        samp_z = samp_z_ref[rows, :]
        wide_copy = samp_z.astype(jnp.float32)
        samp_norm = 0.5 * jnp.sum(wide_copy * wide_copy, axis=-1, keepdims=True)
        inner_prods = [
            lax.dot_general(
                samp_z, pack_ref[:runs, :], ROWS_BY_ROWS, preferred_element_type=jnp.float32
            )
            for pack_ref in packs
        ]
        kernels = []
        for inner_prod, pack_ref in zip(inner_prods, packs):
            norm_parts = pack_ref[runs + 3 * width :, :].astype(jnp.float32)
            arch_norm = jnp.sum(norm_parts, axis=0, keepdims=True)
            kernels.append(jnp.exp(inner_prod - samp_norm - arch_norm))
        total = None
        for kernel, pack_ref in zip(kernels, packs):
            for half, first in ((kernel, runs), (kernel * kernel, runs + width)):
                part = lax.dot_general(
                    half.astype(jnp.bfloat16),
                    pack_ref[first : first + 2 * width, :],
                    ROWS_BY_ROWS,
                    preferred_element_type=jnp.float32,
                )
                total = part if total is None else total + part
        sums_ref[rows, :] = total

    by_blocks(block, samp_z_ref.shape[0])


def outputs_kernel(parts_ref, mean_hbm, var_hbm, mean_ref, var_ref, written):
    width = mean_ref.shape[1]
    summed = jnp.sum(parts_ref[...], axis=0)
    mean_ref[...] = summed[:, :width]
    mean_copy = pltpu.make_async_copy(mean_ref, mean_hbm, written.at[0])
    mean_copy.start()
    var_ref[...] = 1.0 - summed[:, width:]
    var_copy = pltpu.make_async_copy(var_ref, var_hbm, written.at[1])
    var_copy.start()
    mean_copy.wait()
    var_copy.wait()


def by_blocks(block, count):
    if count <= BLOCK:
        block(slice(None))
    else:
        @pl.loop(0, count // BLOCK)
        def _(step):
            block(pl.ds(pl.multiple_of(step * BLOCK, BLOCK), BLOCK))


def call(kernel, out_shape, inputs, flops, transcendentals=0, in_space=pltpu.VMEM, scratch=()):
    moved = sum(array.size * array.dtype.itemsize for array in inputs)
    return pl.pallas_call(
        kernel,
        out_shape=out_shape,
        in_specs=[pl.BlockSpec(memory_space=in_space)] * len(inputs),
        out_specs=jax.tree.map(lambda out: pl.BlockSpec(memory_space=out.memory_space), out_shape),
        scratch_shapes=scratch,
        cost_estimate=pl.CostEstimate(
            flops=flops, bytes_accessed=moved, transcendentals=transcendentals
        ),
        compiler_params=pltpu.CompilerParams(vmem_limit_bytes=VMEM_LIMIT),
    )(*inputs)


def on_device(samples, archive, inv_len, mean_coef, var_coef):
    devices = lax.axis_size(AXES)
    grp = lax.axis_size("grp")
    own_rows = samples.shape[0]
    part_rows = own_rows // PAIR
    rows = devices * part_rows
    runs, width = mean_coef.shape

    arrays = (samples, inv_len.reshape(1, DIN), archive, mean_coef.T, var_coef.T)
    sent, *held = call(
        send_kernel,
        (pltpu.VMEM((devices, part_rows, DIN), jnp.bfloat16),)
        + tuple(pltpu.VMEM(array.shape, array.dtype) for array in arrays[1:]),
        [pltpu.with_memory_space_constraint(array, pltpu.HBM) for array in arrays],
        flops=own_rows * DIN,
        in_space=pltpu.HBM,
        scratch=[pltpu.VMEM(samples.shape, samples.dtype), pltpu.SemaphoreType.DMA((5,))],
    )
    gathered = lax.all_to_all(sent, AXES, split_axis=0, concat_axis=0, tiled=True)
    own = call(
        runs_kernel,
        pltpu.VMEM((runs + 3 * width + NORM_ROWS, DIN), jnp.bfloat16),
        held,
        flops=2 * BLOCK * runs * DIN,
    )
    peer = lax.ppermute(own, "grp", [(i, i ^ 1) for i in range(grp)])
    sums = call(
        sums_kernel,
        pltpu.VMEM((rows, 2 * width), jnp.float32),
        (gathered.reshape(rows, DIN), own, peer),
        flops=4 * rows * runs * (DIN + 4 * width),
        transcendentals=2 * rows * runs,
    )
    sums = sums.reshape(devices, part_rows, 2 * width)
    parts = lax.all_to_all(sums, AXES, split_axis=0, concat_axis=0, tiled=True)
    return tuple(call(
        outputs_kernel,
        (pltpu.HBM((own_rows, width), jnp.float32),) * 2,
        (parts.reshape(devices // PAIR, own_rows, 2 * width),),
        flops=parts.size,
        scratch=[pltpu.VMEM((own_rows, width), jnp.float32)] * 2 + [pltpu.SemaphoreType.DMA((2,))],
    ))


def solution(mesh):
    rows = P(AXES, None)
    return jax.shard_map(
        on_device,
        mesh=mesh,
        in_specs=(rows, rows, P(), rows, rows),
        out_specs=(rows, rows),
        check_vma=False,
    )
```

```python
import jax
import jax.numpy as jnp
from jax import lax
from jax.experimental import pallas as pl
from jax.experimental.pallas import tpu as pltpu
from jax.sharding import PartitionSpec as P

DIN = 512
AXES = ("wide", "grp")
RANKS = ("grp", "wide")
PAIR = 2
BLOCK = 128
NORM_ROWS = 16
VMEM_LIMIT = 40 * 1024 * 1024
ROWS_BY_ROWS = (((1,), (1,)), ((), ()))


def scaled(rows, inv_len):
    factor = inv_len * DIN ** (-0.5)
    return (rows.astype(jnp.float32) * factor).astype(jnp.bfloat16)


def send_kernel(
    samples_hbm, inv_len_hbm, archive_hbm, mean_hbm, var_hbm,
    sent_ref, inv_len_ref, archive_ref, mean_ref, var_ref, samples_ref, arrived,
):
    copies = [
        pltpu.make_async_copy(source, target, arrived.at[number])
        for number, (source, target) in enumerate((
            (samples_hbm, samples_ref),
            (inv_len_hbm, inv_len_ref),
            (archive_hbm, archive_ref),
            (mean_hbm, mean_ref),
            (var_hbm, var_ref),
        ))
    ]
    for copy in copies:
        copy.start()
    for copy in copies[:2]:
        copy.wait()
    samp_z = scaled(samples_ref[...], inv_len_ref[...])
    samp_z = samp_z.reshape((1, PAIR, 1) + sent_ref.shape[3:])
    sent_ref[...] = jnp.broadcast_to(samp_z, sent_ref.shape)
    for copy in copies[2:]:
        copy.wait()


def runs_kernel(inv_len_ref, archive_ref, mean_ref, var_ref, pack_ref):
    runs = archive_ref.shape[0]
    width = mean_ref.shape[0]
    row = lax.broadcasted_iota(jnp.int32, (BLOCK, BLOCK), 0)
    column = lax.broadcasted_iota(jnp.int32, (BLOCK, BLOCK), 1)
    norms = []
    for first in range(0, runs, BLOCK):
        arch_z = scaled(archive_ref[first : first + BLOCK, :], inv_len_ref[...])
        pack_ref[first : first + BLOCK, :] = arch_z
        products = lax.dot_general(arch_z, arch_z, ROWS_BY_ROWS, preferred_element_type=jnp.float32)
        norms.append(jnp.sum(jnp.where(row == column, products, 0.0), axis=0, keepdims=True))
    pack_ref[runs : runs + width, :] = mean_ref[...]
    pack_ref[runs + width : runs + 2 * width, :] = jnp.zeros(mean_ref.shape, jnp.bfloat16)
    pack_ref[runs + 2 * width : runs + 3 * width, :] = var_ref[...]
    rest = jnp.broadcast_to(0.5 * jnp.concatenate(norms, axis=1), (NORM_ROWS, runs))
    part_row = lax.broadcasted_iota(jnp.int32, rest.shape, 0)
    parts = jnp.zeros(rest.shape, jnp.float32)
    for number in range(3):
        part = rest.astype(jnp.bfloat16).astype(jnp.float32)
        parts = jnp.where(part_row == number, part, parts)
        rest = rest - part
    pack_ref[runs + 3 * width :, :] = parts.astype(jnp.bfloat16)


def sums_kernel(samp_z_ref, own_ref, peer_ref, sums_ref):
    width = sums_ref.shape[1] // 2
    runs = own_ref.shape[0] - 3 * width - NORM_ROWS
    packs = (own_ref, peer_ref)

    def block(rows):
        samp_z = samp_z_ref[rows, :]
        wide_copy = samp_z.astype(jnp.float32)
        samp_norm = 0.5 * jnp.sum(wide_copy * wide_copy, axis=-1, keepdims=True)
        inner_prods = [
            lax.dot_general(
                samp_z, pack_ref[:runs, :], ROWS_BY_ROWS, preferred_element_type=jnp.float32
            )
            for pack_ref in packs
        ]
        kernels = []
        for inner_prod, pack_ref in zip(inner_prods, packs):
            norm_parts = pack_ref[runs + 3 * width :, :].astype(jnp.float32)
            arch_norm = jnp.sum(norm_parts, axis=0, keepdims=True)
            kernels.append(jnp.exp(inner_prod - samp_norm - arch_norm))
        total = None
        for kernel, pack_ref in zip(kernels, packs):
            for half, first in ((kernel, runs), (kernel * kernel, runs + width)):
                part = lax.dot_general(
                    half.astype(jnp.bfloat16),
                    pack_ref[first : first + 2 * width, :],
                    ROWS_BY_ROWS,
                    preferred_element_type=jnp.float32,
                )
                total = part if total is None else total + part
        sums_ref[rows, :] = total

    by_blocks(block, samp_z_ref.shape[0])


def outputs_kernel(parts_ref, mean_hbm, var_hbm, mean_ref, var_ref, written):
    width = mean_ref.shape[1]
    summed = jnp.sum(parts_ref[...], axis=(0, 2))
    summed = summed.reshape(mean_ref.shape[0], 2 * width)
    mean_ref[...] = summed[:, :width]
    mean_copy = pltpu.make_async_copy(mean_ref, mean_hbm, written.at[0])
    mean_copy.start()
    var_ref[...] = 1.0 - summed[:, width:]
    var_copy = pltpu.make_async_copy(var_ref, var_hbm, written.at[1])
    var_copy.start()
    mean_copy.wait()
    var_copy.wait()


def by_blocks(block, count):
    if count <= BLOCK:
        block(slice(None))
    else:
        @pl.loop(0, count // BLOCK)
        def _(step):
            block(pl.ds(pl.multiple_of(step * BLOCK, BLOCK), BLOCK))


def call(kernel, out_shape, inputs, flops, transcendentals=0, in_space=pltpu.VMEM, scratch=()):
    moved = sum(array.size * array.dtype.itemsize for array in inputs)
    return pl.pallas_call(
        kernel,
        out_shape=out_shape,
        in_specs=[pl.BlockSpec(memory_space=in_space)] * len(inputs),
        out_specs=jax.tree.map(lambda out: pl.BlockSpec(memory_space=out.memory_space), out_shape),
        scratch_shapes=scratch,
        cost_estimate=pl.CostEstimate(
            flops=flops, bytes_accessed=moved, transcendentals=transcendentals
        ),
        compiler_params=pltpu.CompilerParams(vmem_limit_bytes=VMEM_LIMIT),
    )(*inputs)


def on_device(samples, archive, inv_len, mean_coef, var_coef):
    devices = lax.axis_size(AXES)
    grp = lax.axis_size("grp")
    own_rows = samples.shape[0]
    part_rows = own_rows // PAIR
    rows = devices * part_rows
    slots = (grp // PAIR, PAIR, lax.axis_size("wide"))
    runs, width = mean_coef.shape

    arrays = (samples, inv_len.reshape(1, DIN), archive, mean_coef.T, var_coef.T)
    sent, *held = call(
        send_kernel,
        (pltpu.VMEM(slots + (part_rows, DIN), jnp.bfloat16),)
        + tuple(pltpu.VMEM(array.shape, array.dtype) for array in arrays[1:]),
        [pltpu.with_memory_space_constraint(array, pltpu.HBM) for array in arrays],
        flops=own_rows * DIN,
        in_space=pltpu.HBM,
        scratch=[pltpu.VMEM(samples.shape, samples.dtype), pltpu.SemaphoreType.DMA((5,))],
    )
    gathered = lax.all_to_all(sent.reshape(devices, part_rows, DIN), RANKS, split_axis=0, concat_axis=0, tiled=True)
    own = call(
        runs_kernel,
        pltpu.VMEM((runs + 3 * width + NORM_ROWS, DIN), jnp.bfloat16),
        held,
        flops=2 * BLOCK * runs * DIN,
    )
    peer = lax.ppermute(own, "grp", [(i, i ^ 1) for i in range(grp)])
    sums = call(
        sums_kernel,
        pltpu.VMEM((rows, 2 * width), jnp.float32),
        (gathered.reshape(rows, DIN), own, peer),
        flops=4 * rows * runs * (DIN + 4 * width),
        transcendentals=2 * rows * runs,
    )
    sums = sums.reshape(devices, part_rows, 2 * width)
    parts = lax.all_to_all(sums, RANKS, split_axis=0, concat_axis=0, tiled=True)
    return tuple(call(
        outputs_kernel,
        (pltpu.HBM((own_rows, width), jnp.float32),) * 2,
        (parts.reshape(slots + (part_rows, 2 * width)),),
        flops=parts.size,
        scratch=[pltpu.VMEM((own_rows, width), jnp.float32)] * 2 + [pltpu.SemaphoreType.DMA((2,))],
    ))


def solution(mesh):
    rows = P(AXES, None)
    return jax.shard_map(
        on_device,
        mesh=mesh,
        in_specs=(rows, rows, P(), rows, rows),
        out_specs=(rows, rows),
        check_vma=False,
    )
```

```python
import jax
import jax.numpy as jnp
from jax import lax
from jax.experimental import pallas as pl
from jax.experimental.pallas import tpu as pltpu
from jax.sharding import PartitionSpec as P

DIN = 512
AXES = ("wide", "grp")
RANKS = ("grp", "wide")
PAIR = 2
BLOCK = 128
NORM_ROWS = 16
VMEM_LIMIT = 40 * 1024 * 1024
ROWS_BY_ROWS = (((1,), (1,)), ((), ()))


def scaled(rows, inv_len):
    factor = inv_len * DIN ** (-0.5)
    return (rows.astype(jnp.float32) * factor).astype(jnp.bfloat16)


def send_kernel(
    samples_hbm, inv_len_hbm, archive_hbm, mean_hbm, var_hbm,
    sent_ref, inv_len_ref, archive_ref, mean_ref, var_ref, samples_ref, arrived,
):
    half = archive_hbm.shape[0] // 2
    copies = [
        pltpu.make_async_copy(source, target, arrived.at[number])
        for number, (source, target) in enumerate((
            (archive_hbm.at[pl.ds(0, half)], archive_ref.at[pl.ds(0, half)]),
            (archive_hbm.at[pl.ds(half, half)], archive_ref.at[pl.ds(half, half)]),
            (samples_hbm, samples_ref),
            (inv_len_hbm, inv_len_ref),
            (mean_hbm, mean_ref),
            (var_hbm, var_ref),
        ))
    ]
    for copy in copies:
        copy.start()
    for copy in copies[2:4]:
        copy.wait()
    samp_z = scaled(samples_ref[...], inv_len_ref[...])
    samp_z = samp_z.reshape((1, PAIR, 1) + sent_ref.shape[3:])
    sent_ref[...] = jnp.broadcast_to(samp_z, sent_ref.shape)
    for copy in copies[:2] + copies[4:]:
        copy.wait()


def runs_kernel(inv_len_ref, archive_ref, mean_ref, var_ref, pack_ref):
    runs = archive_ref.shape[0]
    width = mean_ref.shape[0]
    row = lax.broadcasted_iota(jnp.int32, (BLOCK, BLOCK), 0)
    column = lax.broadcasted_iota(jnp.int32, (BLOCK, BLOCK), 1)
    norms = []
    for first in range(0, runs, BLOCK):
        arch_z = scaled(archive_ref[first : first + BLOCK, :], inv_len_ref[...])
        pack_ref[first : first + BLOCK, :] = arch_z
        products = lax.dot_general(arch_z, arch_z, ROWS_BY_ROWS, preferred_element_type=jnp.float32)
        norms.append(jnp.sum(jnp.where(row == column, products, 0.0), axis=0, keepdims=True))
    pack_ref[runs : runs + width, :] = mean_ref[...]
    pack_ref[runs + width : runs + 2 * width, :] = jnp.zeros(mean_ref.shape, jnp.bfloat16)
    pack_ref[runs + 2 * width : runs + 3 * width, :] = var_ref[...]
    rest = jnp.broadcast_to(0.5 * jnp.concatenate(norms, axis=1), (NORM_ROWS, runs))
    part_row = lax.broadcasted_iota(jnp.int32, rest.shape, 0)
    parts = jnp.zeros(rest.shape, jnp.float32)
    for number in range(3):
        part = rest.astype(jnp.bfloat16).astype(jnp.float32)
        parts = jnp.where(part_row == number, part, parts)
        rest = rest - part
    pack_ref[runs + 3 * width :, :] = parts.astype(jnp.bfloat16)


def sums_kernel(samp_z_ref, own_ref, peer_ref, sums_ref):
    width = sums_ref.shape[1] // 2
    runs = own_ref.shape[0] - 3 * width - NORM_ROWS
    packs = (own_ref, peer_ref)

    def block(rows):
        samp_z = samp_z_ref[rows, :]
        wide_copy = samp_z.astype(jnp.float32)
        samp_norm = 0.5 * jnp.sum(wide_copy * wide_copy, axis=-1, keepdims=True)
        inner_prods = [
            lax.dot_general(
                samp_z, pack_ref[:runs, :], ROWS_BY_ROWS, preferred_element_type=jnp.float32
            )
            for pack_ref in packs
        ]
        kernels = []
        for inner_prod, pack_ref in zip(inner_prods, packs):
            norm_parts = pack_ref[runs + 3 * width :, :].astype(jnp.float32)
            arch_norm = jnp.sum(norm_parts, axis=0, keepdims=True)
            kernels.append(jnp.exp(inner_prod - samp_norm - arch_norm))
        total = None
        for kernel, pack_ref in zip(kernels, packs):
            for half, first in ((kernel, runs), (kernel * kernel, runs + width)):
                part = lax.dot_general(
                    half.astype(jnp.bfloat16),
                    pack_ref[first : first + 2 * width, :],
                    ROWS_BY_ROWS,
                    preferred_element_type=jnp.float32,
                )
                total = part if total is None else total + part
        sums_ref[rows, :] = total

    by_blocks(block, samp_z_ref.shape[0])


def outputs_kernel(parts_ref, mean_hbm, var_hbm, mean_ref, var_ref, written):
    width = mean_ref.shape[1]
    summed = jnp.sum(parts_ref[...], axis=(0, 2))
    summed = summed.reshape(mean_ref.shape[0], 2 * width)
    mean_ref[...] = summed[:, :width]
    mean_copy = pltpu.make_async_copy(mean_ref, mean_hbm, written.at[0])
    mean_copy.start()
    var_ref[...] = 1.0 - summed[:, width:]
    var_copy = pltpu.make_async_copy(var_ref, var_hbm, written.at[1])
    var_copy.start()
    mean_copy.wait()
    var_copy.wait()


def by_blocks(block, count):
    if count <= BLOCK:
        block(slice(None))
    else:
        @pl.loop(0, count // BLOCK)
        def _(step):
            block(pl.ds(pl.multiple_of(step * BLOCK, BLOCK), BLOCK))


def call(kernel, out_shape, inputs, flops, transcendentals=0, in_space=pltpu.VMEM, scratch=()):
    moved = sum(array.size * array.dtype.itemsize for array in inputs)
    return pl.pallas_call(
        kernel,
        out_shape=out_shape,
        in_specs=[pl.BlockSpec(memory_space=in_space)] * len(inputs),
        out_specs=jax.tree.map(lambda out: pl.BlockSpec(memory_space=out.memory_space), out_shape),
        scratch_shapes=scratch,
        cost_estimate=pl.CostEstimate(
            flops=flops, bytes_accessed=moved, transcendentals=transcendentals
        ),
        compiler_params=pltpu.CompilerParams(vmem_limit_bytes=VMEM_LIMIT),
    )(*inputs)


def on_device(samples, archive, inv_len, mean_coef, var_coef):
    devices = lax.axis_size(AXES)
    grp = lax.axis_size("grp")
    own_rows = samples.shape[0]
    part_rows = own_rows // PAIR
    rows = devices * part_rows
    slots = (grp // PAIR, PAIR, lax.axis_size("wide"))
    runs, width = mean_coef.shape

    arrays = (samples, inv_len.reshape(1, DIN), archive, mean_coef.T, var_coef.T)
    sent, *held = call(
        send_kernel,
        (pltpu.VMEM(slots + (part_rows, DIN), jnp.bfloat16),)
        + tuple(pltpu.VMEM(array.shape, array.dtype) for array in arrays[1:]),
        [pltpu.with_memory_space_constraint(array, pltpu.HBM) for array in arrays],
        flops=own_rows * DIN,
        in_space=pltpu.HBM,
        scratch=[pltpu.VMEM(samples.shape, samples.dtype), pltpu.SemaphoreType.DMA((6,))],
    )
    gathered = lax.all_to_all(sent.reshape(devices, part_rows, DIN), RANKS, split_axis=0, concat_axis=0, tiled=True)
    own = call(
        runs_kernel,
        pltpu.VMEM((runs + 3 * width + NORM_ROWS, DIN), jnp.bfloat16),
        held,
        flops=2 * BLOCK * runs * DIN,
    )
    peer = lax.ppermute(own, "grp", [(i, i ^ 1) for i in range(grp)])
    sums = call(
        sums_kernel,
        pltpu.VMEM((rows, 2 * width), jnp.float32),
        (gathered.reshape(rows, DIN), own, peer),
        flops=4 * rows * runs * (DIN + 4 * width),
        transcendentals=2 * rows * runs,
    )
    sums = sums.reshape(devices, part_rows, 2 * width)
    parts = lax.all_to_all(sums, RANKS, split_axis=0, concat_axis=0, tiled=True)
    return tuple(call(
        outputs_kernel,
        (pltpu.HBM((own_rows, width), jnp.float32),) * 2,
        (parts.reshape(slots + (part_rows, 2 * width)),),
        flops=parts.size,
        scratch=[pltpu.VMEM((own_rows, width), jnp.float32)] * 2 + [pltpu.SemaphoreType.DMA((2,))],
    ))


def solution(mesh):
    rows = P(AXES, None)
    return jax.shard_map(
        on_device,
        mesh=mesh,
        in_specs=(rows, rows, P(), rows, rows),
        out_specs=(rows, rows),
        check_vma=False,
    )
```

```python
import jax
import jax.numpy as jnp
from jax import lax
from jax.experimental import pallas as pl
from jax.experimental.pallas import tpu as pltpu
from jax.sharding import PartitionSpec as P

DIN = 512
AXES = ("wide", "grp")
RANKS = ("grp", "wide")
PAIR = 2
BLOCK = 128
NORM_ROWS = 16
VMEM_LIMIT = 40 * 1024 * 1024
ROWS_BY_ROWS = (((1,), (1,)), ((), ()))


def scaled(rows, inv_len):
    factor = inv_len * DIN ** (-0.5)
    return (rows.astype(jnp.float32) * factor).astype(jnp.bfloat16)


def send_kernel(
    samples_hbm, inv_len_hbm, archive_hbm, mean_hbm, var_hbm,
    sent_ref, inv_len_ref, archive_ref, mean_ref, var_ref, samples_ref, arrived,
):
    copies = [
        pltpu.make_async_copy(source, target, arrived.at[number])
        for number, (source, target) in enumerate((
            (samples_hbm, samples_ref),
            (inv_len_hbm, inv_len_ref),
            (archive_hbm, archive_ref),
            (mean_hbm, mean_ref),
            (var_hbm, var_ref),
        ))
    ]
    for copy in copies:
        copy.start()
    for copy in copies[:2]:
        copy.wait()
    samp_z = scaled(samples_ref[...], inv_len_ref[...])
    samp_z = samp_z.reshape((1, PAIR, 1) + sent_ref.shape[3:])
    sent_ref[...] = jnp.broadcast_to(samp_z, sent_ref.shape)
    for copy in copies[2:]:
        copy.wait()


def runs_kernel(inv_len_ref, archive_ref, mean_ref, var_ref, pack_ref):
    runs = archive_ref.shape[0]
    width = mean_ref.shape[0]
    row = lax.broadcasted_iota(jnp.int32, (BLOCK, BLOCK), 0)
    column = lax.broadcasted_iota(jnp.int32, (BLOCK, BLOCK), 1)
    norms = []
    for first in range(0, runs, BLOCK):
        arch_z = scaled(archive_ref[first : first + BLOCK, :], inv_len_ref[...])
        pack_ref[first : first + BLOCK, :] = arch_z
        products = lax.dot_general(arch_z, arch_z, ROWS_BY_ROWS, preferred_element_type=jnp.float32)
        norms.append(jnp.sum(jnp.where(row == column, products, 0.0), axis=0, keepdims=True))
    pack_ref[runs : runs + width, :] = mean_ref[...]
    pack_ref[runs + width : runs + 2 * width, :] = var_ref[...]
    rest = jnp.broadcast_to(0.5 * jnp.concatenate(norms, axis=1), (NORM_ROWS, runs))
    part_row = lax.broadcasted_iota(jnp.int32, rest.shape, 0)
    parts = jnp.zeros(rest.shape, jnp.float32)
    for number in range(3):
        part = rest.astype(jnp.bfloat16).astype(jnp.float32)
        parts = jnp.where(part_row == number, part, parts)
        rest = rest - part
    pack_ref[runs + 2 * width :, :] = parts.astype(jnp.bfloat16)


def sums_kernel(samp_z_ref, own_ref, peer_ref, sums_ref):
    width = sums_ref.shape[1] // 2
    runs = own_ref.shape[0] - 2 * width - NORM_ROWS
    packs = (own_ref, peer_ref)

    def block(rows):
        samp_z = samp_z_ref[rows, :]
        wide_copy = samp_z.astype(jnp.float32)
        samp_norm = 0.5 * jnp.sum(wide_copy * wide_copy, axis=-1, keepdims=True)
        inner_prods = [
            lax.dot_general(
                samp_z, pack_ref[:runs, :], ROWS_BY_ROWS, preferred_element_type=jnp.float32
            )
            for pack_ref in packs
        ]
        kernels = []
        for inner_prod, pack_ref in zip(inner_prods, packs):
            norm_parts = pack_ref[runs + 2 * width :, :].astype(jnp.float32)
            arch_norm = jnp.sum(norm_parts, axis=0, keepdims=True)
            kernels.append(jnp.exp(inner_prod - samp_norm - arch_norm))
        total = None
        for kernel, pack_ref in zip(kernels, packs):
            both = jnp.concatenate([kernel, kernel * kernel], axis=0).astype(jnp.bfloat16)
            part = lax.dot_general(
                both,
                pack_ref[runs : runs + 2 * width, :],
                ROWS_BY_ROWS,
                preferred_element_type=jnp.float32,
            )
            total = part if total is None else total + part
        count = samp_z.shape[0]
        lane = lax.broadcasted_iota(jnp.int32, (count, 2 * width), 1)
        sums_ref[rows, :] = jnp.where(lane < width, total[:count], total[count:])

    by_blocks(block, samp_z_ref.shape[0])


def outputs_kernel(parts_ref, mean_hbm, var_hbm, mean_ref, var_ref, written):
    width = mean_ref.shape[1]
    summed = jnp.sum(parts_ref[...], axis=(0, 2))
    summed = summed.reshape(mean_ref.shape[0], 2 * width)
    mean_ref[...] = summed[:, :width]
    mean_copy = pltpu.make_async_copy(mean_ref, mean_hbm, written.at[0])
    mean_copy.start()
    var_ref[...] = 1.0 - summed[:, width:]
    var_copy = pltpu.make_async_copy(var_ref, var_hbm, written.at[1])
    var_copy.start()
    mean_copy.wait()
    var_copy.wait()


def by_blocks(block, count):
    if count <= BLOCK:
        block(slice(None))
    else:
        @pl.loop(0, count // BLOCK)
        def _(step):
            block(pl.ds(pl.multiple_of(step * BLOCK, BLOCK), BLOCK))


def call(kernel, out_shape, inputs, flops, transcendentals=0, in_space=pltpu.VMEM, scratch=()):
    moved = sum(array.size * array.dtype.itemsize for array in inputs)
    return pl.pallas_call(
        kernel,
        out_shape=out_shape,
        in_specs=[pl.BlockSpec(memory_space=in_space)] * len(inputs),
        out_specs=jax.tree.map(lambda out: pl.BlockSpec(memory_space=out.memory_space), out_shape),
        scratch_shapes=scratch,
        cost_estimate=pl.CostEstimate(
            flops=flops, bytes_accessed=moved, transcendentals=transcendentals
        ),
        compiler_params=pltpu.CompilerParams(vmem_limit_bytes=VMEM_LIMIT),
    )(*inputs)


def on_device(samples, archive, inv_len, mean_coef, var_coef):
    devices = lax.axis_size(AXES)
    grp = lax.axis_size("grp")
    own_rows = samples.shape[0]
    part_rows = own_rows // PAIR
    rows = devices * part_rows
    slots = (grp // PAIR, PAIR, lax.axis_size("wide"))
    runs, width = mean_coef.shape

    arrays = (samples, inv_len.reshape(1, DIN), archive, mean_coef.T, var_coef.T)
    sent, *held = call(
        send_kernel,
        (pltpu.VMEM(slots + (part_rows, DIN), jnp.bfloat16),)
        + tuple(pltpu.VMEM(array.shape, array.dtype) for array in arrays[1:]),
        [pltpu.with_memory_space_constraint(array, pltpu.HBM) for array in arrays],
        flops=own_rows * DIN,
        in_space=pltpu.HBM,
        scratch=[pltpu.VMEM(samples.shape, samples.dtype), pltpu.SemaphoreType.DMA((5,))],
    )
    gathered = lax.all_to_all(sent.reshape(devices, part_rows, DIN), RANKS, split_axis=0, concat_axis=0, tiled=True)
    own = call(
        runs_kernel,
        pltpu.VMEM((runs + 2 * width + NORM_ROWS, DIN), jnp.bfloat16),
        held,
        flops=2 * BLOCK * runs * DIN,
    )
    peer = lax.ppermute(own, "grp", [(i, i ^ 1) for i in range(grp)])
    sums = call(
        sums_kernel,
        pltpu.VMEM((rows, 2 * width), jnp.float32),
        (gathered.reshape(rows, DIN), own, peer),
        flops=4 * rows * runs * (DIN + 4 * width),
        transcendentals=2 * rows * runs,
    )
    sums = sums.reshape(devices, part_rows, 2 * width)
    parts = lax.all_to_all(sums, RANKS, split_axis=0, concat_axis=0, tiled=True)
    return tuple(call(
        outputs_kernel,
        (pltpu.HBM((own_rows, width), jnp.float32),) * 2,
        (parts.reshape(slots + (part_rows, 2 * width)),),
        flops=parts.size,
        scratch=[pltpu.VMEM((own_rows, width), jnp.float32)] * 2 + [pltpu.SemaphoreType.DMA((2,))],
    ))


def solution(mesh):
    rows = P(AXES, None)
    return jax.shard_map(
        on_device,
        mesh=mesh,
        in_specs=(rows, rows, P(), rows, rows),
        out_specs=(rows, rows),
        check_vma=False,
    )
```

```python
import jax
import jax.numpy as jnp
from jax import lax
from jax.experimental import pallas as pl
from jax.experimental.pallas import tpu as pltpu
from jax.sharding import PartitionSpec as P

DIN = 512
AXES = ("wide", "grp")
RANKS = ("grp", "wide")
PAIR = 2
BLOCK = 128
NORM_ROWS = 16
VMEM_LIMIT = 40 * 1024 * 1024
ROWS_BY_ROWS = (((1,), (1,)), ((), ()))


def scaled(rows, inv_len):
    factor = inv_len * DIN ** (-0.5)
    return (rows.astype(jnp.float32) * factor).astype(jnp.bfloat16)


def send_kernel(
    samples_hbm, inv_len_hbm, archive_hbm, mean_hbm, var_hbm,
    sent_ref, inv_len_ref, archive_ref, mean_ref, var_ref, samples_ref, arrived,
):
    copies = [
        pltpu.make_async_copy(source, target, arrived.at[number])
        for number, (source, target) in enumerate((
            (samples_hbm, samples_ref),
            (inv_len_hbm, inv_len_ref),
            (archive_hbm, archive_ref),
            (mean_hbm, mean_ref),
            (var_hbm, var_ref),
        ))
    ]
    for copy in copies:
        copy.start()
    for copy in copies[:2]:
        copy.wait()
    samp_z = scaled(samples_ref[...], inv_len_ref[...])
    samp_z = samp_z.reshape((1, PAIR, 1) + sent_ref.shape[3:])
    sent_ref[...] = jnp.broadcast_to(samp_z, sent_ref.shape)
    for copy in copies[2:]:
        copy.wait()


def runs_kernel(inv_len_ref, archive_ref, mean_ref, var_ref, pack_ref):
    runs = archive_ref.shape[0]
    width = mean_ref.shape[0]
    row = lax.broadcasted_iota(jnp.int32, (BLOCK, BLOCK), 0)
    column = lax.broadcasted_iota(jnp.int32, (BLOCK, BLOCK), 1)
    norms = []
    for first in range(0, runs, BLOCK):
        arch_z = scaled(archive_ref[first : first + BLOCK, :], inv_len_ref[...])
        turned = arch_z.T
        pack_ref[:DIN, first : first + BLOCK] = turned
        products = jnp.dot(arch_z, turned, preferred_element_type=jnp.float32)
        norms.append(jnp.sum(jnp.where(row == column, products, 0.0), axis=0, keepdims=True))
    pack_ref[DIN : DIN + width, :] = mean_ref[...]
    pack_ref[DIN + width : DIN + 2 * width, :] = var_ref[...]
    rest = jnp.broadcast_to(0.5 * jnp.concatenate(norms, axis=1), (NORM_ROWS, runs))
    part_row = lax.broadcasted_iota(jnp.int32, rest.shape, 0)
    parts = jnp.zeros(rest.shape, jnp.float32)
    for number in range(3):
        part = rest.astype(jnp.bfloat16).astype(jnp.float32)
        parts = jnp.where(part_row == number, part, parts)
        rest = rest - part
    pack_ref[DIN + 2 * width :, :] = parts.astype(jnp.bfloat16)


def sums_kernel(samp_z_ref, own_ref, peer_ref, sums_ref):
    width = sums_ref.shape[1] // 2
    packs = (own_ref, peer_ref)

    def block(rows):
        samp_z = samp_z_ref[rows, :]
        wide_copy = samp_z.astype(jnp.float32)
        samp_norm = 0.5 * jnp.sum(wide_copy * wide_copy, axis=-1, keepdims=True)
        inner_prods = [
            jnp.dot(samp_z, pack_ref[:DIN, :], preferred_element_type=jnp.float32)
            for pack_ref in packs
        ]
        kernels = []
        for inner_prod, pack_ref in zip(inner_prods, packs):
            norm_parts = pack_ref[DIN + 2 * width :, :].astype(jnp.float32)
            arch_norm = jnp.sum(norm_parts, axis=0, keepdims=True)
            kernels.append(jnp.exp(inner_prod - samp_norm - arch_norm))
        total = None
        for kernel, pack_ref in zip(kernels, packs):
            both = jnp.concatenate([kernel, kernel * kernel], axis=0).astype(jnp.bfloat16)
            part = lax.dot_general(
                both,
                pack_ref[DIN : DIN + 2 * width, :],
                ROWS_BY_ROWS,
                preferred_element_type=jnp.float32,
            )
            total = part if total is None else total + part
        count = samp_z.shape[0]
        lane = lax.broadcasted_iota(jnp.int32, (count, 2 * width), 1)
        sums_ref[rows, :] = jnp.where(lane < width, total[:count], total[count:])

    by_blocks(block, samp_z_ref.shape[0])


def outputs_kernel(parts_ref, mean_hbm, var_hbm, mean_ref, var_ref, written):
    width = mean_ref.shape[1]
    summed = jnp.sum(parts_ref[...], axis=(0, 2))
    summed = summed.reshape(mean_ref.shape[0], 2 * width)
    mean_ref[...] = summed[:, :width]
    mean_copy = pltpu.make_async_copy(mean_ref, mean_hbm, written.at[0])
    mean_copy.start()
    var_ref[...] = 1.0 - summed[:, width:]
    var_copy = pltpu.make_async_copy(var_ref, var_hbm, written.at[1])
    var_copy.start()
    mean_copy.wait()
    var_copy.wait()


def by_blocks(block, count):
    if count <= BLOCK:
        block(slice(None))
    else:
        @pl.loop(0, count // BLOCK)
        def _(step):
            block(pl.ds(pl.multiple_of(step * BLOCK, BLOCK), BLOCK))


def call(kernel, out_shape, inputs, flops, transcendentals=0, in_space=pltpu.VMEM, scratch=()):
    moved = sum(array.size * array.dtype.itemsize for array in inputs)
    return pl.pallas_call(
        kernel,
        out_shape=out_shape,
        in_specs=[pl.BlockSpec(memory_space=in_space)] * len(inputs),
        out_specs=jax.tree.map(lambda out: pl.BlockSpec(memory_space=out.memory_space), out_shape),
        scratch_shapes=scratch,
        cost_estimate=pl.CostEstimate(
            flops=flops, bytes_accessed=moved, transcendentals=transcendentals
        ),
        compiler_params=pltpu.CompilerParams(vmem_limit_bytes=VMEM_LIMIT),
    )(*inputs)


def on_device(samples, archive, inv_len, mean_coef, var_coef):
    devices = lax.axis_size(AXES)
    grp = lax.axis_size("grp")
    own_rows = samples.shape[0]
    part_rows = own_rows // PAIR
    rows = devices * part_rows
    slots = (grp // PAIR, PAIR, lax.axis_size("wide"))
    runs, width = mean_coef.shape

    arrays = (samples, inv_len.reshape(1, DIN), archive, mean_coef.T, var_coef.T)
    sent, *held = call(
        send_kernel,
        (pltpu.VMEM(slots + (part_rows, DIN), jnp.bfloat16),)
        + tuple(pltpu.VMEM(array.shape, array.dtype) for array in arrays[1:]),
        [pltpu.with_memory_space_constraint(array, pltpu.HBM) for array in arrays],
        flops=own_rows * DIN,
        in_space=pltpu.HBM,
        scratch=[pltpu.VMEM(samples.shape, samples.dtype), pltpu.SemaphoreType.DMA((5,))],
    )
    gathered = lax.all_to_all(sent.reshape(devices, part_rows, DIN), RANKS, split_axis=0, concat_axis=0, tiled=True)
    own = call(
        runs_kernel,
        pltpu.VMEM((DIN + 2 * width + NORM_ROWS, runs), jnp.bfloat16),
        held,
        flops=2 * BLOCK * runs * DIN,
    )
    peer = lax.ppermute(own, "grp", [(i, i ^ 1) for i in range(grp)])
    sums = call(
        sums_kernel,
        pltpu.VMEM((rows, 2 * width), jnp.float32),
        (gathered.reshape(rows, DIN), own, peer),
        flops=4 * rows * runs * (DIN + 4 * width),
        transcendentals=2 * rows * runs,
    )
    sums = sums.reshape(devices, part_rows, 2 * width)
    parts = lax.all_to_all(sums, RANKS, split_axis=0, concat_axis=0, tiled=True)
    return tuple(call(
        outputs_kernel,
        (pltpu.HBM((own_rows, width), jnp.float32),) * 2,
        (parts.reshape(slots + (part_rows, 2 * width)),),
        flops=parts.size,
        scratch=[pltpu.VMEM((own_rows, width), jnp.float32)] * 2 + [pltpu.SemaphoreType.DMA((2,))],
    ))


def solution(mesh):
    rows = P(AXES, None)
    return jax.shard_map(
        on_device,
        mesh=mesh,
        in_specs=(rows, rows, P(), rows, rows),
        out_specs=(rows, rows),
        check_vma=False,
    )
```

```python
import jax
import jax.numpy as jnp
from jax import lax
from jax.experimental import pallas as pl
from jax.experimental.pallas import tpu as pltpu
from jax.sharding import PartitionSpec as P

DIN = 512
AXES = ("wide", "grp")
RANKS = ("grp", "wide")
PAIR = 2
BLOCK = 128
NORM_ROWS = 16
VMEM_LIMIT = 40 * 1024 * 1024


def scaled(rows, inv_len):
    factor = inv_len * DIN ** (-0.5)
    return (rows.astype(jnp.float32) * factor).astype(jnp.bfloat16)


def send_kernel(
    samples_hbm, inv_len_hbm, archive_hbm, mean_hbm, var_hbm,
    sent_ref, inv_len_ref, archive_ref, mean_ref, var_ref, samples_ref, arrived,
):
    copies = [
        pltpu.make_async_copy(source, target, arrived.at[number])
        for number, (source, target) in enumerate((
            (samples_hbm, samples_ref),
            (inv_len_hbm, inv_len_ref),
            (archive_hbm, archive_ref),
            (mean_hbm, mean_ref),
            (var_hbm, var_ref),
        ))
    ]
    for copy in copies:
        copy.start()
    for copy in copies[:2]:
        copy.wait()
    samp_z = scaled(samples_ref[...], inv_len_ref[...])
    samp_z = samp_z.reshape((1, PAIR, 1) + sent_ref.shape[3:])
    sent_ref[...] = jnp.broadcast_to(samp_z, sent_ref.shape)
    for copy in copies[2:]:
        copy.wait()


def runs_kernel(inv_len_ref, archive_ref, mean_ref, var_ref, pack_ref):
    runs = archive_ref.shape[0]
    width = mean_ref.shape[0]
    row = lax.broadcasted_iota(jnp.int32, (BLOCK, BLOCK), 0)
    column = lax.broadcasted_iota(jnp.int32, (BLOCK, BLOCK), 1)
    norms = []
    for first in range(0, runs, BLOCK):
        arch_z = scaled(archive_ref[first : first + BLOCK, :], inv_len_ref[...])
        turned = arch_z.T
        pack_ref[:DIN, first : first + BLOCK] = turned
        products = jnp.dot(arch_z, turned, preferred_element_type=jnp.float32)
        norms.append(jnp.sum(jnp.where(row == column, products, 0.0), axis=0, keepdims=True))
    coefs = jnp.concatenate([mean_ref[...], var_ref[...]], axis=0)
    for first in range(0, runs, 2 * width):
        block = slice(first, first + 2 * width)
        pack_ref[DIN : DIN + 2 * width, block] = coefs[:, block].T
    rest = jnp.broadcast_to(0.5 * jnp.concatenate(norms, axis=1), (NORM_ROWS, runs))
    part_row = lax.broadcasted_iota(jnp.int32, rest.shape, 0)
    parts = jnp.zeros(rest.shape, jnp.float32)
    for number in range(3):
        part = rest.astype(jnp.bfloat16).astype(jnp.float32)
        parts = jnp.where(part_row == number, part, parts)
        rest = rest - part
    pack_ref[DIN + 2 * width :, :] = parts.astype(jnp.bfloat16)


def sums_kernel(samp_z_ref, own_ref, peer_ref, sums_ref):
    width = sums_ref.shape[1] // 2
    packs = (own_ref, peer_ref)

    def block(rows):
        samp_z = samp_z_ref[rows, :]
        wide_copy = samp_z.astype(jnp.float32)
        samp_norm = 0.5 * jnp.sum(wide_copy * wide_copy, axis=-1, keepdims=True)
        inner_prods = [
            jnp.dot(samp_z, pack_ref[:DIN, :], preferred_element_type=jnp.float32)
            for pack_ref in packs
        ]
        kernels = []
        for inner_prod, pack_ref in zip(inner_prods, packs):
            norm_parts = pack_ref[DIN + 2 * width :, :].astype(jnp.float32)
            arch_norm = jnp.sum(norm_parts, axis=0, keepdims=True)
            kernels.append(jnp.exp(inner_prod - samp_norm - arch_norm))
        total = None
        for kernel, pack_ref in zip(kernels, packs):
            both = jnp.concatenate([kernel, kernel * kernel], axis=0).astype(jnp.bfloat16)
            blocks = range(0, pack_ref.shape[1], 2 * width)
            coefs = jnp.concatenate(
                [pack_ref[DIN : DIN + 2 * width, first : first + 2 * width] for first in blocks],
                axis=0,
            )
            part = jnp.dot(both, coefs, preferred_element_type=jnp.float32)
            total = part if total is None else total + part
        count = samp_z.shape[0]
        lane = lax.broadcasted_iota(jnp.int32, (count, 2 * width), 1)
        sums_ref[rows, :] = jnp.where(lane < width, total[:count], total[count:])

    by_blocks(block, samp_z_ref.shape[0])


def outputs_kernel(parts_ref, mean_hbm, var_hbm, mean_ref, var_ref, written):
    width = mean_ref.shape[1]
    summed = jnp.sum(parts_ref[...], axis=(0, 2))
    summed = summed.reshape(mean_ref.shape[0], 2 * width)
    mean_ref[...] = summed[:, :width]
    mean_copy = pltpu.make_async_copy(mean_ref, mean_hbm, written.at[0])
    mean_copy.start()
    var_ref[...] = 1.0 - summed[:, width:]
    var_copy = pltpu.make_async_copy(var_ref, var_hbm, written.at[1])
    var_copy.start()
    mean_copy.wait()
    var_copy.wait()


def by_blocks(block, count):
    if count <= BLOCK:
        block(slice(None))
    else:
        @pl.loop(0, count // BLOCK)
        def _(step):
            block(pl.ds(pl.multiple_of(step * BLOCK, BLOCK), BLOCK))


def call(kernel, out_shape, inputs, flops, transcendentals=0, in_space=pltpu.VMEM, scratch=()):
    moved = sum(array.size * array.dtype.itemsize for array in inputs)
    return pl.pallas_call(
        kernel,
        out_shape=out_shape,
        in_specs=[pl.BlockSpec(memory_space=in_space)] * len(inputs),
        out_specs=jax.tree.map(lambda out: pl.BlockSpec(memory_space=out.memory_space), out_shape),
        scratch_shapes=scratch,
        cost_estimate=pl.CostEstimate(
            flops=flops, bytes_accessed=moved, transcendentals=transcendentals
        ),
        compiler_params=pltpu.CompilerParams(vmem_limit_bytes=VMEM_LIMIT),
    )(*inputs)


def on_device(samples, archive, inv_len, mean_coef, var_coef):
    devices = lax.axis_size(AXES)
    grp = lax.axis_size("grp")
    own_rows = samples.shape[0]
    part_rows = own_rows // PAIR
    rows = devices * part_rows
    slots = (grp // PAIR, PAIR, lax.axis_size("wide"))
    runs, width = mean_coef.shape

    arrays = (samples, inv_len.reshape(1, DIN), archive, mean_coef.T, var_coef.T)
    sent, *held = call(
        send_kernel,
        (pltpu.VMEM(slots + (part_rows, DIN), jnp.bfloat16),)
        + tuple(pltpu.VMEM(array.shape, array.dtype) for array in arrays[1:]),
        [pltpu.with_memory_space_constraint(array, pltpu.HBM) for array in arrays],
        flops=own_rows * DIN,
        in_space=pltpu.HBM,
        scratch=[pltpu.VMEM(samples.shape, samples.dtype), pltpu.SemaphoreType.DMA((5,))],
    )
    gathered = lax.all_to_all(sent.reshape(devices, part_rows, DIN), RANKS, split_axis=0, concat_axis=0, tiled=True)
    own = call(
        runs_kernel,
        pltpu.VMEM((DIN + 2 * width + NORM_ROWS, runs), jnp.bfloat16),
        held,
        flops=2 * BLOCK * runs * DIN,
    )
    peer = lax.ppermute(own, "grp", [(i, i ^ 1) for i in range(grp)])
    sums = call(
        sums_kernel,
        pltpu.VMEM((rows, 2 * width), jnp.float32),
        (gathered.reshape(rows, DIN), own, peer),
        flops=4 * rows * runs * (DIN + 4 * width),
        transcendentals=2 * rows * runs,
    )
    sums = sums.reshape(devices, part_rows, 2 * width)
    parts = lax.all_to_all(sums, RANKS, split_axis=0, concat_axis=0, tiled=True)
    return tuple(call(
        outputs_kernel,
        (pltpu.HBM((own_rows, width), jnp.float32),) * 2,
        (parts.reshape(slots + (part_rows, 2 * width)),),
        flops=parts.size,
        scratch=[pltpu.VMEM((own_rows, width), jnp.float32)] * 2 + [pltpu.SemaphoreType.DMA((2,))],
    ))


def solution(mesh):
    rows = P(AXES, None)
    return jax.shard_map(
        on_device,
        mesh=mesh,
        in_specs=(rows, rows, P(), rows, rows),
        out_specs=(rows, rows),
        check_vma=False,
    )
```

```python
import jax
import jax.numpy as jnp
from jax import lax
from jax.experimental import pallas as pl
from jax.experimental.pallas import tpu as pltpu
from jax.sharding import PartitionSpec as P

DIN = 512
AXES = ("wide", "grp")
RANKS = ("grp", "wide")
PAIR = 2
BLOCK = 128
NORM_ROWS = 16
LANES = 128
NORMS_WEIGHT = 400000
VMEM_LIMIT = 40 * 1024 * 1024


def scaled(rows, inv_len):
    factor = inv_len * DIN ** (-0.5)
    return (rows.astype(jnp.float32) * factor).astype(jnp.bfloat16)


def send_kernel(
    samples_hbm, inv_len_hbm, archive_hbm, mean_hbm, var_hbm,
    sent_hbm, inv_len_ref, archive_ref, mean_ref, var_ref, samples_ref, sent_ref, arrived,
):
    copies = [
        pltpu.make_async_copy(source, target, arrived.at[number])
        for number, (source, target) in enumerate((
            (samples_hbm, samples_ref),
            (inv_len_hbm, inv_len_ref),
            (archive_hbm, archive_ref),
            (mean_hbm, mean_ref),
            (var_hbm, var_ref),
            (sent_ref, sent_hbm),
        ))
    ]
    for copy in copies[:5]:
        copy.start()
    for copy in copies[:2]:
        copy.wait()
    samp_z = scaled(samples_ref[...], inv_len_ref[...])
    samp_z = samp_z.reshape((1, PAIR, 1) + sent_ref.shape[3:])
    sent_ref[...] = jnp.broadcast_to(samp_z, sent_ref.shape)
    copies[5].start()
    for copy in copies[2:]:
        copy.wait()


def runs_kernel(inv_len_ref, archive_ref, mean_ref, var_ref, pack_ref):
    runs = archive_ref.shape[0]
    width = mean_ref.shape[0]
    row = lax.broadcasted_iota(jnp.int32, (BLOCK, BLOCK), 0)
    column = lax.broadcasted_iota(jnp.int32, (BLOCK, BLOCK), 1)
    norms = []
    for first in range(0, runs, BLOCK):
        arch_z = scaled(archive_ref[first : first + BLOCK, :], inv_len_ref[...])
        turned = arch_z.T
        pack_ref[:DIN, first : first + BLOCK] = turned
        products = jnp.dot(arch_z, turned, preferred_element_type=jnp.float32)
        norms.append(jnp.sum(jnp.where(row == column, products, 0.0), axis=0, keepdims=True))
    coefs = jnp.concatenate([mean_ref[...], var_ref[...]], axis=0)
    for first in range(0, runs, 2 * width):
        block = slice(first, first + 2 * width)
        pack_ref[DIN : DIN + 2 * width, block] = coefs[:, block].T
    rest = jnp.broadcast_to(0.5 * jnp.concatenate(norms, axis=1), (NORM_ROWS, runs))
    part_row = lax.broadcasted_iota(jnp.int32, rest.shape, 0)
    parts = jnp.zeros(rest.shape, jnp.float32)
    for number in range(3):
        part = rest.astype(jnp.bfloat16).astype(jnp.float32)
        parts = jnp.where(part_row == number, part, parts)
        rest = rest - part
    pack_ref[DIN + 2 * width :, :] = parts.astype(jnp.bfloat16)


def norms_kernel(samp_z_ref, norm_ref):
    def block(rows):
        wide_copy = samp_z_ref[rows, :].astype(jnp.float32)
        norm = 0.5 * jnp.sum(wide_copy * wide_copy, axis=-1, keepdims=True)
        norm_ref[rows, :] = jnp.broadcast_to(norm, (norm.shape[0], LANES))

    by_blocks(block, samp_z_ref.shape[0])


def sums_kernel(samp_z_ref, samp_norm_ref, own_ref, peer_ref, sums_ref):
    width = sums_ref.shape[1] // 2
    packs = (own_ref, peer_ref)

    def block(rows):
        samp_z = samp_z_ref[rows, :]
        samp_norm = samp_norm_ref[rows, :1]
        inner_prods = [
            jnp.dot(samp_z, pack_ref[:DIN, :], preferred_element_type=jnp.float32)
            for pack_ref in packs
        ]
        kernels = []
        for inner_prod, pack_ref in zip(inner_prods, packs):
            norm_parts = pack_ref[DIN + 2 * width :, :].astype(jnp.float32)
            arch_norm = jnp.sum(norm_parts, axis=0, keepdims=True)
            kernels.append(jnp.exp(inner_prod - samp_norm - arch_norm))
        total = None
        for kernel, pack_ref in zip(kernels, packs):
            both = jnp.concatenate([kernel, kernel * kernel], axis=0).astype(jnp.bfloat16)
            blocks = range(0, pack_ref.shape[1], 2 * width)
            coefs = jnp.concatenate(
                [pack_ref[DIN : DIN + 2 * width, first : first + 2 * width] for first in blocks],
                axis=0,
            )
            part = jnp.dot(both, coefs, preferred_element_type=jnp.float32)
            total = part if total is None else total + part
        count = samp_z.shape[0]
        lane = lax.broadcasted_iota(jnp.int32, (count, 2 * width), 1)
        sums_ref[rows, :] = jnp.where(lane < width, total[:count], total[count:])

    by_blocks(block, samp_z_ref.shape[0])


def outputs_kernel(parts_ref, mean_hbm, var_hbm, mean_ref, var_ref, written):
    width = mean_ref.shape[1]
    summed = jnp.sum(parts_ref[...], axis=(0, 2))
    summed = summed.reshape(mean_ref.shape[0], 2 * width)
    mean_ref[...] = summed[:, :width]
    mean_copy = pltpu.make_async_copy(mean_ref, mean_hbm, written.at[0])
    mean_copy.start()
    var_ref[...] = 1.0 - summed[:, width:]
    var_copy = pltpu.make_async_copy(var_ref, var_hbm, written.at[1])
    var_copy.start()
    mean_copy.wait()
    var_copy.wait()


def by_blocks(block, count):
    if count <= BLOCK:
        block(slice(None))
    else:
        @pl.loop(0, count // BLOCK)
        def _(step):
            block(pl.ds(pl.multiple_of(step * BLOCK, BLOCK), BLOCK))


def call(kernel, out_shape, inputs, flops, transcendentals=0, in_space=pltpu.VMEM, scratch=()):
    moved = sum(array.size * array.dtype.itemsize for array in inputs)
    return pl.pallas_call(
        kernel,
        out_shape=out_shape,
        in_specs=[pl.BlockSpec(memory_space=in_space)] * len(inputs),
        out_specs=jax.tree.map(lambda out: pl.BlockSpec(memory_space=out.memory_space), out_shape),
        scratch_shapes=scratch,
        cost_estimate=pl.CostEstimate(
            flops=flops, bytes_accessed=moved, transcendentals=transcendentals
        ),
        compiler_params=pltpu.CompilerParams(vmem_limit_bytes=VMEM_LIMIT),
    )(*inputs)


def on_device(samples, archive, inv_len, mean_coef, var_coef):
    devices = lax.axis_size(AXES)
    grp = lax.axis_size("grp")
    own_rows = samples.shape[0]
    part_rows = own_rows // PAIR
    rows = devices * part_rows
    slots = (grp // PAIR, PAIR, lax.axis_size("wide"))
    runs, width = mean_coef.shape

    arrays = (samples, inv_len.reshape(1, DIN), archive, mean_coef.T, var_coef.T)
    sent, *held = call(
        send_kernel,
        (pltpu.HBM(slots + (part_rows, DIN), jnp.bfloat16),)
        + tuple(pltpu.VMEM(array.shape, array.dtype) for array in arrays[1:]),
        [pltpu.with_memory_space_constraint(array, pltpu.HBM) for array in arrays],
        flops=own_rows * DIN,
        in_space=pltpu.HBM,
        scratch=[
            pltpu.VMEM(samples.shape, samples.dtype),
            pltpu.VMEM(slots + (part_rows, DIN), jnp.bfloat16),
            pltpu.SemaphoreType.DMA((6,)),
        ],
    )
    gathered = lax.all_to_all(sent.reshape(devices, part_rows, DIN), RANKS, split_axis=0, concat_axis=0, tiled=True)
    own = call(
        runs_kernel,
        pltpu.VMEM((DIN + 2 * width + NORM_ROWS, runs), jnp.bfloat16),
        held,
        flops=2 * BLOCK * runs * DIN,
    )
    peer = lax.ppermute(own, "grp", [(i, i ^ 1) for i in range(grp)])
    samp_z = gathered.reshape(rows, DIN)
    samp_norm = call(
        norms_kernel,
        pltpu.VMEM((rows, LANES), jnp.float32),
        (samp_z,),
        flops=NORMS_WEIGHT * rows * DIN,
    )
    sums = call(
        sums_kernel,
        pltpu.VMEM((rows, 2 * width), jnp.float32),
        (samp_z, samp_norm, own, peer),
        flops=4 * rows * runs * (DIN + 4 * width),
        transcendentals=2 * rows * runs,
    )
    sums = sums.reshape(devices, part_rows, 2 * width)
    parts = lax.all_to_all(sums, RANKS, split_axis=0, concat_axis=0, tiled=True)
    return tuple(call(
        outputs_kernel,
        (pltpu.HBM((own_rows, width), jnp.float32),) * 2,
        (parts.reshape(slots + (part_rows, 2 * width)),),
        flops=parts.size,
        scratch=[pltpu.VMEM((own_rows, width), jnp.float32)] * 2 + [pltpu.SemaphoreType.DMA((2,))],
    ))


def solution(mesh):
    rows = P(AXES, None)
    return jax.shard_map(
        on_device,
        mesh=mesh,
        in_specs=(rows, rows, P(), rows, rows),
        out_specs=(rows, rows),
        check_vma=False,
    )
```

```python
import jax
import jax.numpy as jnp
from jax import lax
from jax.experimental import pallas as pl
from jax.experimental.pallas import tpu as pltpu
from jax.sharding import PartitionSpec as P

DIN = 512
AXES = ("wide", "grp")
RANKS = ("grp", "wide")
PAIR = 2
BLOCK = 128
NORM_ROWS = 16
LANES = 128
NORMS_WEIGHT = 400000
VMEM_LIMIT = 40 * 1024 * 1024


def scaled(rows, inv_len):
    factor = inv_len * DIN ** (-0.5)
    return (rows.astype(jnp.float32) * factor).astype(jnp.bfloat16)


def load_kernel(inv_len_hbm, archive_hbm, mean_hbm, var_hbm, inv_len_ref, archive_ref, mean_ref, var_ref, arrived):
    copies = [
        pltpu.make_async_copy(source, target, arrived.at[number])
        for number, (source, target) in enumerate((
            (inv_len_hbm, inv_len_ref),
            (archive_hbm, archive_ref),
            (mean_hbm, mean_ref),
            (var_hbm, var_ref),
        ))
    ]
    for copy in copies:
        copy.start()
    for copy in copies:
        copy.wait()


def runs_kernel(inv_len_ref, archive_ref, mean_ref, var_ref, pack_ref):
    runs = archive_ref.shape[0]
    width = mean_ref.shape[0]
    row = lax.broadcasted_iota(jnp.int32, (BLOCK, BLOCK), 0)
    column = lax.broadcasted_iota(jnp.int32, (BLOCK, BLOCK), 1)
    norms = []
    for first in range(0, runs, BLOCK):
        arch_z = scaled(archive_ref[first : first + BLOCK, :], inv_len_ref[...])
        turned = arch_z.T
        pack_ref[:DIN, first : first + BLOCK] = turned
        products = jnp.dot(arch_z, turned, preferred_element_type=jnp.float32)
        norms.append(jnp.sum(jnp.where(row == column, products, 0.0), axis=0, keepdims=True))
    coefs = jnp.concatenate([mean_ref[...], var_ref[...]], axis=0)
    for first in range(0, runs, 2 * width):
        block = slice(first, first + 2 * width)
        pack_ref[DIN : DIN + 2 * width, block] = coefs[:, block].T
    rest = jnp.broadcast_to(0.5 * jnp.concatenate(norms, axis=1), (NORM_ROWS, runs))
    part_row = lax.broadcasted_iota(jnp.int32, rest.shape, 0)
    parts = jnp.zeros(rest.shape, jnp.float32)
    for number in range(3):
        part = rest.astype(jnp.bfloat16).astype(jnp.float32)
        parts = jnp.where(part_row == number, part, parts)
        rest = rest - part
    pack_ref[DIN + 2 * width :, :] = parts.astype(jnp.bfloat16)


def samples_kernel(inv_len_ref, samples_ref, samp_z_ref, norm_ref):
    def block(rows):
        samp_z = scaled(samples_ref[rows, :], inv_len_ref[...])
        samp_z_ref[rows, :] = samp_z
        wide_copy = samp_z.astype(jnp.float32)
        norm = 0.5 * jnp.sum(wide_copy * wide_copy, axis=-1, keepdims=True)
        norm_ref[rows, :] = jnp.broadcast_to(norm, (norm.shape[0], LANES))

    by_blocks(block, samples_ref.shape[0])


def sums_kernel(samp_z_ref, samp_norm_ref, own_ref, peer_ref, sums_ref):
    width = sums_ref.shape[1] // 2
    packs = (own_ref, peer_ref)

    def block(rows):
        samp_z = samp_z_ref[rows, :]
        samp_norm = samp_norm_ref[rows, :1]
        inner_prods = [
            jnp.dot(samp_z, pack_ref[:DIN, :], preferred_element_type=jnp.float32)
            for pack_ref in packs
        ]
        kernels = []
        for inner_prod, pack_ref in zip(inner_prods, packs):
            norm_parts = pack_ref[DIN + 2 * width :, :].astype(jnp.float32)
            arch_norm = jnp.sum(norm_parts, axis=0, keepdims=True)
            kernels.append(jnp.exp(inner_prod - samp_norm - arch_norm))
        total = None
        for kernel, pack_ref in zip(kernels, packs):
            both = jnp.concatenate([kernel, kernel * kernel], axis=0).astype(jnp.bfloat16)
            blocks = range(0, pack_ref.shape[1], 2 * width)
            coefs = jnp.concatenate(
                [pack_ref[DIN : DIN + 2 * width, first : first + 2 * width] for first in blocks],
                axis=0,
            )
            part = jnp.dot(both, coefs, preferred_element_type=jnp.float32)
            total = part if total is None else total + part
        count = samp_z.shape[0]
        lane = lax.broadcasted_iota(jnp.int32, (count, 2 * width), 1)
        sums_ref[rows, :] = jnp.where(lane < width, total[:count], total[count:])

    by_blocks(block, samp_z_ref.shape[0])


def outputs_kernel(parts_ref, mean_hbm, var_hbm, mean_ref, var_ref, written):
    width = mean_ref.shape[1]
    summed = jnp.sum(parts_ref[...], axis=(0, 2))
    summed = summed.reshape(mean_ref.shape[0], 2 * width)
    mean_ref[...] = summed[:, :width]
    mean_copy = pltpu.make_async_copy(mean_ref, mean_hbm, written.at[0])
    mean_copy.start()
    var_ref[...] = 1.0 - summed[:, width:]
    var_copy = pltpu.make_async_copy(var_ref, var_hbm, written.at[1])
    var_copy.start()
    mean_copy.wait()
    var_copy.wait()


def by_blocks(block, count):
    if count <= BLOCK:
        block(slice(None))
    else:
        @pl.loop(0, count // BLOCK)
        def _(step):
            block(pl.ds(pl.multiple_of(step * BLOCK, BLOCK), BLOCK))


def call(kernel, out_shape, inputs, flops, transcendentals=0, in_spaces=None, scratch=()):
    moved = sum(array.size * array.dtype.itemsize for array in inputs)
    in_spaces = in_spaces or [pltpu.VMEM] * len(inputs)
    inputs = [
        pltpu.with_memory_space_constraint(array, space) if space == pltpu.HBM else array
        for array, space in zip(inputs, in_spaces)
    ]
    return pl.pallas_call(
        kernel,
        out_shape=out_shape,
        in_specs=[pl.BlockSpec(memory_space=space) for space in in_spaces],
        out_specs=jax.tree.map(lambda out: pl.BlockSpec(memory_space=out.memory_space), out_shape),
        scratch_shapes=scratch,
        cost_estimate=pl.CostEstimate(
            flops=flops, bytes_accessed=moved, transcendentals=transcendentals
        ),
        compiler_params=pltpu.CompilerParams(vmem_limit_bytes=VMEM_LIMIT),
    )(*inputs)


def on_device(samples, archive, inv_len, mean_coef, var_coef):
    devices = lax.axis_size(AXES)
    grp = lax.axis_size("grp")
    own_rows = samples.shape[0]
    part_rows = own_rows // PAIR
    rows = devices * part_rows
    slots = (grp // PAIR, PAIR, lax.axis_size("wide"))
    runs, width = mean_coef.shape

    arrays = (inv_len.reshape(1, DIN), archive, mean_coef.T, var_coef.T)
    held = call(
        load_kernel,
        tuple(pltpu.VMEM(array.shape, array.dtype) for array in arrays),
        arrays,
        flops=1,
        in_spaces=[pltpu.HBM] * 4,
        scratch=[pltpu.SemaphoreType.DMA((4,))],
    )
    sent = samples.reshape((1, PAIR, 1, part_rows, DIN))
    sent = jnp.broadcast_to(sent, slots + (part_rows, DIN))
    gathered = lax.all_to_all(sent.reshape(devices, part_rows, DIN), RANKS, split_axis=0, concat_axis=0, tiled=True)
    own = call(
        runs_kernel,
        pltpu.VMEM((DIN + 2 * width + NORM_ROWS, runs), jnp.bfloat16),
        held,
        flops=2 * BLOCK * runs * DIN,
    )
    peer = lax.ppermute(own, "grp", [(i, i ^ 1) for i in range(grp)])
    samp_z, samp_norm = call(
        samples_kernel,
        (pltpu.VMEM((rows, DIN), jnp.bfloat16), pltpu.VMEM((rows, LANES), jnp.float32)),
        (held[0], gathered.reshape(rows, DIN)),
        flops=NORMS_WEIGHT * rows * DIN,
    )
    sums = call(
        sums_kernel,
        pltpu.VMEM((rows, 2 * width), jnp.float32),
        (samp_z, samp_norm, own, peer),
        flops=4 * rows * runs * (DIN + 4 * width),
        transcendentals=2 * rows * runs,
    )
    sums = sums.reshape(devices, part_rows, 2 * width)
    parts = lax.all_to_all(sums, RANKS, split_axis=0, concat_axis=0, tiled=True)
    return tuple(call(
        outputs_kernel,
        (pltpu.HBM((own_rows, width), jnp.float32),) * 2,
        (parts.reshape(slots + (part_rows, 2 * width)),),
        flops=parts.size,
        scratch=[pltpu.VMEM((own_rows, width), jnp.float32)] * 2 + [pltpu.SemaphoreType.DMA((2,))],
    ))


def solution(mesh):
    rows = P(AXES, None)
    return jax.shard_map(
        on_device,
        mesh=mesh,
        in_specs=(rows, rows, P(), rows, rows),
        out_specs=(rows, rows),
        check_vma=False,
    )
```

```python
import jax
import jax.numpy as jnp
from jax import lax
from jax.experimental import pallas as pl
from jax.experimental.pallas import tpu as pltpu
from jax.sharding import PartitionSpec as P

DIN = 512
AXES = ("wide", "grp")
RANKS = ("grp", "wide")
PAIR = 2
BLOCK = 128
RUN_BLOCK = 256
NORM_ROWS = 16
LANES = 128
NORMS_WEIGHT = 400000
VMEM_LIMIT = 40 * 1024 * 1024


def scaled(rows, inv_len):
    factor = inv_len * DIN ** (-0.5)
    return (rows.astype(jnp.float32) * factor).astype(jnp.bfloat16)


def send_kernel(
    samples_hbm, inv_len_hbm, archive_hbm, mean_hbm, var_hbm,
    sent_hbm, inv_len_ref, archive_ref, mean_ref, var_ref, samples_ref, sent_ref, arrived,
):
    copies = [
        pltpu.make_async_copy(source, target, arrived.at[number])
        for number, (source, target) in enumerate((
            (samples_hbm, samples_ref),
            (inv_len_hbm, inv_len_ref),
            (archive_hbm, archive_ref),
            (mean_hbm, mean_ref),
            (var_hbm, var_ref),
            (sent_ref, sent_hbm),
        ))
    ]
    for copy in copies[:5]:
        copy.start()
    for copy in copies[:2]:
        copy.wait()
    samp_z = scaled(samples_ref[...], inv_len_ref[...])
    samp_z = samp_z.reshape((1, PAIR, 1) + sent_ref.shape[3:])
    sent_ref[...] = jnp.broadcast_to(samp_z, sent_ref.shape)
    copies[5].start()
    for copy in copies[2:]:
        copy.wait()


def runs_kernel(inv_len_ref, archive_ref, mean_ref, var_ref, pack_ref):
    runs = archive_ref.shape[0]
    width = mean_ref.shape[0]
    row = lax.broadcasted_iota(jnp.int32, (BLOCK, BLOCK), 0)
    column = lax.broadcasted_iota(jnp.int32, (BLOCK, BLOCK), 1)
    norms = []
    for first in range(0, runs, BLOCK):
        arch_z = scaled(archive_ref[first : first + BLOCK, :], inv_len_ref[...])
        turned = arch_z.T
        pack_ref[:DIN, first : first + BLOCK] = turned
        products = jnp.dot(arch_z, turned, preferred_element_type=jnp.float32)
        norms.append(jnp.sum(jnp.where(row == column, products, 0.0), axis=0, keepdims=True))
    coefs = jnp.concatenate([mean_ref[...], var_ref[...]], axis=0)
    for first in range(0, runs, 2 * width):
        block = slice(first, first + 2 * width)
        pack_ref[DIN : DIN + 2 * width, block] = coefs[:, block].T
    rest = jnp.broadcast_to(0.5 * jnp.concatenate(norms, axis=1), (NORM_ROWS, runs))
    part_row = lax.broadcasted_iota(jnp.int32, rest.shape, 0)
    parts = jnp.zeros(rest.shape, jnp.float32)
    for number in range(3):
        part = rest.astype(jnp.bfloat16).astype(jnp.float32)
        parts = jnp.where(part_row == number, part, parts)
        rest = rest - part
    pack_ref[DIN + 2 * width :, :] = parts.astype(jnp.bfloat16)


def norms_kernel(samp_z_ref, norm_ref):
    def block(rows):
        wide_copy = samp_z_ref[rows, :].astype(jnp.float32)
        norm = 0.5 * jnp.sum(wide_copy * wide_copy, axis=-1, keepdims=True)
        norm_ref[rows, :] = jnp.broadcast_to(norm, (norm.shape[0], LANES))

    by_blocks(block, samp_z_ref.shape[0])


def sums_kernel(samp_z_ref, samp_norm_ref, own_ref, peer_ref, sums_ref):
    width = sums_ref.shape[1] // 2

    def block(rows):
        samp_z = samp_z_ref[rows, :]
        samp_norm = samp_norm_ref[rows, :1]
        total = None
        for pack_ref in (own_ref, peer_ref):
            for first in range(0, pack_ref.shape[1], RUN_BLOCK):
                runs = slice(first, first + RUN_BLOCK)
                inner_prod = jnp.dot(samp_z, pack_ref[:DIN, runs], preferred_element_type=jnp.float32)
                norm_parts = pack_ref[DIN + 2 * width :, runs].astype(jnp.float32)
                arch_norm = jnp.sum(norm_parts, axis=0, keepdims=True)
                kernel = jnp.exp(inner_prod - samp_norm - arch_norm)
                both = jnp.concatenate([kernel, kernel * kernel], axis=0).astype(jnp.bfloat16)
                blocks = range(first, first + RUN_BLOCK, 2 * width)
                coefs = jnp.concatenate(
                    [pack_ref[DIN : DIN + 2 * width, start : start + 2 * width] for start in blocks],
                    axis=0,
                )
                part = jnp.dot(both, coefs, preferred_element_type=jnp.float32)
                total = part if total is None else total + part
        count = samp_z.shape[0]
        lane = lax.broadcasted_iota(jnp.int32, (count, 2 * width), 1)
        sums_ref[rows, :] = jnp.where(lane < width, total[:count], total[count:])

    by_blocks(block, samp_z_ref.shape[0])


def outputs_kernel(parts_ref, mean_hbm, var_hbm, mean_ref, var_ref, written):
    width = mean_ref.shape[1]
    summed = jnp.sum(parts_ref[...], axis=(0, 2))
    summed = summed.reshape(mean_ref.shape[0], 2 * width)
    mean_ref[...] = summed[:, :width]
    mean_copy = pltpu.make_async_copy(mean_ref, mean_hbm, written.at[0])
    mean_copy.start()
    var_ref[...] = 1.0 - summed[:, width:]
    var_copy = pltpu.make_async_copy(var_ref, var_hbm, written.at[1])
    var_copy.start()
    mean_copy.wait()
    var_copy.wait()


def by_blocks(block, count):
    if count <= BLOCK:
        block(slice(None))
    else:
        @pl.loop(0, count // BLOCK)
        def _(step):
            block(pl.ds(pl.multiple_of(step * BLOCK, BLOCK), BLOCK))


def call(kernel, out_shape, inputs, flops, transcendentals=0, in_space=pltpu.VMEM, scratch=()):
    moved = sum(array.size * array.dtype.itemsize for array in inputs)
    return pl.pallas_call(
        kernel,
        out_shape=out_shape,
        in_specs=[pl.BlockSpec(memory_space=in_space)] * len(inputs),
        out_specs=jax.tree.map(lambda out: pl.BlockSpec(memory_space=out.memory_space), out_shape),
        scratch_shapes=scratch,
        cost_estimate=pl.CostEstimate(
            flops=flops, bytes_accessed=moved, transcendentals=transcendentals
        ),
        compiler_params=pltpu.CompilerParams(vmem_limit_bytes=VMEM_LIMIT),
    )(*inputs)


def on_device(samples, archive, inv_len, mean_coef, var_coef):
    devices = lax.axis_size(AXES)
    grp = lax.axis_size("grp")
    own_rows = samples.shape[0]
    part_rows = own_rows // PAIR
    rows = devices * part_rows
    slots = (grp // PAIR, PAIR, lax.axis_size("wide"))
    runs, width = mean_coef.shape

    arrays = (samples, inv_len.reshape(1, DIN), archive, mean_coef.T, var_coef.T)
    sent, *held = call(
        send_kernel,
        (pltpu.HBM(slots + (part_rows, DIN), jnp.bfloat16),)
        + tuple(pltpu.VMEM(array.shape, array.dtype) for array in arrays[1:]),
        [pltpu.with_memory_space_constraint(array, pltpu.HBM) for array in arrays],
        flops=own_rows * DIN,
        in_space=pltpu.HBM,
        scratch=[
            pltpu.VMEM(samples.shape, samples.dtype),
            pltpu.VMEM(slots + (part_rows, DIN), jnp.bfloat16),
            pltpu.SemaphoreType.DMA((6,)),
        ],
    )
    gathered = lax.all_to_all(sent.reshape(devices, part_rows, DIN), RANKS, split_axis=0, concat_axis=0, tiled=True)
    own = call(
        runs_kernel,
        pltpu.VMEM((DIN + 2 * width + NORM_ROWS, runs), jnp.bfloat16),
        held,
        flops=2 * BLOCK * runs * DIN,
    )
    peer = lax.ppermute(own, "grp", [(i, i ^ 1) for i in range(grp)])
    samp_z = gathered.reshape(rows, DIN)
    samp_norm = call(
        norms_kernel,
        pltpu.VMEM((rows, LANES), jnp.float32),
        (samp_z,),
        flops=NORMS_WEIGHT * rows * DIN,
    )
    sums = call(
        sums_kernel,
        pltpu.VMEM((rows, 2 * width), jnp.float32),
        (samp_z, samp_norm, own, peer),
        flops=4 * rows * runs * (DIN + 4 * width),
        transcendentals=2 * rows * runs,
    )
    sums = sums.reshape(devices, part_rows, 2 * width)
    parts = lax.all_to_all(sums, RANKS, split_axis=0, concat_axis=0, tiled=True)
    return tuple(call(
        outputs_kernel,
        (pltpu.HBM((own_rows, width), jnp.float32),) * 2,
        (parts.reshape(slots + (part_rows, 2 * width)),),
        flops=parts.size,
        scratch=[pltpu.VMEM((own_rows, width), jnp.float32)] * 2 + [pltpu.SemaphoreType.DMA((2,))],
    ))


def solution(mesh):
    rows = P(AXES, None)
    return jax.shard_map(
        on_device,
        mesh=mesh,
        in_specs=(rows, rows, P(), rows, rows),
        out_specs=(rows, rows),
        check_vma=False,
    )
```

```python
import jax
import jax.numpy as jnp
from jax import lax
from jax.experimental import pallas as pl
from jax.experimental.pallas import tpu as pltpu
from jax.sharding import PartitionSpec as P

DIN = 512
AXES = ("wide", "grp")
RANKS = ("grp", "wide")
PAIR = 2
BLOCK = 128
NORM_ROWS = 16
LANES = 128
NORMS_WEIGHT = 400000
VMEM_LIMIT = 40 * 1024 * 1024


def scaled(rows, inv_len):
    factor = inv_len * DIN ** (-0.5)
    return (rows.astype(jnp.float32) * factor).astype(jnp.bfloat16)


def send_kernel(
    samples_hbm, inv_len_hbm, archive_hbm, mean_hbm, var_hbm,
    sent_hbm, inv_len_ref, archive_ref, mean_ref, var_ref, samples_ref, sent_ref, arrived,
):
    copies = [
        pltpu.make_async_copy(source, target, arrived.at[number])
        for number, (source, target) in enumerate((
            (samples_hbm, samples_ref),
            (inv_len_hbm, inv_len_ref),
            (archive_hbm, archive_ref),
            (mean_hbm, mean_ref),
            (var_hbm, var_ref),
            (sent_ref, sent_hbm),
        ))
    ]
    for copy in copies[:5]:
        copy.start()
    for copy in copies[:2]:
        copy.wait()
    samp_z = scaled(samples_ref[...], inv_len_ref[...])
    samp_z = samp_z.reshape((1, PAIR, 1) + sent_ref.shape[3:])
    sent_ref[...] = jnp.broadcast_to(samp_z, sent_ref.shape)
    copies[5].start()
    for copy in copies[2:]:
        copy.wait()


def runs_kernel(inv_len_ref, archive_ref, mean_ref, var_ref, pack_ref):
    runs = archive_ref.shape[0]
    width = mean_ref.shape[0]
    row = lax.broadcasted_iota(jnp.int32, (BLOCK, BLOCK), 0)
    column = lax.broadcasted_iota(jnp.int32, (BLOCK, BLOCK), 1)
    norms = []
    for first in range(0, runs, BLOCK):
        arch_z = scaled(archive_ref[first : first + BLOCK, :], inv_len_ref[...])
        turned = arch_z.T
        pack_ref[:DIN, first : first + BLOCK] = turned
        products = jnp.dot(arch_z, turned, preferred_element_type=jnp.float32)
        norms.append(jnp.sum(jnp.where(row == column, products, 0.0), axis=0, keepdims=True))
    coefs = jnp.concatenate([mean_ref[...], var_ref[...]], axis=0)
    for first in range(0, runs, 2 * width):
        block = slice(first, first + 2 * width)
        pack_ref[DIN : DIN + 2 * width, block] = coefs[:, block].T
    rest = jnp.broadcast_to(0.5 * jnp.concatenate(norms, axis=1), (NORM_ROWS, runs))
    part_row = lax.broadcasted_iota(jnp.int32, rest.shape, 0)
    parts = jnp.zeros(rest.shape, jnp.float32)
    for number in range(3):
        part = rest.astype(jnp.bfloat16).astype(jnp.float32)
        parts = jnp.where(part_row == number, part, parts)
        rest = rest - part
    pack_ref[DIN + 2 * width :, :] = parts.astype(jnp.bfloat16)


def norms_kernel(samp_z_ref, norm_ref):
    def block(rows):
        wide_copy = samp_z_ref[rows, :].astype(jnp.float32)
        norm = 0.5 * jnp.sum(wide_copy * wide_copy, axis=-1, keepdims=True)
        norm_ref[rows, :] = jnp.broadcast_to(norm, (norm.shape[0], LANES))

    by_blocks(block, samp_z_ref.shape[0])


def sums_kernel(samp_z_ref, samp_norm_ref, own_ref, peer_ref, sums_ref):
    width = sums_ref.shape[1] // 2
    packs = (own_ref, peer_ref)

    def block(rows):
        samp_z = samp_z_ref[rows, :]
        samp_norm = samp_norm_ref[rows, :1]
        arch_z = jnp.concatenate([pack_ref[:DIN, :] for pack_ref in packs], axis=1)
        inner_prod = jnp.dot(samp_z, arch_z, preferred_element_type=jnp.float32)
        norm_parts = jnp.concatenate([pack_ref[DIN + 2 * width :, :] for pack_ref in packs], axis=1)
        arch_norm = jnp.sum(norm_parts.astype(jnp.float32), axis=0, keepdims=True)
        kernel = jnp.exp(inner_prod - samp_norm - arch_norm)
        both = jnp.concatenate([kernel, kernel * kernel], axis=0).astype(jnp.bfloat16)
        coefs = jnp.concatenate(
            [
                pack_ref[DIN : DIN + 2 * width, first : first + 2 * width]
                for pack_ref in packs
                for first in range(0, pack_ref.shape[1], 2 * width)
            ],
            axis=0,
        )
        total = jnp.dot(both, coefs, preferred_element_type=jnp.float32)
        count = samp_z.shape[0]
        lane = lax.broadcasted_iota(jnp.int32, (count, 2 * width), 1)
        sums_ref[rows, :] = jnp.where(lane < width, total[:count], total[count:])

    by_blocks(block, samp_z_ref.shape[0])


def outputs_kernel(parts_ref, mean_hbm, var_hbm, mean_ref, var_ref, written):
    width = mean_ref.shape[1]
    summed = jnp.sum(parts_ref[...], axis=(0, 2))
    summed = summed.reshape(mean_ref.shape[0], 2 * width)
    mean_ref[...] = summed[:, :width]
    mean_copy = pltpu.make_async_copy(mean_ref, mean_hbm, written.at[0])
    mean_copy.start()
    var_ref[...] = 1.0 - summed[:, width:]
    var_copy = pltpu.make_async_copy(var_ref, var_hbm, written.at[1])
    var_copy.start()
    mean_copy.wait()
    var_copy.wait()


def by_blocks(block, count):
    if count <= BLOCK:
        block(slice(None))
    else:
        @pl.loop(0, count // BLOCK)
        def _(step):
            block(pl.ds(pl.multiple_of(step * BLOCK, BLOCK), BLOCK))


def call(kernel, out_shape, inputs, flops, transcendentals=0, in_space=pltpu.VMEM, scratch=()):
    moved = sum(array.size * array.dtype.itemsize for array in inputs)
    return pl.pallas_call(
        kernel,
        out_shape=out_shape,
        in_specs=[pl.BlockSpec(memory_space=in_space)] * len(inputs),
        out_specs=jax.tree.map(lambda out: pl.BlockSpec(memory_space=out.memory_space), out_shape),
        scratch_shapes=scratch,
        cost_estimate=pl.CostEstimate(
            flops=flops, bytes_accessed=moved, transcendentals=transcendentals
        ),
        compiler_params=pltpu.CompilerParams(vmem_limit_bytes=VMEM_LIMIT),
    )(*inputs)


def on_device(samples, archive, inv_len, mean_coef, var_coef):
    devices = lax.axis_size(AXES)
    grp = lax.axis_size("grp")
    own_rows = samples.shape[0]
    part_rows = own_rows // PAIR
    rows = devices * part_rows
    slots = (grp // PAIR, PAIR, lax.axis_size("wide"))
    runs, width = mean_coef.shape

    arrays = (samples, inv_len.reshape(1, DIN), archive, mean_coef.T, var_coef.T)
    sent, *held = call(
        send_kernel,
        (pltpu.HBM(slots + (part_rows, DIN), jnp.bfloat16),)
        + tuple(pltpu.VMEM(array.shape, array.dtype) for array in arrays[1:]),
        [pltpu.with_memory_space_constraint(array, pltpu.HBM) for array in arrays],
        flops=own_rows * DIN,
        in_space=pltpu.HBM,
        scratch=[
            pltpu.VMEM(samples.shape, samples.dtype),
            pltpu.VMEM(slots + (part_rows, DIN), jnp.bfloat16),
            pltpu.SemaphoreType.DMA((6,)),
        ],
    )
    gathered = lax.all_to_all(sent.reshape(devices, part_rows, DIN), RANKS, split_axis=0, concat_axis=0, tiled=True)
    own = call(
        runs_kernel,
        pltpu.VMEM((DIN + 2 * width + NORM_ROWS, runs), jnp.bfloat16),
        held,
        flops=2 * BLOCK * runs * DIN,
    )
    peer = lax.ppermute(own, "grp", [(i, i ^ 1) for i in range(grp)])
    samp_z = gathered.reshape(rows, DIN)
    samp_norm = call(
        norms_kernel,
        pltpu.VMEM((rows, LANES), jnp.float32),
        (samp_z,),
        flops=NORMS_WEIGHT * rows * DIN,
    )
    sums = call(
        sums_kernel,
        pltpu.VMEM((rows, 2 * width), jnp.float32),
        (samp_z, samp_norm, own, peer),
        flops=4 * rows * runs * (DIN + 4 * width),
        transcendentals=2 * rows * runs,
    )
    sums = sums.reshape(devices, part_rows, 2 * width)
    parts = lax.all_to_all(sums, RANKS, split_axis=0, concat_axis=0, tiled=True)
    return tuple(call(
        outputs_kernel,
        (pltpu.HBM((own_rows, width), jnp.float32),) * 2,
        (parts.reshape(slots + (part_rows, 2 * width)),),
        flops=parts.size,
        scratch=[pltpu.VMEM((own_rows, width), jnp.float32)] * 2 + [pltpu.SemaphoreType.DMA((2,))],
    ))


def solution(mesh):
    rows = P(AXES, None)
    return jax.shard_map(
        on_device,
        mesh=mesh,
        in_specs=(rows, rows, P(), rows, rows),
        out_specs=(rows, rows),
        check_vma=False,
    )
```

```python
import jax
import jax.numpy as jnp
from jax import lax
from jax.experimental import pallas as pl
from jax.experimental.pallas import tpu as pltpu
from jax.sharding import PartitionSpec as P

DIN = 512
AXES = ("wide", "grp")
RANKS = ("grp", "wide")
PAIR = 2
BLOCK = 128
GRAM = 256
NORM_ROWS = 16
VMEM_LIMIT = 40 * 1024 * 1024


def scaled(rows, inv_len):
    factor = inv_len * DIN ** (-0.5)
    return (rows.astype(jnp.float32) * factor).astype(jnp.bfloat16)


def send_kernel(
    samples_hbm, inv_len_hbm, archive_hbm, mean_hbm, var_hbm,
    sent_ref, inv_len_ref, archive_ref, mean_ref, var_ref, samples_ref, arrived,
):
    copies = [
        pltpu.make_async_copy(source, target, arrived.at[number])
        for number, (source, target) in enumerate((
            (samples_hbm, samples_ref),
            (inv_len_hbm, inv_len_ref),
            (archive_hbm, archive_ref),
            (mean_hbm, mean_ref),
            (var_hbm, var_ref),
        ))
    ]
    for copy in copies:
        copy.start()
    for copy in copies[:2]:
        copy.wait()
    samp_z = scaled(samples_ref[...], inv_len_ref[...])
    samp_z = samp_z.reshape((1, PAIR, 1) + sent_ref.shape[3:])
    sent_ref[...] = jnp.broadcast_to(samp_z, sent_ref.shape)
    for copy in copies[2:]:
        copy.wait()


def runs_kernel(inv_len_ref, archive_ref, mean_ref, var_ref, pack_ref):
    runs = archive_ref.shape[0]
    width = mean_ref.shape[0]
    row = lax.broadcasted_iota(jnp.int32, (GRAM, GRAM), 0)
    column = lax.broadcasted_iota(jnp.int32, (GRAM, GRAM), 1)
    arch_z = scaled(archive_ref[...], inv_len_ref[...])
    turned = arch_z.T
    pack_ref[:DIN, :] = turned
    products = [
        jnp.dot(
            arch_z[first : first + GRAM], turned[:, first : first + GRAM],
            preferred_element_type=jnp.float32,
        )
        for first in range(0, runs, GRAM)
    ]
    norms = [
        jnp.sum(jnp.where(row == column, product, 0.0), axis=0, keepdims=True)
        for product in products
    ]
    coefs = jnp.concatenate([mean_ref[...], var_ref[...]], axis=0)
    for first in range(0, runs, 2 * width):
        block = slice(first, first + 2 * width)
        pack_ref[DIN : DIN + 2 * width, block] = coefs[:, block].T
    rest = jnp.broadcast_to(0.5 * jnp.concatenate(norms, axis=1), (NORM_ROWS, runs))
    part_row = lax.broadcasted_iota(jnp.int32, rest.shape, 0)
    parts = jnp.zeros(rest.shape, jnp.float32)
    for number in range(3):
        part = rest.astype(jnp.bfloat16).astype(jnp.float32)
        parts = jnp.where(part_row == number, part, parts)
        rest = rest - part
    pack_ref[DIN + 2 * width :, :] = parts.astype(jnp.bfloat16)


def sums_kernel(samp_z_ref, own_ref, peer_ref, sums_ref):
    width = sums_ref.shape[1] // 2
    packs = (own_ref, peer_ref)

    def block(rows):
        samp_z = samp_z_ref[rows, :]
        wide_copy = samp_z.astype(jnp.float32)
        samp_norm = 0.5 * jnp.sum(wide_copy * wide_copy, axis=-1, keepdims=True)
        arch_z = jnp.concatenate([pack_ref[:DIN, :] for pack_ref in packs], axis=1)
        inner_prod = jnp.dot(samp_z, arch_z, preferred_element_type=jnp.float32)
        norm_parts = jnp.concatenate([pack_ref[DIN + 2 * width :, :] for pack_ref in packs], axis=1)
        arch_norm = jnp.sum(norm_parts.astype(jnp.float32), axis=0, keepdims=True)
        kernel = jnp.exp(inner_prod - samp_norm - arch_norm)
        both = jnp.concatenate([kernel, kernel * kernel], axis=0).astype(jnp.bfloat16)
        coefs = jnp.concatenate(
            [
                pack_ref[DIN : DIN + 2 * width, first : first + 2 * width]
                for pack_ref in packs
                for first in range(0, pack_ref.shape[1], 2 * width)
            ],
            axis=0,
        )
        total = jnp.dot(both, coefs, preferred_element_type=jnp.float32)
        count = samp_z.shape[0]
        lane = lax.broadcasted_iota(jnp.int32, (count, 2 * width), 1)
        sums_ref[rows, :] = jnp.where(lane < width, total[:count], total[count:])

    by_blocks(block, samp_z_ref.shape[0])


def outputs_kernel(parts_ref, mean_hbm, var_hbm, mean_ref, var_ref, written):
    width = mean_ref.shape[1]
    summed = jnp.sum(parts_ref[...], axis=(0, 2))
    summed = summed.reshape(mean_ref.shape[0], 2 * width)
    mean_ref[...] = summed[:, :width]
    mean_copy = pltpu.make_async_copy(mean_ref, mean_hbm, written.at[0])
    mean_copy.start()
    var_ref[...] = 1.0 - summed[:, width:]
    var_copy = pltpu.make_async_copy(var_ref, var_hbm, written.at[1])
    var_copy.start()
    mean_copy.wait()
    var_copy.wait()


def by_blocks(block, count):
    if count <= BLOCK:
        block(slice(None))
    else:
        @pl.loop(0, count // BLOCK)
        def _(step):
            block(pl.ds(pl.multiple_of(step * BLOCK, BLOCK), BLOCK))


def call(kernel, out_shape, inputs, flops, transcendentals=0, in_space=pltpu.VMEM, scratch=()):
    moved = sum(array.size * array.dtype.itemsize for array in inputs)
    return pl.pallas_call(
        kernel,
        out_shape=out_shape,
        in_specs=[pl.BlockSpec(memory_space=in_space)] * len(inputs),
        out_specs=jax.tree.map(lambda out: pl.BlockSpec(memory_space=out.memory_space), out_shape),
        scratch_shapes=scratch,
        cost_estimate=pl.CostEstimate(
            flops=flops, bytes_accessed=moved, transcendentals=transcendentals
        ),
        compiler_params=pltpu.CompilerParams(vmem_limit_bytes=VMEM_LIMIT),
    )(*inputs)


def on_device(samples, archive, inv_len, mean_coef, var_coef):
    devices = lax.axis_size(AXES)
    grp = lax.axis_size("grp")
    own_rows = samples.shape[0]
    part_rows = own_rows // PAIR
    rows = devices * part_rows
    slots = (grp // PAIR, PAIR, lax.axis_size("wide"))
    runs, width = mean_coef.shape

    arrays = (samples, inv_len.reshape(1, DIN), archive, mean_coef.T, var_coef.T)
    sent, *held = call(
        send_kernel,
        (pltpu.VMEM(slots + (part_rows, DIN), jnp.bfloat16),)
        + tuple(pltpu.VMEM(array.shape, array.dtype) for array in arrays[1:]),
        [pltpu.with_memory_space_constraint(array, pltpu.HBM) for array in arrays],
        flops=own_rows * DIN,
        in_space=pltpu.HBM,
        scratch=[pltpu.VMEM(samples.shape, samples.dtype), pltpu.SemaphoreType.DMA((5,))],
    )
    gathered = lax.all_to_all(sent.reshape(devices, part_rows, DIN), RANKS, split_axis=0, concat_axis=0, tiled=True)
    own = call(
        runs_kernel,
        pltpu.VMEM((DIN + 2 * width + NORM_ROWS, runs), jnp.bfloat16),
        held,
        flops=2 * BLOCK * runs * DIN,
    )
    peer = lax.ppermute(own, "grp", [(i, i ^ 1) for i in range(grp)])
    sums = call(
        sums_kernel,
        pltpu.VMEM((rows, 2 * width), jnp.float32),
        (gathered.reshape(rows, DIN), own, peer),
        flops=4 * rows * runs * (DIN + 4 * width),
        transcendentals=2 * rows * runs,
    )
    sums = sums.reshape(devices, part_rows, 2 * width)
    parts = lax.all_to_all(sums, RANKS, split_axis=0, concat_axis=0, tiled=True)
    return tuple(call(
        outputs_kernel,
        (pltpu.HBM((own_rows, width), jnp.float32),) * 2,
        (parts.reshape(slots + (part_rows, 2 * width)),),
        flops=parts.size,
        scratch=[pltpu.VMEM((own_rows, width), jnp.float32)] * 2 + [pltpu.SemaphoreType.DMA((2,))],
    ))


def solution(mesh):
    rows = P(AXES, None)
    return jax.shard_map(
        on_device,
        mesh=mesh,
        in_specs=(rows, rows, P(), rows, rows),
        out_specs=(rows, rows),
        check_vma=False,
    )
```

```python
import jax
import jax.numpy as jnp
from jax import lax
from jax.experimental import pallas as pl
from jax.experimental.pallas import tpu as pltpu
from jax.sharding import PartitionSpec as P

DIN = 512
AXES = ("wide", "grp")
RANKS = ("grp", "wide")
PAIR = 2
BLOCK = 128
GRAM = 256
NORM_ROWS = 16
VMEM_LIMIT = 40 * 1024 * 1024


def scaled(rows, inv_len):
    factor = inv_len * DIN ** (-0.5)
    return (rows.astype(jnp.float32) * factor).astype(jnp.bfloat16)


def load_kernel(*refs):
    count = len(refs) // 2
    sources, targets, arrived = refs[:count], refs[count:-1], refs[-1]
    copies = [
        pltpu.make_async_copy(source, target, arrived.at[number])
        for number, (source, target) in enumerate(zip(sources, targets))
    ]
    for copy in copies:
        copy.start()
    for copy in copies:
        copy.wait()


def runs_kernel(inv_len_ref, archive_ref, mean_ref, var_ref, pack_ref):
    runs = archive_ref.shape[0]
    width = mean_ref.shape[0]
    row = lax.broadcasted_iota(jnp.int32, (GRAM, GRAM), 0)
    column = lax.broadcasted_iota(jnp.int32, (GRAM, GRAM), 1)
    arch_z = scaled(archive_ref[...], inv_len_ref[...])
    turned = arch_z.T
    pack_ref[:DIN, :] = turned
    products = [
        jnp.dot(
            arch_z[first : first + GRAM], turned[:, first : first + GRAM],
            preferred_element_type=jnp.float32,
        )
        for first in range(0, runs, GRAM)
    ]
    norms = [
        jnp.sum(jnp.where(row == column, product, 0.0), axis=0, keepdims=True)
        for product in products
    ]
    coefs = jnp.concatenate([mean_ref[...], var_ref[...]], axis=0)
    for first in range(0, runs, 2 * width):
        block = slice(first, first + 2 * width)
        pack_ref[DIN : DIN + 2 * width, block] = coefs[:, block].T
    rest = jnp.broadcast_to(0.5 * jnp.concatenate(norms, axis=1), (NORM_ROWS, runs))
    part_row = lax.broadcasted_iota(jnp.int32, rest.shape, 0)
    parts = jnp.zeros(rest.shape, jnp.float32)
    for number in range(3):
        part = rest.astype(jnp.bfloat16).astype(jnp.float32)
        parts = jnp.where(part_row == number, part, parts)
        rest = rest - part
    pack_ref[DIN + 2 * width :, :] = parts.astype(jnp.bfloat16)


def sums_kernel(inv_len_ref, samples_ref, own_ref, peer_ref, sums_ref):
    width = sums_ref.shape[-1] // 2
    packs = (own_ref, peer_ref)
    pairs, _, chips, own_rows, _ = sums_ref.shape

    def block(pair, chip, count):
        samp_z = samples_ref[pair, pl.ds(chip, count)].reshape(count * own_rows, DIN)
        samp_z = scaled(samp_z, inv_len_ref[...])
        wide_copy = samp_z.astype(jnp.float32)
        samp_norm = 0.5 * jnp.sum(wide_copy * wide_copy, axis=-1, keepdims=True)
        arch_z = jnp.concatenate([pack_ref[:DIN, :] for pack_ref in packs], axis=1)
        inner_prod = jnp.dot(samp_z, arch_z, preferred_element_type=jnp.float32)
        norm_parts = jnp.concatenate([pack_ref[DIN + 2 * width :, :] for pack_ref in packs], axis=1)
        arch_norm = jnp.sum(norm_parts.astype(jnp.float32), axis=0, keepdims=True)
        kernel = jnp.exp(inner_prod - samp_norm - arch_norm)
        both = jnp.concatenate([kernel, kernel * kernel], axis=0).astype(jnp.bfloat16)
        coefs = jnp.concatenate(
            [
                pack_ref[DIN : DIN + 2 * width, first : first + 2 * width]
                for pack_ref in packs
                for first in range(0, pack_ref.shape[1], 2 * width)
            ],
            axis=0,
        )
        total = jnp.dot(both, coefs, preferred_element_type=jnp.float32)
        half = samp_z.shape[0]
        lane = lax.broadcasted_iota(jnp.int32, (half, 2 * width), 1)
        sums = jnp.where(lane < width, total[:half], total[half:])
        sums = sums.reshape(count, own_rows, 2 * width)
        for core in range(PAIR):
            sums_ref[pair, core, pl.ds(chip, count)] = sums

    step = min(chips, BLOCK // own_rows)
    if pairs == 1 and step == chips:
        block(0, 0, chips)
    else:
        @pl.loop(0, pairs * (chips // step))
        def _(number):
            block(number // (chips // step), number % (chips // step) * step, step)


def outputs_kernel(parts_ref, mean_hbm, var_hbm, mean_ref, var_ref, written):
    width = mean_ref.shape[1]
    core = lax.rem(lax.axis_index("grp"), PAIR)
    summed = jnp.sum(parts_ref[:, pl.ds(core, 1)], axis=(0, 1, 2))
    mean_ref[...] = summed[:, :width]
    mean_copy = pltpu.make_async_copy(mean_ref, mean_hbm, written.at[0])
    mean_copy.start()
    var_ref[...] = 1.0 - summed[:, width:]
    var_copy = pltpu.make_async_copy(var_ref, var_hbm, written.at[1])
    var_copy.start()
    mean_copy.wait()
    var_copy.wait()


def digits(size):
    found, stride = [], 1
    while stride < size:
        radix = 4 if size // stride % 4 == 0 else size // stride
        found.append((stride, radix))
        stride *= radix
    return found


def gather(array, axis, start, size):
    whole = start * size
    for stride, radix in digits(size):
        stride *= start
        groups = [
            [first + stride * k for k in range(radix)]
            for first in range(whole)
            if first // stride % radix == 0
        ]
        array = lax.all_gather(array, axis, axis_index_groups=groups, axis=0, tiled=True)
    return array


def call(kernel, out_shape, inputs, flops, transcendentals=0, in_space=pltpu.VMEM, scratch=()):
    moved = sum(array.size * array.dtype.itemsize for array in inputs)
    return pl.pallas_call(
        kernel,
        out_shape=out_shape,
        in_specs=[pl.BlockSpec(memory_space=in_space)] * len(inputs),
        out_specs=jax.tree.map(lambda out: pl.BlockSpec(memory_space=out.memory_space), out_shape),
        scratch_shapes=scratch,
        cost_estimate=pl.CostEstimate(
            flops=flops, bytes_accessed=moved, transcendentals=transcendentals
        ),
        compiler_params=pltpu.CompilerParams(vmem_limit_bytes=VMEM_LIMIT),
    )(*inputs)


def on_device(samples, archive, inv_len, mean_coef, var_coef):
    devices = lax.axis_size(RANKS)
    wide = lax.axis_size("wide")
    grp = lax.axis_size("grp")
    own_rows = samples.shape[0]
    runs, width = mean_coef.shape
    rows = devices // PAIR * own_rows

    gathered = gather(samples[None], "wide", 1, wide)
    gathered = gather(gathered, "grp", PAIR, grp // PAIR)
    arrays = (inv_len.reshape(1, DIN), archive, mean_coef.T, var_coef.T)
    held = call(
        load_kernel,
        tuple(pltpu.VMEM(array.shape, array.dtype) for array in arrays),
        [pltpu.with_memory_space_constraint(array, pltpu.HBM) for array in arrays],
        flops=1,
        in_space=pltpu.HBM,
        scratch=[pltpu.SemaphoreType.DMA((4,))],
    )
    own = call(
        runs_kernel,
        pltpu.VMEM((DIN + 2 * width + NORM_ROWS, runs), jnp.bfloat16),
        held,
        flops=2 * BLOCK * runs * DIN,
    )
    peer = lax.ppermute(own, "grp", [(i, i ^ 1) for i in range(grp)])
    sums = call(
        sums_kernel,
        pltpu.VMEM((grp // PAIR, PAIR, wide, own_rows, 2 * width), jnp.float32),
        (held[0], gathered.reshape(grp // PAIR, wide, own_rows, DIN), own, peer),
        flops=4 * rows * runs * (DIN + 2 * width),
        transcendentals=2 * rows * runs,
    )
    sums = sums.reshape(devices, own_rows, 2 * width)
    parts = lax.all_to_all(sums, RANKS, split_axis=0, concat_axis=0, tiled=True)
    return tuple(call(
        outputs_kernel,
        (pltpu.HBM((own_rows, width), jnp.float32),) * 2,
        (parts.reshape(grp // PAIR, PAIR, wide, own_rows, 2 * width),),
        flops=parts.size,
        scratch=[pltpu.VMEM((own_rows, width), jnp.float32)] * 2 + [pltpu.SemaphoreType.DMA((2,))],
    ))


def solution(mesh):
    rows = P(AXES, None)
    return jax.shard_map(
        on_device,
        mesh=mesh,
        in_specs=(rows, rows, P(), rows, rows),
        out_specs=(rows, rows),
        check_vma=False,
    )
```

```python
import jax
import jax.numpy as jnp
from jax import lax
from jax.experimental import pallas as pl
from jax.experimental.pallas import tpu as pltpu
from jax.sharding import PartitionSpec as P

DIN = 512
AXES = ("wide", "grp")
RANKS = ("grp", "wide")
PAIR = 2
BLOCK = 128
NORM_ROWS = 16
VMEM_LIMIT = 40 * 1024 * 1024


def scaled(rows, inv_len):
    factor = inv_len * DIN ** (-0.5)
    return (rows.astype(jnp.float32) * factor).astype(jnp.bfloat16)


def send_kernel(
    samples_hbm, inv_len_hbm, archive_hbm, mean_hbm, var_hbm,
    sent_ref, inv_len_ref, archive_ref, mean_ref, var_ref, samples_ref, arrived,
):
    copies = [
        pltpu.make_async_copy(source, target, arrived.at[number])
        for number, (source, target) in enumerate((
            (samples_hbm, samples_ref),
            (inv_len_hbm, inv_len_ref),
            (archive_hbm, archive_ref),
            (mean_hbm, mean_ref),
            (var_hbm, var_ref),
        ))
    ]
    for copy in copies:
        copy.start()
    for copy in copies[:2]:
        copy.wait()
    samp_z = scaled(samples_ref[...], inv_len_ref[...])
    samp_z = samp_z.reshape((1, PAIR, 1) + sent_ref.shape[3:])
    sent_ref[...] = jnp.broadcast_to(samp_z, sent_ref.shape)
    for copy in copies[2:]:
        copy.wait()


def runs_kernel(inv_len_ref, archive_ref, mean_ref, var_ref, pack_ref):
    runs = archive_ref.shape[0]
    width = mean_ref.shape[0]
    row = lax.broadcasted_iota(jnp.int32, (BLOCK, BLOCK), 0)
    column = lax.broadcasted_iota(jnp.int32, (BLOCK, BLOCK), 1)
    norms = []
    for first in range(0, runs, BLOCK):
        arch_z = scaled(archive_ref[first : first + BLOCK, :], inv_len_ref[...])
        turned = arch_z.T
        pack_ref[:DIN, first : first + BLOCK] = turned
        products = jnp.dot(arch_z, turned, preferred_element_type=jnp.float32)
        norms.append(jnp.sum(jnp.where(row == column, products, 0.0), axis=0, keepdims=True))
    coefs = jnp.concatenate([mean_ref[...], var_ref[...]], axis=0)
    for first in range(0, runs, 2 * width):
        block = slice(first, first + 2 * width)
        pack_ref[DIN : DIN + 2 * width, block] = coefs[:, block].T
    rest = jnp.broadcast_to(0.5 * jnp.concatenate(norms, axis=1), (NORM_ROWS, runs))
    part_row = lax.broadcasted_iota(jnp.int32, rest.shape, 0)
    parts = jnp.zeros(rest.shape, jnp.float32)
    for number in range(3):
        part = rest.astype(jnp.bfloat16).astype(jnp.float32)
        parts = jnp.where(part_row == number, part, parts)
        rest = rest - part
    pack_ref[DIN + 2 * width :, :] = parts.astype(jnp.bfloat16)


def sums_kernel(samp_z_ref, own_ref, peer_ref, sums_ref):
    width = sums_ref.shape[1] // 2
    packs = (own_ref, peer_ref)

    def block(rows):
        samp_z = samp_z_ref[rows, :]
        wide_copy = samp_z.astype(jnp.float32)
        samp_norm = 0.5 * jnp.sum(wide_copy * wide_copy, axis=-1, keepdims=True)
        arch_z = jnp.concatenate([pack_ref[:DIN, :] for pack_ref in packs], axis=1)
        inner_prod = jnp.dot(samp_z, arch_z, preferred_element_type=jnp.float32)
        norm_parts = jnp.concatenate([pack_ref[DIN + 2 * width :, :] for pack_ref in packs], axis=1)
        arch_norm = jnp.sum(norm_parts.astype(jnp.float32), axis=0, keepdims=True)
        kernel = jnp.exp(inner_prod - samp_norm - arch_norm)
        both = jnp.concatenate([kernel, kernel * kernel], axis=0).astype(jnp.bfloat16)
        coefs = jnp.concatenate(
            [
                pack_ref[DIN : DIN + 2 * width, first : first + 2 * width]
                for pack_ref in packs
                for first in range(0, pack_ref.shape[1], 2 * width)
            ],
            axis=0,
        )
        total = jnp.dot(both, coefs, preferred_element_type=jnp.float32)
        count = samp_z.shape[0]
        lane = lax.broadcasted_iota(jnp.int32, (count, 2 * width), 1)
        sums_ref[rows, :] = jnp.where(lane < width, total[:count], total[count:])

    by_blocks(block, samp_z_ref.shape[0])


def outputs_kernel(parts_ref, mean_hbm, var_hbm, mean_ref, var_ref, written):
    width = mean_ref.shape[1]
    summed = jnp.sum(parts_ref[...], axis=(0, 2))
    summed = summed.reshape(mean_ref.shape[0], 2 * width)
    mean_ref[...] = summed[:, :width]
    mean_copy = pltpu.make_async_copy(mean_ref, mean_hbm, written.at[0])
    mean_copy.start()
    var_ref[...] = 1.0 - summed[:, width:]
    var_copy = pltpu.make_async_copy(var_ref, var_hbm, written.at[1])
    var_copy.start()
    mean_copy.wait()
    var_copy.wait()


def by_blocks(block, count):
    if count <= BLOCK:
        block(slice(None))
    else:
        @pl.loop(0, count // BLOCK)
        def _(step):
            block(pl.ds(pl.multiple_of(step * BLOCK, BLOCK), BLOCK))


def call(kernel, out_shape, inputs, flops, transcendentals=0, in_space=pltpu.VMEM, scratch=()):
    moved = sum(array.size * array.dtype.itemsize for array in inputs)
    return pl.pallas_call(
        kernel,
        out_shape=out_shape,
        in_specs=[pl.BlockSpec(memory_space=in_space)] * len(inputs),
        out_specs=jax.tree.map(lambda out: pl.BlockSpec(memory_space=out.memory_space), out_shape),
        scratch_shapes=scratch,
        cost_estimate=pl.CostEstimate(
            flops=flops, bytes_accessed=moved, transcendentals=transcendentals
        ),
        compiler_params=pltpu.CompilerParams(vmem_limit_bytes=VMEM_LIMIT),
    )(*inputs)


def on_device(samples, archive, inv_len, mean_coef, var_coef):
    devices = lax.axis_size(AXES)
    grp = lax.axis_size("grp")
    own_rows = samples.shape[0]
    part_rows = own_rows // PAIR
    rows = devices * part_rows
    slots = (grp // PAIR, PAIR, lax.axis_size("wide"))
    runs, width = mean_coef.shape

    arrays = (samples, inv_len.reshape(1, DIN), archive, mean_coef.T, var_coef.T)
    sent, *held = call(
        send_kernel,
        (pltpu.VMEM(slots + (part_rows, DIN), jnp.bfloat16),)
        + tuple(pltpu.VMEM(array.shape, array.dtype) for array in arrays[1:]),
        [pltpu.with_memory_space_constraint(array, pltpu.HBM) for array in arrays],
        flops=own_rows * DIN,
        in_space=pltpu.HBM,
        scratch=[pltpu.VMEM(samples.shape, samples.dtype), pltpu.SemaphoreType.DMA((5,))],
    )
    gathered = lax.all_to_all(sent.reshape(devices, part_rows, DIN), RANKS, split_axis=0, concat_axis=0, tiled=True)
    own = call(
        runs_kernel,
        pltpu.VMEM((DIN + 2 * width + NORM_ROWS, runs), jnp.bfloat16),
        held,
        flops=2 * BLOCK * runs * DIN,
    )
    peer = lax.ppermute(own, "grp", [(i, i ^ 1) for i in range(grp)])
    sums = call(
        sums_kernel,
        pltpu.VMEM((rows, 2 * width), jnp.float32),
        (gathered.reshape(rows, DIN), own, peer),
        flops=4 * rows * runs * (DIN + 4 * width),
        transcendentals=2 * rows * runs,
    )
    sums = sums.reshape(devices, part_rows, 2 * width)
    parts = lax.all_to_all(sums, RANKS, split_axis=0, concat_axis=0, tiled=True)
    return tuple(call(
        outputs_kernel,
        (pltpu.HBM((own_rows, width), jnp.float32),) * 2,
        (parts.reshape(slots + (part_rows, 2 * width)),),
        flops=parts.size,
        scratch=[pltpu.VMEM((own_rows, width), jnp.float32)] * 2 + [pltpu.SemaphoreType.DMA((2,))],
    ))


def solution(mesh):
    rows = P(AXES, None)
    return jax.shard_map(
        on_device,
        mesh=mesh,
        in_specs=(rows, rows, P(), rows, rows),
        out_specs=(rows, rows),
        check_vma=False,
    )
```

```python
import jax
import jax.numpy as jnp
from jax import lax
from jax.experimental import pallas as pl
from jax.experimental.pallas import tpu as pltpu
from jax.sharding import PartitionSpec as P

DIN = 512
AXES = ("wide", "grp")
RANKS = ("grp", "wide")
PAIR = 2
BLOCK = 128
NORM_ROWS = 16
VMEM_LIMIT = 40 * 1024 * 1024


def scaled(rows, inv_len):
    factor = inv_len * DIN ** (-0.5)
    return (rows.astype(jnp.float32) * factor).astype(jnp.bfloat16)


def prepare_kernel(
    samples_hbm, inv_len_hbm, archive_hbm, mean_hbm, var_hbm,
    sent_ref, pack_ref, samples_ref, inv_len_ref, archive_ref, coefs_ref, arrived,
):
    runs = archive_ref.shape[0]
    width = mean_hbm.shape[0]
    half = runs // 2
    copies = [
        pltpu.make_async_copy(source, target, arrived.at[number])
        for number, (source, target) in enumerate((
            (samples_hbm, samples_ref),
            (inv_len_hbm, inv_len_ref),
            (archive_hbm.at[pl.ds(0, half)], archive_ref.at[pl.ds(0, half)]),
            (archive_hbm.at[pl.ds(half, half)], archive_ref.at[pl.ds(half, half)]),
            (mean_hbm, coefs_ref.at[pl.ds(0, width)]),
            (var_hbm, coefs_ref.at[pl.ds(width, width)]),
        ))
    ]
    for copy in copies:
        copy.start()
    copies[0].wait()
    copies[1].wait()
    samp_z = scaled(samples_ref[...], inv_len_ref[...])
    samp_z = samp_z.reshape((1, PAIR, 1) + sent_ref.shape[3:])
    sent_ref[...] = jnp.broadcast_to(samp_z, sent_ref.shape)
    row = lax.broadcasted_iota(jnp.int32, (BLOCK, BLOCK), 0)
    column = lax.broadcasted_iota(jnp.int32, (BLOCK, BLOCK), 1)
    norms = []
    for part_number in range(2):
        copies[2 + part_number].wait()
        for first in range(part_number * half, (part_number + 1) * half, BLOCK):
            arch_z = scaled(archive_ref[first : first + BLOCK, :], inv_len_ref[...])
            turned = arch_z.T
            pack_ref[:DIN, first : first + BLOCK] = turned
            products = jnp.dot(arch_z, turned, preferred_element_type=jnp.float32)
            norms.append(jnp.sum(jnp.where(row == column, products, 0.0), axis=0, keepdims=True))
    copies[4].wait()
    copies[5].wait()
    coefs = coefs_ref[...]
    for first in range(0, runs, 2 * width):
        block = slice(first, first + 2 * width)
        pack_ref[DIN : DIN + 2 * width, block] = coefs[:, block].T
    rest = jnp.broadcast_to(0.5 * jnp.concatenate(norms, axis=1), (NORM_ROWS, runs))
    part_row = lax.broadcasted_iota(jnp.int32, rest.shape, 0)
    parts = jnp.zeros(rest.shape, jnp.float32)
    for number in range(3):
        part = rest.astype(jnp.bfloat16).astype(jnp.float32)
        parts = jnp.where(part_row == number, part, parts)
        rest = rest - part
    pack_ref[DIN + 2 * width :, :] = parts.astype(jnp.bfloat16)


def sums_kernel(samp_z_ref, own_ref, peer_ref, sums_ref):
    width = sums_ref.shape[1] // 2
    packs = (own_ref, peer_ref)

    def block(rows):
        samp_z = samp_z_ref[rows, :]
        wide_copy = samp_z.astype(jnp.float32)
        samp_norm = 0.5 * jnp.sum(wide_copy * wide_copy, axis=-1, keepdims=True)
        arch_z = jnp.concatenate([pack_ref[:DIN, :] for pack_ref in packs], axis=1)
        inner_prod = jnp.dot(samp_z, arch_z, preferred_element_type=jnp.float32)
        norm_parts = jnp.concatenate([pack_ref[DIN + 2 * width :, :] for pack_ref in packs], axis=1)
        arch_norm = jnp.sum(norm_parts.astype(jnp.float32), axis=0, keepdims=True)
        kernel = jnp.exp(inner_prod - samp_norm - arch_norm)
        both = jnp.concatenate([kernel, kernel * kernel], axis=0).astype(jnp.bfloat16)
        coefs = jnp.concatenate(
            [
                pack_ref[DIN : DIN + 2 * width, first : first + 2 * width]
                for pack_ref in packs
                for first in range(0, pack_ref.shape[1], 2 * width)
            ],
            axis=0,
        )
        total = jnp.dot(both, coefs, preferred_element_type=jnp.float32)
        count = samp_z.shape[0]
        lane = lax.broadcasted_iota(jnp.int32, (count, 2 * width), 1)
        sums_ref[rows, :] = jnp.where(lane < width, total[:count], total[count:])

    by_blocks(block, samp_z_ref.shape[0])


def outputs_kernel(parts_ref, mean_hbm, var_hbm, mean_ref, var_ref, written):
    width = mean_ref.shape[1]
    summed = jnp.sum(parts_ref[...], axis=(0, 2))
    summed = summed.reshape(mean_ref.shape[0], 2 * width)
    mean_ref[...] = summed[:, :width]
    mean_copy = pltpu.make_async_copy(mean_ref, mean_hbm, written.at[0])
    mean_copy.start()
    var_ref[...] = 1.0 - summed[:, width:]
    var_copy = pltpu.make_async_copy(var_ref, var_hbm, written.at[1])
    var_copy.start()
    mean_copy.wait()
    var_copy.wait()


def by_blocks(block, count):
    if count <= BLOCK:
        block(slice(None))
    else:
        @pl.loop(0, count // BLOCK)
        def _(step):
            block(pl.ds(pl.multiple_of(step * BLOCK, BLOCK), BLOCK))


def call(kernel, out_shape, inputs, flops, transcendentals=0, in_space=pltpu.VMEM, scratch=()):
    moved = sum(array.size * array.dtype.itemsize for array in inputs)
    return pl.pallas_call(
        kernel,
        out_shape=out_shape,
        in_specs=[pl.BlockSpec(memory_space=in_space)] * len(inputs),
        out_specs=jax.tree.map(lambda out: pl.BlockSpec(memory_space=out.memory_space), out_shape),
        scratch_shapes=scratch,
        cost_estimate=pl.CostEstimate(
            flops=flops, bytes_accessed=moved, transcendentals=transcendentals
        ),
        compiler_params=pltpu.CompilerParams(vmem_limit_bytes=VMEM_LIMIT),
    )(*inputs)


def on_device(samples, archive, inv_len, mean_coef, var_coef):
    devices = lax.axis_size(AXES)
    grp = lax.axis_size("grp")
    own_rows = samples.shape[0]
    part_rows = own_rows // PAIR
    rows = devices * part_rows
    slots = (grp // PAIR, PAIR, lax.axis_size("wide"))
    runs, width = mean_coef.shape

    arrays = (samples, inv_len.reshape(1, DIN), archive, mean_coef.T, var_coef.T)
    sent, own = call(
        prepare_kernel,
        (
            pltpu.VMEM(slots + (part_rows, DIN), jnp.bfloat16),
            pltpu.VMEM((DIN + 2 * width + NORM_ROWS, runs), jnp.bfloat16),
        ),
        [pltpu.with_memory_space_constraint(array, pltpu.HBM) for array in arrays],
        flops=2 * BLOCK * runs * DIN,
        in_space=pltpu.HBM,
        scratch=[pltpu.VMEM(array.shape, array.dtype) for array in arrays[:3]]
        + [pltpu.VMEM((2 * width, runs), jnp.bfloat16), pltpu.SemaphoreType.DMA((6,))],
    )
    gathered = lax.all_to_all(
        sent.reshape(devices, part_rows, DIN), RANKS, split_axis=0, concat_axis=0, tiled=True
    )
    peer = lax.ppermute(own, "grp", [(i, i ^ 1) for i in range(grp)])
    sums = call(
        sums_kernel,
        pltpu.VMEM((rows, 2 * width), jnp.float32),
        (gathered.reshape(rows, DIN), own, peer),
        flops=4 * rows * runs * (DIN + 4 * width),
        transcendentals=2 * rows * runs,
    )
    sums = sums.reshape(devices, part_rows, 2 * width)
    parts = lax.all_to_all(sums, RANKS, split_axis=0, concat_axis=0, tiled=True)
    return tuple(call(
        outputs_kernel,
        (pltpu.HBM((own_rows, width), jnp.float32),) * 2,
        (parts.reshape(slots + (part_rows, 2 * width)),),
        flops=parts.size,
        scratch=[pltpu.VMEM((own_rows, width), jnp.float32)] * 2 + [pltpu.SemaphoreType.DMA((2,))],
    ))


def solution(mesh):
    rows = P(AXES, None)
    return jax.shard_map(
        on_device,
        mesh=mesh,
        in_specs=(rows, rows, P(), rows, rows),
        out_specs=(rows, rows),
        check_vma=False,
    )
```

```python
import jax
import jax.numpy as jnp
from jax import lax
from jax.experimental import pallas as pl
from jax.experimental.pallas import tpu as pltpu
from jax.sharding import PartitionSpec as P

DIN = 512
AXES = ("wide", "grp")
RANKS = ("grp", "wide")
PAIR = 2
BLOCK = 128
NORM_ROWS = 16
LANES = 128
NORMS_WEIGHT = 400000
VMEM_LIMIT = 40 * 1024 * 1024


def scaled(rows, inv_len):
    factor = inv_len * DIN ** (-0.5)
    return (rows.astype(jnp.float32) * factor).astype(jnp.bfloat16)


def send_kernel(
    samples_hbm, inv_len_hbm, archive_hbm, mean_hbm, var_hbm,
    sent_hbm, inv_len_ref, archive_ref, mean_ref, var_ref, samples_ref, sent_ref, arrived,
):
    copies = [
        pltpu.make_async_copy(source, target, arrived.at[number])
        for number, (source, target) in enumerate((
            (samples_hbm, samples_ref),
            (inv_len_hbm, inv_len_ref),
            (archive_hbm, archive_ref),
            (mean_hbm, mean_ref),
            (var_hbm, var_ref),
            (sent_ref, sent_hbm),
        ))
    ]
    for copy in copies[:5]:
        copy.start()
    for copy in copies[:2]:
        copy.wait()
    samp_z = scaled(samples_ref[...], inv_len_ref[...])
    samp_z = samp_z.reshape((1, PAIR, 1) + sent_ref.shape[3:])
    sent_ref[...] = jnp.broadcast_to(samp_z, sent_ref.shape)
    copies[5].start()
    for copy in copies[2:]:
        copy.wait()


def runs_kernel(inv_len_ref, archive_ref, mean_ref, var_ref, pack_ref):
    runs = archive_ref.shape[0]
    width = mean_ref.shape[0]
    row = lax.broadcasted_iota(jnp.int32, (BLOCK, BLOCK), 0)
    column = lax.broadcasted_iota(jnp.int32, (BLOCK, BLOCK), 1)
    norms = []
    for first in range(0, runs, BLOCK):
        arch_z = scaled(archive_ref[first : first + BLOCK, :], inv_len_ref[...])
        turned = arch_z.T
        pack_ref[:DIN, first : first + BLOCK] = turned
        products = jnp.dot(arch_z, turned, preferred_element_type=jnp.float32)
        norms.append(jnp.sum(jnp.where(row == column, products, 0.0), axis=0, keepdims=True))
    coefs = jnp.concatenate([mean_ref[...], var_ref[...]], axis=0)
    for first in range(0, runs, 2 * width):
        block = slice(first, first + 2 * width)
        pack_ref[DIN : DIN + 2 * width, block] = coefs[:, block].T
    rest = jnp.broadcast_to(0.5 * jnp.concatenate(norms, axis=1), (NORM_ROWS, runs))
    part_row = lax.broadcasted_iota(jnp.int32, rest.shape, 0)
    parts = jnp.zeros(rest.shape, jnp.float32)
    for number in range(3):
        part = rest.astype(jnp.bfloat16).astype(jnp.float32)
        parts = jnp.where(part_row == number, part, parts)
        rest = rest - part
    pack_ref[DIN + 2 * width :, :] = parts.astype(jnp.bfloat16)


def samples_kernel(slots_ref, samp_z_ref, norm_ref):
    part_rows = slots_ref.shape[1]

    def block(first, rows):
        samp_z = slots_ref[pl.ds(first // part_rows, rows // part_rows)].reshape(rows, DIN)
        samp_z_ref[pl.ds(first, rows), :] = samp_z
        wide_copy = samp_z.astype(jnp.float32)
        norm = 0.5 * jnp.sum(wide_copy * wide_copy, axis=-1, keepdims=True)
        norm_ref[pl.ds(first, rows), :] = jnp.broadcast_to(norm, (rows, LANES))

    count = samp_z_ref.shape[0]
    if count <= BLOCK:
        block(0, count)
    else:
        @pl.loop(0, count // BLOCK)
        def _(step):
            block(pl.multiple_of(step * BLOCK, BLOCK), BLOCK)


def sums_kernel(samp_z_ref, samp_norm_ref, own_ref, peer_ref, sums_ref):
    width = sums_ref.shape[1] // 2
    packs = (own_ref, peer_ref)

    def block(rows):
        samp_z = samp_z_ref[rows, :]
        samp_norm = samp_norm_ref[rows, :1]
        arch_z = jnp.concatenate([pack_ref[:DIN, :] for pack_ref in packs], axis=1)
        inner_prod = jnp.dot(samp_z, arch_z, preferred_element_type=jnp.float32)
        norm_parts = jnp.concatenate([pack_ref[DIN + 2 * width :, :] for pack_ref in packs], axis=1)
        arch_norm = jnp.sum(norm_parts.astype(jnp.float32), axis=0, keepdims=True)
        kernel = jnp.exp(inner_prod - samp_norm - arch_norm)
        both = jnp.concatenate([kernel, kernel * kernel], axis=0).astype(jnp.bfloat16)
        coefs = jnp.concatenate(
            [
                pack_ref[DIN : DIN + 2 * width, first : first + 2 * width]
                for pack_ref in packs
                for first in range(0, pack_ref.shape[1], 2 * width)
            ],
            axis=0,
        )
        total = jnp.dot(both, coefs, preferred_element_type=jnp.float32)
        count = samp_z.shape[0]
        lane = lax.broadcasted_iota(jnp.int32, (count, 2 * width), 1)
        sums_ref[rows, :] = jnp.where(lane < width, total[:count], total[count:])

    by_blocks(block, samp_z_ref.shape[0])


def outputs_kernel(parts_ref, mean_hbm, var_hbm, mean_ref, var_ref, written):
    width = mean_ref.shape[1]
    summed = jnp.sum(parts_ref[...], axis=(0, 2))
    summed = summed.reshape(mean_ref.shape[0], 2 * width)
    mean_ref[...] = summed[:, :width]
    mean_copy = pltpu.make_async_copy(mean_ref, mean_hbm, written.at[0])
    mean_copy.start()
    var_ref[...] = 1.0 - summed[:, width:]
    var_copy = pltpu.make_async_copy(var_ref, var_hbm, written.at[1])
    var_copy.start()
    mean_copy.wait()
    var_copy.wait()


def by_blocks(block, count):
    if count <= BLOCK:
        block(slice(None))
    else:
        @pl.loop(0, count // BLOCK)
        def _(step):
            block(pl.ds(pl.multiple_of(step * BLOCK, BLOCK), BLOCK))


def call(kernel, out_shape, inputs, flops, transcendentals=0, in_space=pltpu.VMEM, scratch=()):
    moved = sum(array.size * array.dtype.itemsize for array in inputs)
    return pl.pallas_call(
        kernel,
        out_shape=out_shape,
        in_specs=[pl.BlockSpec(memory_space=in_space)] * len(inputs),
        out_specs=jax.tree.map(lambda out: pl.BlockSpec(memory_space=out.memory_space), out_shape),
        scratch_shapes=scratch,
        cost_estimate=pl.CostEstimate(
            flops=flops, bytes_accessed=moved, transcendentals=transcendentals
        ),
        compiler_params=pltpu.CompilerParams(vmem_limit_bytes=VMEM_LIMIT),
    )(*inputs)


def on_device(samples, archive, inv_len, mean_coef, var_coef):
    devices = lax.axis_size(AXES)
    grp = lax.axis_size("grp")
    own_rows = samples.shape[0]
    part_rows = own_rows // PAIR
    rows = devices * part_rows
    slots = (grp // PAIR, PAIR, lax.axis_size("wide"))
    runs, width = mean_coef.shape

    arrays = (samples, inv_len.reshape(1, DIN), archive, mean_coef.T, var_coef.T)
    sent, *held = call(
        send_kernel,
        (pltpu.HBM(slots + (part_rows, DIN), jnp.bfloat16),)
        + tuple(pltpu.VMEM(array.shape, array.dtype) for array in arrays[1:]),
        [pltpu.with_memory_space_constraint(array, pltpu.HBM) for array in arrays],
        flops=own_rows * DIN,
        in_space=pltpu.HBM,
        scratch=[
            pltpu.VMEM(samples.shape, samples.dtype),
            pltpu.VMEM(slots + (part_rows, DIN), jnp.bfloat16),
            pltpu.SemaphoreType.DMA((6,)),
        ],
    )
    gathered = lax.all_to_all(sent.reshape(devices, part_rows, DIN), RANKS, split_axis=0, concat_axis=0, tiled=True)
    own = call(
        runs_kernel,
        pltpu.VMEM((DIN + 2 * width + NORM_ROWS, runs), jnp.bfloat16),
        held,
        flops=2 * BLOCK * runs * DIN,
    )
    peer = lax.ppermute(own, "grp", [(i, i ^ 1) for i in range(grp)])
    samp_z, samp_norm = call(
        samples_kernel,
        (pltpu.VMEM((rows, DIN), jnp.bfloat16), pltpu.VMEM((rows, LANES), jnp.float32)),
        (gathered,),
        flops=NORMS_WEIGHT * rows * DIN,
    )
    sums = call(
        sums_kernel,
        pltpu.VMEM((rows, 2 * width), jnp.float32),
        (samp_z, samp_norm, own, peer),
        flops=4 * rows * runs * (DIN + 4 * width),
        transcendentals=2 * rows * runs,
    )
    sums = sums.reshape(devices, part_rows, 2 * width)
    parts = lax.all_to_all(sums, RANKS, split_axis=0, concat_axis=0, tiled=True)
    return tuple(call(
        outputs_kernel,
        (pltpu.HBM((own_rows, width), jnp.float32),) * 2,
        (parts.reshape(slots + (part_rows, 2 * width)),),
        flops=parts.size,
        scratch=[pltpu.VMEM((own_rows, width), jnp.float32)] * 2 + [pltpu.SemaphoreType.DMA((2,))],
    ))


def solution(mesh):
    rows = P(AXES, None)
    return jax.shard_map(
        on_device,
        mesh=mesh,
        in_specs=(rows, rows, P(), rows, rows),
        out_specs=(rows, rows),
        check_vma=False,
    )
```

```python
import jax
import jax.numpy as jnp
from jax import lax
from jax.experimental import pallas as pl
from jax.experimental.pallas import tpu as pltpu
from jax.sharding import PartitionSpec as P

DIN = 512
AXES = ("wide", "grp")
RANKS = ("grp", "wide")
PAIR = 2
BLOCK = 128
NORM_ROWS = 16
VMEM_LIMIT = 40 * 1024 * 1024


def scaled(rows, inv_len):
    factor = inv_len * DIN ** (-0.5)
    return (rows.astype(jnp.float32) * factor).astype(jnp.bfloat16)


def send_kernel(
    samples_hbm, inv_len_hbm, archive_hbm, mean_hbm, var_hbm,
    sent_ref, inv_len_ref, archive_ref, mean_ref, var_ref, samples_ref, arrived,
):
    runs = archive_hbm.shape[0]
    moves = [
        (samples_hbm, samples_ref),
        (inv_len_hbm, inv_len_ref),
        (mean_hbm, mean_ref),
        (var_hbm, var_ref),
    ]
    for first in range(0, runs, BLOCK):
        place = pl.ds(first, BLOCK)
        moves.append((archive_hbm.at[place], archive_ref.at[place]))
    copies = [
        pltpu.make_async_copy(source, target, arrived.at[number])
        for number, (source, target) in enumerate(moves)
    ]
    for copy in copies:
        copy.start()
    for copy in copies[:2]:
        copy.wait()
    samp_z = scaled(samples_ref[...], inv_len_ref[...])
    samp_z = samp_z.reshape((1, PAIR, 1) + sent_ref.shape[3:])
    sent_ref[...] = jnp.broadcast_to(samp_z, sent_ref.shape)
    for copy in copies[2:]:
        copy.wait()


def runs_kernel(inv_len_ref, archive_ref, mean_ref, var_ref, pack_ref):
    runs = archive_ref.shape[0]
    width = mean_ref.shape[0]
    row = lax.broadcasted_iota(jnp.int32, (BLOCK, BLOCK), 0)
    column = lax.broadcasted_iota(jnp.int32, (BLOCK, BLOCK), 1)
    norms = []
    for first in range(0, runs, BLOCK):
        arch_z = scaled(archive_ref[first : first + BLOCK, :], inv_len_ref[...])
        turned = arch_z.T
        pack_ref[:DIN, first : first + BLOCK] = turned
        products = jnp.dot(arch_z, turned, preferred_element_type=jnp.float32)
        norms.append(jnp.sum(jnp.where(row == column, products, 0.0), axis=0, keepdims=True))
    coefs = jnp.concatenate([mean_ref[...], var_ref[...]], axis=0)
    for first in range(0, runs, 2 * width):
        block = slice(first, first + 2 * width)
        pack_ref[DIN : DIN + 2 * width, block] = coefs[:, block].T
    rest = jnp.broadcast_to(0.5 * jnp.concatenate(norms, axis=1), (NORM_ROWS, runs))
    part_row = lax.broadcasted_iota(jnp.int32, rest.shape, 0)
    parts = jnp.zeros(rest.shape, jnp.float32)
    for number in range(3):
        part = rest.astype(jnp.bfloat16).astype(jnp.float32)
        parts = jnp.where(part_row == number, part, parts)
        rest = rest - part
    pack_ref[DIN + 2 * width :, :] = parts.astype(jnp.bfloat16)


def sums_kernel(samp_z_ref, own_ref, peer_ref, sums_ref):
    width = sums_ref.shape[1] // 2
    packs = (own_ref, peer_ref)

    def block(rows):
        samp_z = samp_z_ref[rows, :]
        wide_copy = samp_z.astype(jnp.float32)
        samp_norm = 0.5 * jnp.sum(wide_copy * wide_copy, axis=-1, keepdims=True)
        arch_z = jnp.concatenate([pack_ref[:DIN, :] for pack_ref in packs], axis=1)
        inner_prod = jnp.dot(samp_z, arch_z, preferred_element_type=jnp.float32)
        norm_parts = jnp.concatenate([pack_ref[DIN + 2 * width :, :] for pack_ref in packs], axis=1)
        arch_norm = jnp.sum(norm_parts.astype(jnp.float32), axis=0, keepdims=True)
        kernel = jnp.exp(inner_prod - samp_norm - arch_norm)
        both = jnp.concatenate([kernel, kernel * kernel], axis=0).astype(jnp.bfloat16)
        coefs = jnp.concatenate(
            [
                pack_ref[DIN : DIN + 2 * width, first : first + 2 * width]
                for pack_ref in packs
                for first in range(0, pack_ref.shape[1], 2 * width)
            ],
            axis=0,
        )
        total = jnp.dot(both, coefs, preferred_element_type=jnp.float32)
        count = samp_z.shape[0]
        lane = lax.broadcasted_iota(jnp.int32, (count, 2 * width), 1)
        sums_ref[rows, :] = jnp.where(lane < width, total[:count], total[count:])

    by_blocks(block, samp_z_ref.shape[0])


def outputs_kernel(parts_ref, mean_hbm, var_hbm, mean_ref, var_ref, written):
    width = mean_ref.shape[1]
    summed = jnp.sum(parts_ref[...], axis=(0, 2))
    summed = summed.reshape(mean_ref.shape[0], 2 * width)
    mean_ref[...] = summed[:, :width]
    mean_copy = pltpu.make_async_copy(mean_ref, mean_hbm, written.at[0])
    mean_copy.start()
    var_ref[...] = 1.0 - summed[:, width:]
    var_copy = pltpu.make_async_copy(var_ref, var_hbm, written.at[1])
    var_copy.start()
    mean_copy.wait()
    var_copy.wait()


def by_blocks(block, count):
    if count <= BLOCK:
        block(slice(None))
    else:
        @pl.loop(0, count // BLOCK)
        def _(step):
            block(pl.ds(pl.multiple_of(step * BLOCK, BLOCK), BLOCK))


def call(kernel, out_shape, inputs, flops, transcendentals=0, in_space=pltpu.VMEM, scratch=()):
    moved = sum(array.size * array.dtype.itemsize for array in inputs)
    return pl.pallas_call(
        kernel,
        out_shape=out_shape,
        in_specs=[pl.BlockSpec(memory_space=in_space)] * len(inputs),
        out_specs=jax.tree.map(lambda out: pl.BlockSpec(memory_space=out.memory_space), out_shape),
        scratch_shapes=scratch,
        cost_estimate=pl.CostEstimate(
            flops=flops, bytes_accessed=moved, transcendentals=transcendentals
        ),
        compiler_params=pltpu.CompilerParams(vmem_limit_bytes=VMEM_LIMIT),
    )(*inputs)


def on_device(samples, archive, inv_len, mean_coef, var_coef):
    devices = lax.axis_size(AXES)
    grp = lax.axis_size("grp")
    own_rows = samples.shape[0]
    part_rows = own_rows // PAIR
    rows = devices * part_rows
    slots = (grp // PAIR, PAIR, lax.axis_size("wide"))
    runs, width = mean_coef.shape

    arrays = (samples, inv_len.reshape(1, DIN), archive, mean_coef.T, var_coef.T)
    sent, *held = call(
        send_kernel,
        (pltpu.VMEM(slots + (part_rows, DIN), jnp.bfloat16),)
        + tuple(pltpu.VMEM(array.shape, array.dtype) for array in arrays[1:]),
        [pltpu.with_memory_space_constraint(array, pltpu.HBM) for array in arrays],
        flops=own_rows * DIN,
        in_space=pltpu.HBM,
        scratch=[pltpu.VMEM(samples.shape, samples.dtype), pltpu.SemaphoreType.DMA((4 + runs // BLOCK,))],
    )
    gathered = lax.all_to_all(sent.reshape(devices, part_rows, DIN), RANKS, split_axis=0, concat_axis=0, tiled=True)
    own = call(
        runs_kernel,
        pltpu.VMEM((DIN + 2 * width + NORM_ROWS, runs), jnp.bfloat16),
        held,
        flops=2 * BLOCK * runs * DIN,
    )
    peer = lax.ppermute(own, "grp", [(i, i ^ 1) for i in range(grp)])
    sums = call(
        sums_kernel,
        pltpu.VMEM((rows, 2 * width), jnp.float32),
        (gathered.reshape(rows, DIN), own, peer),
        flops=4 * rows * runs * (DIN + 4 * width),
        transcendentals=2 * rows * runs,
    )
    sums = sums.reshape(devices, part_rows, 2 * width)
    parts = lax.all_to_all(sums, RANKS, split_axis=0, concat_axis=0, tiled=True)
    return tuple(call(
        outputs_kernel,
        (pltpu.HBM((own_rows, width), jnp.float32),) * 2,
        (parts.reshape(slots + (part_rows, 2 * width)),),
        flops=parts.size,
        scratch=[pltpu.VMEM((own_rows, width), jnp.float32)] * 2 + [pltpu.SemaphoreType.DMA((2,))],
    ))


def solution(mesh):
    rows = P(AXES, None)
    return jax.shard_map(
        on_device,
        mesh=mesh,
        in_specs=(rows, rows, P(), rows, rows),
        out_specs=(rows, rows),
        check_vma=False,
    )
```

```python
import jax
import jax.numpy as jnp
from jax import lax
from jax.experimental import pallas as pl
from jax.experimental.pallas import tpu as pltpu
from jax.sharding import PartitionSpec as P

DIN = 512
AXES = ("wide", "grp")
RANKS = ("grp", "wide")
PAIR = 2
BLOCK = 128
NORM_ROWS = 16
VMEM_LIMIT = 40 * 1024 * 1024


def scaled(rows, inv_len):
    factor = inv_len * DIN ** (-0.5)
    return (rows.astype(jnp.float32) * factor).astype(jnp.bfloat16)


def send_kernel(
    samples_hbm, inv_len_hbm, archive_hbm, mean_hbm, var_hbm,
    sent_ref, inv_len_ref, archive_ref, mean_ref, var_ref, samples_ref, arrived,
):
    copies = [
        pltpu.make_async_copy(source, target, arrived.at[number])
        for number, (source, target) in enumerate((
            (archive_hbm, archive_ref),
            (samples_hbm, samples_ref),
            (inv_len_hbm, inv_len_ref),
            (mean_hbm, mean_ref),
            (var_hbm, var_ref),
        ))
    ]
    for copy in copies:
        copy.start()
    for copy in copies[1:3]:
        copy.wait()
    samp_z = scaled(samples_ref[...], inv_len_ref[...])
    samp_z = samp_z.reshape((1, PAIR, 1) + sent_ref.shape[3:])
    sent_ref[...] = jnp.broadcast_to(samp_z, sent_ref.shape)
    for copy in copies[:1] + copies[3:]:
        copy.wait()


def runs_kernel(inv_len_ref, archive_ref, mean_ref, var_ref, pack_ref):
    runs = archive_ref.shape[0]
    width = mean_ref.shape[0]
    row = lax.broadcasted_iota(jnp.int32, (BLOCK, BLOCK), 0)
    column = lax.broadcasted_iota(jnp.int32, (BLOCK, BLOCK), 1)
    norms = []
    for first in range(0, runs, BLOCK):
        arch_z = scaled(archive_ref[first : first + BLOCK, :], inv_len_ref[...])
        turned = arch_z.T
        pack_ref[:DIN, first : first + BLOCK] = turned
        products = jnp.dot(arch_z, turned, preferred_element_type=jnp.float32)
        norms.append(jnp.sum(jnp.where(row == column, products, 0.0), axis=0, keepdims=True))
    coefs = jnp.concatenate([mean_ref[...], var_ref[...]], axis=0)
    for first in range(0, runs, 2 * width):
        block = slice(first, first + 2 * width)
        pack_ref[DIN : DIN + 2 * width, block] = coefs[:, block].T
    rest = jnp.broadcast_to(0.5 * jnp.concatenate(norms, axis=1), (NORM_ROWS, runs))
    part_row = lax.broadcasted_iota(jnp.int32, rest.shape, 0)
    parts = jnp.zeros(rest.shape, jnp.float32)
    for number in range(3):
        part = rest.astype(jnp.bfloat16).astype(jnp.float32)
        parts = jnp.where(part_row == number, part, parts)
        rest = rest - part
    pack_ref[DIN + 2 * width :, :] = parts.astype(jnp.bfloat16)


def sums_kernel(samp_z_ref, own_ref, peer_ref, sums_ref):
    width = sums_ref.shape[1] // 2
    packs = (own_ref, peer_ref)

    def block(rows):
        samp_z = samp_z_ref[rows, :]
        wide_copy = samp_z.astype(jnp.float32)
        samp_norm = 0.5 * jnp.sum(wide_copy * wide_copy, axis=-1, keepdims=True)
        arch_z = jnp.concatenate([pack_ref[:DIN, :] for pack_ref in packs], axis=1)
        inner_prod = jnp.dot(samp_z, arch_z, preferred_element_type=jnp.float32)
        norm_parts = jnp.concatenate([pack_ref[DIN + 2 * width :, :] for pack_ref in packs], axis=1)
        arch_norm = jnp.sum(norm_parts.astype(jnp.float32), axis=0, keepdims=True)
        kernel = jnp.exp(inner_prod - samp_norm - arch_norm)
        both = jnp.concatenate([kernel, kernel * kernel], axis=0).astype(jnp.bfloat16)
        coefs = jnp.concatenate(
            [
                pack_ref[DIN : DIN + 2 * width, first : first + 2 * width]
                for pack_ref in packs
                for first in range(0, pack_ref.shape[1], 2 * width)
            ],
            axis=0,
        )
        total = jnp.dot(both, coefs, preferred_element_type=jnp.float32)
        count = samp_z.shape[0]
        lane = lax.broadcasted_iota(jnp.int32, (count, 2 * width), 1)
        sums_ref[rows, :] = jnp.where(lane < width, total[:count], total[count:])

    by_blocks(block, samp_z_ref.shape[0])


def outputs_kernel(parts_ref, mean_hbm, var_hbm, mean_ref, var_ref, written):
    width = mean_ref.shape[1]
    summed = jnp.sum(parts_ref[...], axis=(0, 2))
    summed = summed.reshape(mean_ref.shape[0], 2 * width)
    mean_ref[...] = summed[:, :width]
    mean_copy = pltpu.make_async_copy(mean_ref, mean_hbm, written.at[0])
    mean_copy.start()
    var_ref[...] = 1.0 - summed[:, width:]
    var_copy = pltpu.make_async_copy(var_ref, var_hbm, written.at[1])
    var_copy.start()
    mean_copy.wait()
    var_copy.wait()


def by_blocks(block, count):
    if count <= BLOCK:
        block(slice(None))
    else:
        @pl.loop(0, count // BLOCK)
        def _(step):
            block(pl.ds(pl.multiple_of(step * BLOCK, BLOCK), BLOCK))


def call(kernel, out_shape, inputs, flops, transcendentals=0, in_space=pltpu.VMEM, scratch=()):
    moved = sum(array.size * array.dtype.itemsize for array in inputs)
    return pl.pallas_call(
        kernel,
        out_shape=out_shape,
        in_specs=[pl.BlockSpec(memory_space=in_space)] * len(inputs),
        out_specs=jax.tree.map(lambda out: pl.BlockSpec(memory_space=out.memory_space), out_shape),
        scratch_shapes=scratch,
        cost_estimate=pl.CostEstimate(
            flops=flops, bytes_accessed=moved, transcendentals=transcendentals
        ),
        compiler_params=pltpu.CompilerParams(vmem_limit_bytes=VMEM_LIMIT),
    )(*inputs)


def on_device(samples, archive, inv_len, mean_coef, var_coef):
    devices = lax.axis_size(AXES)
    grp = lax.axis_size("grp")
    own_rows = samples.shape[0]
    part_rows = own_rows // PAIR
    rows = devices * part_rows
    slots = (grp // PAIR, PAIR, lax.axis_size("wide"))
    runs, width = mean_coef.shape

    arrays = (samples, inv_len.reshape(1, DIN), archive, mean_coef.T, var_coef.T)
    sent, *held = call(
        send_kernel,
        (pltpu.VMEM(slots + (part_rows, DIN), jnp.bfloat16),)
        + tuple(pltpu.VMEM(array.shape, array.dtype) for array in arrays[1:]),
        [pltpu.with_memory_space_constraint(array, pltpu.HBM) for array in arrays],
        flops=own_rows * DIN,
        in_space=pltpu.HBM,
        scratch=[pltpu.VMEM(samples.shape, samples.dtype), pltpu.SemaphoreType.DMA((5,))],
    )
    gathered = lax.all_to_all(sent.reshape(devices, part_rows, DIN), RANKS, split_axis=0, concat_axis=0, tiled=True)
    own = call(
        runs_kernel,
        pltpu.VMEM((DIN + 2 * width + NORM_ROWS, runs), jnp.bfloat16),
        held,
        flops=2 * BLOCK * runs * DIN,
    )
    peer = lax.ppermute(own, "grp", [(i, i ^ 1) for i in range(grp)])
    sums = call(
        sums_kernel,
        pltpu.VMEM((rows, 2 * width), jnp.float32),
        (gathered.reshape(rows, DIN), own, peer),
        flops=4 * rows * runs * (DIN + 4 * width),
        transcendentals=2 * rows * runs,
    )
    sums = sums.reshape(devices, part_rows, 2 * width)
    parts = lax.all_to_all(sums, RANKS, split_axis=0, concat_axis=0, tiled=True)
    return tuple(call(
        outputs_kernel,
        (pltpu.HBM((own_rows, width), jnp.float32),) * 2,
        (parts.reshape(slots + (part_rows, 2 * width)),),
        flops=parts.size,
        scratch=[pltpu.VMEM((own_rows, width), jnp.float32)] * 2 + [pltpu.SemaphoreType.DMA((2,))],
    ))


def solution(mesh):
    rows = P(AXES, None)
    return jax.shard_map(
        on_device,
        mesh=mesh,
        in_specs=(rows, rows, P(), rows, rows),
        out_specs=(rows, rows),
        check_vma=False,
    )
```

```python
import jax
import jax.numpy as jnp
from jax import lax
from jax.experimental import pallas as pl
from jax.experimental.pallas import tpu as pltpu
from jax.sharding import PartitionSpec as P

DIN = 512
AXES = ("wide", "grp")
RANKS = ("grp", "wide")
PAIR = 2
BLOCK = 128
NORM_ROWS = 16
VMEM_LIMIT = 40 * 1024 * 1024


def scaled(rows, inv_len):
    factor = inv_len * DIN ** (-0.5)
    return (rows.astype(jnp.float32) * factor).astype(jnp.bfloat16)


def send_kernel(
    samples_hbm, inv_len_hbm, archive_hbm, mean_hbm, var_hbm,
    sent_ref, inv_len_ref, archive_ref, mean_ref, var_ref, samples_ref, arrived,
):
    copies = [
        pltpu.make_async_copy(source, target, arrived.at[number])
        for number, (source, target) in enumerate((
            (archive_hbm, archive_ref),
            (samples_hbm, samples_ref),
            (inv_len_hbm, inv_len_ref),
            (mean_hbm, mean_ref),
            (var_hbm, var_ref),
        ))
    ]
    for copy in copies:
        copy.start()
    for copy in copies[1:3]:
        copy.wait()
    samp_z = scaled(samples_ref[...], inv_len_ref[...])
    samp_z = samp_z.reshape((1, PAIR, 1) + sent_ref.shape[3:])
    sent_ref[...] = jnp.broadcast_to(samp_z, sent_ref.shape)
    for copy in copies[:1] + copies[3:]:
        copy.wait()


def runs_kernel(inv_len_ref, archive_ref, mean_ref, var_ref, pack_ref):
    runs = archive_ref.shape[0]
    width = mean_ref.shape[0]
    coefs = jnp.concatenate([mean_ref[...], var_ref[...]], axis=0)
    for first in range(0, runs, 2 * width):
        block = slice(first, first + 2 * width)
        pack_ref[DIN : DIN + 2 * width, block] = coefs[:, block].T
    firsts = range(0, runs, BLOCK)
    arch_z = [scaled(archive_ref[first : first + BLOCK, :], inv_len_ref[...]) for first in firsts]
    turned = [rows.T for rows in arch_z]
    for first, columns in zip(firsts, turned):
        pack_ref[:DIN, first : first + BLOCK] = columns
    products = [
        jnp.dot(rows, columns, preferred_element_type=jnp.float32)
        for rows, columns in zip(arch_z, turned)
    ]
    row = lax.broadcasted_iota(jnp.int32, (BLOCK, BLOCK), 0)
    column = lax.broadcasted_iota(jnp.int32, (BLOCK, BLOCK), 1)
    norms = [
        jnp.sum(jnp.where(row == column, product, 0.0), axis=0, keepdims=True)
        for product in products
    ]
    rest = jnp.broadcast_to(0.5 * jnp.concatenate(norms, axis=1), (NORM_ROWS, runs))
    part_row = lax.broadcasted_iota(jnp.int32, rest.shape, 0)
    parts = jnp.zeros(rest.shape, jnp.float32)
    for number in range(3):
        part = rest.astype(jnp.bfloat16).astype(jnp.float32)
        parts = jnp.where(part_row == number, part, parts)
        rest = rest - part
    pack_ref[DIN + 2 * width :, :] = parts.astype(jnp.bfloat16)


def sums_kernel(samp_z_ref, own_ref, peer_ref, sums_ref):
    width = sums_ref.shape[1] // 2
    packs = (own_ref, peer_ref)

    def block(rows):
        samp_z = samp_z_ref[rows, :]
        wide_copy = samp_z.astype(jnp.float32)
        samp_norm = 0.5 * jnp.sum(wide_copy * wide_copy, axis=-1, keepdims=True)
        arch_z = jnp.concatenate([pack_ref[:DIN, :] for pack_ref in packs], axis=1)
        inner_prod = jnp.dot(samp_z, arch_z, preferred_element_type=jnp.float32)
        norm_parts = jnp.concatenate([pack_ref[DIN + 2 * width :, :] for pack_ref in packs], axis=1)
        arch_norm = jnp.sum(norm_parts.astype(jnp.float32), axis=0, keepdims=True)
        kernel = jnp.exp(inner_prod - samp_norm - arch_norm)
        both = jnp.concatenate([kernel, kernel * kernel], axis=0).astype(jnp.bfloat16)
        coefs = jnp.concatenate(
            [
                pack_ref[DIN : DIN + 2 * width, first : first + 2 * width]
                for pack_ref in packs
                for first in range(0, pack_ref.shape[1], 2 * width)
            ],
            axis=0,
        )
        total = jnp.dot(both, coefs, preferred_element_type=jnp.float32)
        count = samp_z.shape[0]
        lane = lax.broadcasted_iota(jnp.int32, (count, 2 * width), 1)
        sums_ref[rows, :] = jnp.where(lane < width, total[:count], total[count:])

    by_blocks(block, samp_z_ref.shape[0])


def outputs_kernel(parts_ref, mean_hbm, var_hbm, mean_ref, var_ref, written):
    width = mean_ref.shape[1]
    summed = jnp.sum(parts_ref[...], axis=(0, 2))
    summed = summed.reshape(mean_ref.shape[0], 2 * width)
    mean_ref[...] = summed[:, :width]
    mean_copy = pltpu.make_async_copy(mean_ref, mean_hbm, written.at[0])
    mean_copy.start()
    var_ref[...] = 1.0 - summed[:, width:]
    var_copy = pltpu.make_async_copy(var_ref, var_hbm, written.at[1])
    var_copy.start()
    mean_copy.wait()
    var_copy.wait()


def by_blocks(block, count):
    if count <= BLOCK:
        block(slice(None))
    else:
        @pl.loop(0, count // BLOCK)
        def _(step):
            block(pl.ds(pl.multiple_of(step * BLOCK, BLOCK), BLOCK))


def call(kernel, out_shape, inputs, flops, transcendentals=0, in_space=pltpu.VMEM, scratch=()):
    moved = sum(array.size * array.dtype.itemsize for array in inputs)
    return pl.pallas_call(
        kernel,
        out_shape=out_shape,
        in_specs=[pl.BlockSpec(memory_space=in_space)] * len(inputs),
        out_specs=jax.tree.map(lambda out: pl.BlockSpec(memory_space=out.memory_space), out_shape),
        scratch_shapes=scratch,
        cost_estimate=pl.CostEstimate(
            flops=flops, bytes_accessed=moved, transcendentals=transcendentals
        ),
        compiler_params=pltpu.CompilerParams(vmem_limit_bytes=VMEM_LIMIT),
    )(*inputs)


def on_device(samples, archive, inv_len, mean_coef, var_coef):
    devices = lax.axis_size(AXES)
    grp = lax.axis_size("grp")
    own_rows = samples.shape[0]
    part_rows = own_rows // PAIR
    rows = devices * part_rows
    slots = (grp // PAIR, PAIR, lax.axis_size("wide"))
    runs, width = mean_coef.shape

    arrays = (samples, inv_len.reshape(1, DIN), archive, mean_coef.T, var_coef.T)
    sent, *held = call(
        send_kernel,
        (pltpu.VMEM(slots + (part_rows, DIN), jnp.bfloat16),)
        + tuple(pltpu.VMEM(array.shape, array.dtype) for array in arrays[1:]),
        [pltpu.with_memory_space_constraint(array, pltpu.HBM) for array in arrays],
        flops=own_rows * DIN,
        in_space=pltpu.HBM,
        scratch=[pltpu.VMEM(samples.shape, samples.dtype), pltpu.SemaphoreType.DMA((5,))],
    )
    gathered = lax.all_to_all(sent.reshape(devices, part_rows, DIN), RANKS, split_axis=0, concat_axis=0, tiled=True)
    own = call(
        runs_kernel,
        pltpu.VMEM((DIN + 2 * width + NORM_ROWS, runs), jnp.bfloat16),
        held,
        flops=2 * BLOCK * runs * DIN,
    )
    peer = lax.ppermute(own, "grp", [(i, i ^ 1) for i in range(grp)])
    sums = call(
        sums_kernel,
        pltpu.VMEM((rows, 2 * width), jnp.float32),
        (gathered.reshape(rows, DIN), own, peer),
        flops=4 * rows * runs * (DIN + 4 * width),
        transcendentals=2 * rows * runs,
    )
    sums = sums.reshape(devices, part_rows, 2 * width)
    parts = lax.all_to_all(sums, RANKS, split_axis=0, concat_axis=0, tiled=True)
    return tuple(call(
        outputs_kernel,
        (pltpu.HBM((own_rows, width), jnp.float32),) * 2,
        (parts.reshape(slots + (part_rows, 2 * width)),),
        flops=parts.size,
        scratch=[pltpu.VMEM((own_rows, width), jnp.float32)] * 2 + [pltpu.SemaphoreType.DMA((2,))],
    ))


def solution(mesh):
    rows = P(AXES, None)
    return jax.shard_map(
        on_device,
        mesh=mesh,
        in_specs=(rows, rows, P(), rows, rows),
        out_specs=(rows, rows),
        check_vma=False,
    )
```

```python
import jax
import jax.numpy as jnp
from jax import lax
from jax.experimental import pallas as pl
from jax.experimental.pallas import tpu as pltpu
from jax.sharding import PartitionSpec as P

DIN = 512
AXES = ("wide", "grp")
RANKS = ("grp", "wide")
PAIR = 2
BLOCK = 128
NORM_ROWS = 16
LANES = 128
NORMS_WEIGHT = 400000
VMEM_LIMIT = 40 * 1024 * 1024


def scaled(rows, inv_len):
    factor = inv_len * DIN ** (-0.5)
    return (rows.astype(jnp.float32) * factor).astype(jnp.bfloat16)


def send_kernel(
    samples_hbm, inv_len_hbm, archive_hbm, mean_hbm, var_hbm,
    sent_hbm, inv_len_ref, archive_ref, mean_ref, var_ref, samples_ref, sent_ref, arrived,
):
    copies = [
        pltpu.make_async_copy(source, target, arrived.at[number])
        for number, (source, target) in enumerate((
            (samples_hbm, samples_ref),
            (archive_hbm, archive_ref),
            (inv_len_hbm, inv_len_ref),
            (mean_hbm, mean_ref),
            (var_hbm, var_ref),
            (sent_ref, sent_hbm),
        ))
    ]
    for copy in copies[:5]:
        copy.start()
    copies[0].wait()
    samples = samples_ref[...].reshape((1, PAIR, 1) + sent_ref.shape[3:])
    sent_ref[...] = jnp.broadcast_to(samples, sent_ref.shape)
    copies[5].start()
    for copy in copies[1:]:
        copy.wait()


def runs_kernel(inv_len_ref, archive_ref, mean_ref, var_ref, pack_ref):
    runs = archive_ref.shape[0]
    width = mean_ref.shape[0]
    row = lax.broadcasted_iota(jnp.int32, (BLOCK, BLOCK), 0)
    column = lax.broadcasted_iota(jnp.int32, (BLOCK, BLOCK), 1)
    norms = []
    for first in range(0, runs, BLOCK):
        arch_z = scaled(archive_ref[first : first + BLOCK, :], inv_len_ref[...])
        turned = arch_z.T
        pack_ref[:DIN, first : first + BLOCK] = turned
        products = jnp.dot(arch_z, turned, preferred_element_type=jnp.float32)
        norms.append(jnp.sum(jnp.where(row == column, products, 0.0), axis=0, keepdims=True))
    coefs = jnp.concatenate([mean_ref[...], var_ref[...]], axis=0)
    for first in range(0, runs, 2 * width):
        block = slice(first, first + 2 * width)
        pack_ref[DIN : DIN + 2 * width, block] = coefs[:, block].T
    rest = jnp.broadcast_to(0.5 * jnp.concatenate(norms, axis=1), (NORM_ROWS, runs))
    part_row = lax.broadcasted_iota(jnp.int32, rest.shape, 0)
    parts = jnp.zeros(rest.shape, jnp.float32)
    for number in range(3):
        part = rest.astype(jnp.bfloat16).astype(jnp.float32)
        parts = jnp.where(part_row == number, part, parts)
        rest = rest - part
    pack_ref[DIN + 2 * width :, :] = parts.astype(jnp.bfloat16)


def samples_kernel(inv_len_ref, slots_ref, samp_z_ref, norm_ref):
    part_rows = slots_ref.shape[1]

    def block(first, rows):
        samples = slots_ref[pl.ds(first // part_rows, rows // part_rows)].reshape(rows, DIN)
        samp_z = scaled(samples, inv_len_ref[...])
        samp_z_ref[pl.ds(first, rows), :] = samp_z
        wide_copy = samp_z.astype(jnp.float32)
        norm = 0.5 * jnp.sum(wide_copy * wide_copy, axis=-1, keepdims=True)
        norm_ref[pl.ds(first, rows), :] = jnp.broadcast_to(norm, (rows, LANES))

    count = samp_z_ref.shape[0]
    if count <= BLOCK:
        block(0, count)
    else:
        @pl.loop(0, count // BLOCK)
        def _(step):
            block(pl.multiple_of(step * BLOCK, BLOCK), BLOCK)


def sums_kernel(samp_z_ref, samp_norm_ref, own_ref, peer_ref, sums_ref):
    width = sums_ref.shape[1] // 2
    packs = (own_ref, peer_ref)

    def block(rows):
        samp_z = samp_z_ref[rows, :]
        samp_norm = samp_norm_ref[rows, :1]
        arch_z = jnp.concatenate([pack_ref[:DIN, :] for pack_ref in packs], axis=1)
        inner_prod = jnp.dot(samp_z, arch_z, preferred_element_type=jnp.float32)
        norm_parts = jnp.concatenate([pack_ref[DIN + 2 * width :, :] for pack_ref in packs], axis=1)
        arch_norm = jnp.sum(norm_parts.astype(jnp.float32), axis=0, keepdims=True)
        kernel = jnp.exp(inner_prod - samp_norm - arch_norm)
        both = jnp.concatenate([kernel, kernel * kernel], axis=0).astype(jnp.bfloat16)
        coefs = jnp.concatenate(
            [
                pack_ref[DIN : DIN + 2 * width, first : first + 2 * width]
                for pack_ref in packs
                for first in range(0, pack_ref.shape[1], 2 * width)
            ],
            axis=0,
        )
        total = jnp.dot(both, coefs, preferred_element_type=jnp.float32)
        count = samp_z.shape[0]
        lane = lax.broadcasted_iota(jnp.int32, (count, 2 * width), 1)
        sums_ref[rows, :] = jnp.where(lane < width, total[:count], total[count:])

    by_blocks(block, samp_z_ref.shape[0])


def outputs_kernel(parts_ref, mean_hbm, var_hbm, mean_ref, var_ref, written):
    width = mean_ref.shape[1]
    summed = jnp.sum(parts_ref[...], axis=(0, 2))
    summed = summed.reshape(mean_ref.shape[0], 2 * width)
    mean_ref[...] = summed[:, :width]
    mean_copy = pltpu.make_async_copy(mean_ref, mean_hbm, written.at[0])
    mean_copy.start()
    var_ref[...] = 1.0 - summed[:, width:]
    var_copy = pltpu.make_async_copy(var_ref, var_hbm, written.at[1])
    var_copy.start()
    mean_copy.wait()
    var_copy.wait()


def by_blocks(block, count):
    if count <= BLOCK:
        block(slice(None))
    else:
        @pl.loop(0, count // BLOCK)
        def _(step):
            block(pl.ds(pl.multiple_of(step * BLOCK, BLOCK), BLOCK))


def call(kernel, out_shape, inputs, flops, transcendentals=0, in_space=pltpu.VMEM, scratch=()):
    moved = sum(array.size * array.dtype.itemsize for array in inputs)
    return pl.pallas_call(
        kernel,
        out_shape=out_shape,
        in_specs=[pl.BlockSpec(memory_space=in_space)] * len(inputs),
        out_specs=jax.tree.map(lambda out: pl.BlockSpec(memory_space=out.memory_space), out_shape),
        scratch_shapes=scratch,
        cost_estimate=pl.CostEstimate(
            flops=flops, bytes_accessed=moved, transcendentals=transcendentals
        ),
        compiler_params=pltpu.CompilerParams(vmem_limit_bytes=VMEM_LIMIT),
    )(*inputs)


def on_device(samples, archive, inv_len, mean_coef, var_coef):
    devices = lax.axis_size(AXES)
    grp = lax.axis_size("grp")
    own_rows = samples.shape[0]
    part_rows = own_rows // PAIR
    rows = devices * part_rows
    slots = (grp // PAIR, PAIR, lax.axis_size("wide"))
    runs, width = mean_coef.shape

    arrays = (samples, inv_len.reshape(1, DIN), archive, mean_coef.T, var_coef.T)
    sent, *held = call(
        send_kernel,
        (pltpu.HBM(slots + (part_rows, DIN), jnp.bfloat16),)
        + tuple(pltpu.VMEM(array.shape, array.dtype) for array in arrays[1:]),
        [pltpu.with_memory_space_constraint(array, pltpu.HBM) for array in arrays],
        flops=own_rows * DIN,
        in_space=pltpu.HBM,
        scratch=[
            pltpu.VMEM(samples.shape, samples.dtype),
            pltpu.VMEM(slots + (part_rows, DIN), jnp.bfloat16),
            pltpu.SemaphoreType.DMA((6,)),
        ],
    )
    gathered = lax.all_to_all(sent.reshape(devices, part_rows, DIN), RANKS, split_axis=0, concat_axis=0, tiled=True)
    own = call(
        runs_kernel,
        pltpu.VMEM((DIN + 2 * width + NORM_ROWS, runs), jnp.bfloat16),
        held,
        flops=2 * BLOCK * runs * DIN,
    )
    peer = lax.ppermute(own, "grp", [(i, i ^ 1) for i in range(grp)])
    samp_z, samp_norm = call(
        samples_kernel,
        (pltpu.VMEM((rows, DIN), jnp.bfloat16), pltpu.VMEM((rows, LANES), jnp.float32)),
        (held[0], gathered),
        flops=NORMS_WEIGHT * rows * DIN,
    )
    sums = call(
        sums_kernel,
        pltpu.VMEM((rows, 2 * width), jnp.float32),
        (samp_z, samp_norm, own, peer),
        flops=4 * rows * runs * (DIN + 4 * width),
        transcendentals=2 * rows * runs,
    )
    sums = sums.reshape(devices, part_rows, 2 * width)
    parts = lax.all_to_all(sums, RANKS, split_axis=0, concat_axis=0, tiled=True)
    return tuple(call(
        outputs_kernel,
        (pltpu.HBM((own_rows, width), jnp.float32),) * 2,
        (parts.reshape(slots + (part_rows, 2 * width)),),
        flops=parts.size,
        scratch=[pltpu.VMEM((own_rows, width), jnp.float32)] * 2 + [pltpu.SemaphoreType.DMA((2,))],
    ))


def solution(mesh):
    rows = P(AXES, None)
    return jax.shard_map(
        on_device,
        mesh=mesh,
        in_specs=(rows, rows, P(), rows, rows),
        out_specs=(rows, rows),
        check_vma=False,
    )
```

```python
import jax
import jax.numpy as jnp
from jax import lax
from jax.experimental import pallas as pl
from jax.experimental.pallas import tpu as pltpu
from jax.sharding import PartitionSpec as P

DIN = 512
AXES = ("wide", "grp")
RANKS = ("grp", "wide")
PAIR = 2
BLOCK = 128
NORM_ROWS = 16
VMEM_LIMIT = 40 * 1024 * 1024


def scaled(rows, inv_len):
    factor = inv_len * DIN ** (-0.5)
    return (rows.astype(jnp.float32) * factor).astype(jnp.bfloat16)


def send_kernel(
    samples_hbm, inv_len_hbm, archive_hbm, mean_hbm, var_hbm,
    sent_ref, inv_len_ref, archive_ref, mean_ref, var_ref, samples_ref, arrived,
):
    copies = [
        pltpu.make_async_copy(source, target, arrived.at[number])
        for number, (source, target) in enumerate((
            (archive_hbm, archive_ref),
            (samples_hbm, samples_ref),
            (inv_len_hbm, inv_len_ref),
            (mean_hbm, mean_ref),
            (var_hbm, var_ref),
        ))
    ]
    for copy in copies:
        copy.start()
    for copy in copies[1:3]:
        copy.wait()
    samp_z = scaled(samples_ref[...], inv_len_ref[...])
    samp_z = samp_z.reshape((1, PAIR, 1) + sent_ref.shape[3:])
    sent_ref[...] = jnp.broadcast_to(samp_z, sent_ref.shape)
    for copy in copies[:1] + copies[3:]:
        copy.wait()


def runs_kernel(inv_len_ref, archive_ref, mean_ref, var_ref, pack_ref):
    runs = archive_ref.shape[0]
    width = mean_ref.shape[0]
    row = lax.broadcasted_iota(jnp.int32, (BLOCK, BLOCK), 0)
    column = lax.broadcasted_iota(jnp.int32, (BLOCK, BLOCK), 1)
    norms = []
    for first in range(0, runs, BLOCK):
        arch_z = scaled(archive_ref[first : first + BLOCK, :], inv_len_ref[...])
        turned = arch_z.T
        pack_ref[:DIN, first : first + BLOCK] = turned
        products = jnp.dot(arch_z, turned, preferred_element_type=jnp.float32)
        norms.append(jnp.sum(jnp.where(row == column, products, 0.0), axis=0, keepdims=True))
    coefs = jnp.concatenate([mean_ref[...], var_ref[...]], axis=0)
    for first in range(0, runs, 2 * width):
        block = slice(first, first + 2 * width)
        pack_ref[DIN : DIN + 2 * width, block] = coefs[:, block].T
    rest = jnp.broadcast_to(0.5 * jnp.concatenate(norms, axis=1), (NORM_ROWS, runs))
    part_row = lax.broadcasted_iota(jnp.int32, rest.shape, 0)
    parts = jnp.zeros(rest.shape, jnp.float32)
    for number in range(3):
        part = rest.astype(jnp.bfloat16).astype(jnp.float32)
        parts = jnp.where(part_row == number, part, parts)
        rest = rest - part
    pack_ref[DIN + 2 * width :, :] = parts.astype(jnp.bfloat16)


def sums_kernel(slots_ref, own_ref, peer_ref, sums_ref):
    width = sums_ref.shape[1] // 2
    packs = (own_ref, peer_ref)
    slots, part_rows, _ = slots_ref.shape

    def block(first, count):
        samp_z = slots_ref[pl.ds(first, count)].reshape(count * part_rows, DIN)
        wide_copy = samp_z.astype(jnp.float32)
        samp_norm = 0.5 * jnp.sum(wide_copy * wide_copy, axis=-1, keepdims=True)
        arch_z = jnp.concatenate([pack_ref[:DIN, :] for pack_ref in packs], axis=1)
        inner_prod = jnp.dot(samp_z, arch_z, preferred_element_type=jnp.float32)
        norm_parts = jnp.concatenate([pack_ref[DIN + 2 * width :, :] for pack_ref in packs], axis=1)
        arch_norm = jnp.sum(norm_parts.astype(jnp.float32), axis=0, keepdims=True)
        kernel = jnp.exp(inner_prod - samp_norm - arch_norm)
        both = jnp.concatenate([kernel, kernel * kernel], axis=0).astype(jnp.bfloat16)
        coefs = jnp.concatenate(
            [
                pack_ref[DIN : DIN + 2 * width, first : first + 2 * width]
                for pack_ref in packs
                for first in range(0, pack_ref.shape[1], 2 * width)
            ],
            axis=0,
        )
        total = jnp.dot(both, coefs, preferred_element_type=jnp.float32)
        rows = count * part_rows
        lane = lax.broadcasted_iota(jnp.int32, (rows, 2 * width), 1)
        sums = jnp.where(lane < width, total[:rows], total[rows:])
        sums_ref[pl.ds(pl.multiple_of(first * part_rows, rows), rows), :] = sums

    step = min(slots, BLOCK // part_rows)
    if step == slots:
        block(0, slots)
    else:
        @pl.loop(0, slots // step)
        def _(number):
            block(number * step, step)


def outputs_kernel(parts_ref, mean_hbm, var_hbm, mean_ref, var_ref, written):
    width = mean_ref.shape[1]
    summed = jnp.sum(parts_ref[...], axis=(0, 2))
    summed = summed.reshape(mean_ref.shape[0], 2 * width)
    mean_ref[...] = summed[:, :width]
    mean_copy = pltpu.make_async_copy(mean_ref, mean_hbm, written.at[0])
    mean_copy.start()
    var_ref[...] = 1.0 - summed[:, width:]
    var_copy = pltpu.make_async_copy(var_ref, var_hbm, written.at[1])
    var_copy.start()
    mean_copy.wait()
    var_copy.wait()


def call(kernel, out_shape, inputs, flops, transcendentals=0, in_space=pltpu.VMEM, scratch=()):
    moved = sum(array.size * array.dtype.itemsize for array in inputs)
    return pl.pallas_call(
        kernel,
        out_shape=out_shape,
        in_specs=[pl.BlockSpec(memory_space=in_space)] * len(inputs),
        out_specs=jax.tree.map(lambda out: pl.BlockSpec(memory_space=out.memory_space), out_shape),
        scratch_shapes=scratch,
        cost_estimate=pl.CostEstimate(
            flops=flops, bytes_accessed=moved, transcendentals=transcendentals
        ),
        compiler_params=pltpu.CompilerParams(vmem_limit_bytes=VMEM_LIMIT),
    )(*inputs)


def on_device(samples, archive, inv_len, mean_coef, var_coef):
    devices = lax.axis_size(AXES)
    grp = lax.axis_size("grp")
    own_rows = samples.shape[0]
    part_rows = own_rows // PAIR
    rows = devices * part_rows
    slots = (grp // PAIR, PAIR, lax.axis_size("wide"))
    runs, width = mean_coef.shape

    arrays = (samples, inv_len.reshape(1, DIN), archive, mean_coef.T, var_coef.T)
    sent, *held = call(
        send_kernel,
        (pltpu.VMEM(slots + (part_rows, DIN), jnp.bfloat16),)
        + tuple(pltpu.VMEM(array.shape, array.dtype) for array in arrays[1:]),
        [pltpu.with_memory_space_constraint(array, pltpu.HBM) for array in arrays],
        flops=own_rows * DIN,
        in_space=pltpu.HBM,
        scratch=[pltpu.VMEM(samples.shape, samples.dtype), pltpu.SemaphoreType.DMA((5,))],
    )
    gathered = lax.all_to_all(sent.reshape(devices, part_rows, DIN), RANKS, split_axis=0, concat_axis=0, tiled=True)
    own = call(
        runs_kernel,
        pltpu.VMEM((DIN + 2 * width + NORM_ROWS, runs), jnp.bfloat16),
        held,
        flops=2 * BLOCK * runs * DIN,
    )
    peer = lax.ppermute(own, "grp", [(i, i ^ 1) for i in range(grp)])
    sums = call(
        sums_kernel,
        pltpu.VMEM((rows, 2 * width), jnp.float32),
        (gathered, own, peer),
        flops=4 * rows * runs * (DIN + 4 * width),
        transcendentals=2 * rows * runs,
    )
    sums = sums.reshape(devices, part_rows, 2 * width)
    parts = lax.all_to_all(sums, RANKS, split_axis=0, concat_axis=0, tiled=True)
    return tuple(call(
        outputs_kernel,
        (pltpu.HBM((own_rows, width), jnp.float32),) * 2,
        (parts.reshape(slots + (part_rows, 2 * width)),),
        flops=parts.size,
        scratch=[pltpu.VMEM((own_rows, width), jnp.float32)] * 2 + [pltpu.SemaphoreType.DMA((2,))],
    ))


def solution(mesh):
    rows = P(AXES, None)
    return jax.shard_map(
        on_device,
        mesh=mesh,
        in_specs=(rows, rows, P(), rows, rows),
        out_specs=(rows, rows),
        check_vma=False,
    )
```

```python
import jax
import jax.numpy as jnp
from jax import lax
from jax.experimental import pallas as pl
from jax.experimental.pallas import tpu as pltpu
from jax.sharding import PartitionSpec as P

DIN = 512
AXES = ("wide", "grp")
RANKS = ("grp", "wide")
PAIR = 2
BLOCK = 128
NORM_ROWS = 16
VMEM_LIMIT = 40 * 1024 * 1024


def scaled(rows, inv_len):
    factor = inv_len * DIN ** (-0.5)
    return (rows.astype(jnp.float32) * factor).astype(jnp.bfloat16)


def send_kernel(
    samples_hbm, inv_len_hbm, archive_hbm, mean_hbm, var_hbm,
    sent_ref, inv_len_ref, archive_ref, mean_ref, var_ref, samples_ref, arrived,
):
    copies = [
        pltpu.make_async_copy(source, target, arrived.at[number])
        for number, (source, target) in enumerate((
            (archive_hbm, archive_ref),
            (mean_hbm, mean_ref),
            (var_hbm, var_ref),
            (samples_hbm, samples_ref),
            (inv_len_hbm, inv_len_ref),
        ))
    ]
    for copy in copies:
        copy.start()
    for copy in copies[3:]:
        copy.wait()
    samp_z = scaled(samples_ref[...], inv_len_ref[...])
    samp_z = samp_z.reshape((1, PAIR, 1) + sent_ref.shape[3:])
    sent_ref[...] = jnp.broadcast_to(samp_z, sent_ref.shape)
    for copy in copies[:3]:
        copy.wait()


def runs_kernel(inv_len_ref, archive_ref, mean_ref, var_ref, pack_ref):
    runs = archive_ref.shape[0]
    width = mean_ref.shape[0]
    row = lax.broadcasted_iota(jnp.int32, (BLOCK, BLOCK), 0)
    column = lax.broadcasted_iota(jnp.int32, (BLOCK, BLOCK), 1)
    norms = []
    for first in range(0, runs, BLOCK):
        arch_z = scaled(archive_ref[first : first + BLOCK, :], inv_len_ref[...])
        turned = arch_z.T
        pack_ref[:DIN, first : first + BLOCK] = turned
        products = jnp.dot(arch_z, turned, preferred_element_type=jnp.float32)
        norms.append(jnp.sum(jnp.where(row == column, products, 0.0), axis=0, keepdims=True))
    coefs = jnp.concatenate([mean_ref[...], var_ref[...]], axis=0)
    for first in range(0, runs, 2 * width):
        block = slice(first, first + 2 * width)
        pack_ref[DIN : DIN + 2 * width, block] = coefs[:, block].T
    rest = jnp.broadcast_to(0.5 * jnp.concatenate(norms, axis=1), (NORM_ROWS, runs))
    part_row = lax.broadcasted_iota(jnp.int32, rest.shape, 0)
    parts = jnp.zeros(rest.shape, jnp.float32)
    for number in range(3):
        part = rest.astype(jnp.bfloat16).astype(jnp.float32)
        parts = jnp.where(part_row == number, part, parts)
        rest = rest - part
    pack_ref[DIN + 2 * width :, :] = parts.astype(jnp.bfloat16)


def sums_kernel(slots_ref, own_ref, peer_ref, sums_ref):
    width = sums_ref.shape[1] // 2
    packs = (own_ref, peer_ref)
    slots, part_rows, _ = slots_ref.shape

    def block(first, count):
        samp_z = slots_ref[pl.ds(first, count)].reshape(count * part_rows, DIN)
        wide_copy = samp_z.astype(jnp.float32)
        samp_norm = 0.5 * jnp.sum(wide_copy * wide_copy, axis=-1, keepdims=True)
        arch_z = jnp.concatenate([pack_ref[:DIN, :] for pack_ref in packs], axis=1)
        inner_prod = jnp.dot(samp_z, arch_z, preferred_element_type=jnp.float32)
        norm_parts = jnp.concatenate([pack_ref[DIN + 2 * width :, :] for pack_ref in packs], axis=1)
        arch_norm = jnp.sum(norm_parts.astype(jnp.float32), axis=0, keepdims=True)
        kernel = jnp.exp(inner_prod - samp_norm - arch_norm)
        both = jnp.concatenate([kernel, kernel * kernel], axis=0).astype(jnp.bfloat16)
        coefs = jnp.concatenate(
            [
                pack_ref[DIN : DIN + 2 * width, first : first + 2 * width]
                for pack_ref in packs
                for first in range(0, pack_ref.shape[1], 2 * width)
            ],
            axis=0,
        )
        total = jnp.dot(both, coefs, preferred_element_type=jnp.float32)
        rows = count * part_rows
        lane = lax.broadcasted_iota(jnp.int32, (rows, 2 * width), 1)
        sums = jnp.where(lane < width, total[:rows], total[rows:])
        sums_ref[pl.ds(pl.multiple_of(first * part_rows, rows), rows), :] = sums

    step = min(slots, BLOCK // part_rows)
    if step == slots:
        block(0, slots)
    else:
        @pl.loop(0, slots // step)
        def _(number):
            block(number * step, step)


def outputs_kernel(parts_ref, mean_hbm, var_hbm, mean_ref, var_ref, written):
    width = mean_ref.shape[1]
    summed = jnp.sum(parts_ref[...], axis=(0, 2))
    summed = summed.reshape(mean_ref.shape[0], 2 * width)
    mean_ref[...] = summed[:, :width]
    mean_copy = pltpu.make_async_copy(mean_ref, mean_hbm, written.at[0])
    mean_copy.start()
    var_ref[...] = 1.0 - summed[:, width:]
    var_copy = pltpu.make_async_copy(var_ref, var_hbm, written.at[1])
    var_copy.start()
    mean_copy.wait()
    var_copy.wait()


def call(kernel, out_shape, inputs, flops, transcendentals=0, in_space=pltpu.VMEM, scratch=()):
    moved = sum(array.size * array.dtype.itemsize for array in inputs)
    return pl.pallas_call(
        kernel,
        out_shape=out_shape,
        in_specs=[pl.BlockSpec(memory_space=in_space)] * len(inputs),
        out_specs=jax.tree.map(lambda out: pl.BlockSpec(memory_space=out.memory_space), out_shape),
        scratch_shapes=scratch,
        cost_estimate=pl.CostEstimate(
            flops=flops, bytes_accessed=moved, transcendentals=transcendentals
        ),
        compiler_params=pltpu.CompilerParams(vmem_limit_bytes=VMEM_LIMIT),
    )(*inputs)


def on_device(samples, archive, inv_len, mean_coef, var_coef):
    devices = lax.axis_size(AXES)
    grp = lax.axis_size("grp")
    own_rows = samples.shape[0]
    part_rows = own_rows // PAIR
    rows = devices * part_rows
    slots = (grp // PAIR, PAIR, lax.axis_size("wide"))
    runs, width = mean_coef.shape

    arrays = (samples, inv_len.reshape(1, DIN), archive, mean_coef.T, var_coef.T)
    sent, *held = call(
        send_kernel,
        (pltpu.VMEM(slots + (part_rows, DIN), jnp.bfloat16),)
        + tuple(pltpu.VMEM(array.shape, array.dtype) for array in arrays[1:]),
        [pltpu.with_memory_space_constraint(array, pltpu.HBM) for array in arrays],
        flops=own_rows * DIN,
        in_space=pltpu.HBM,
        scratch=[pltpu.VMEM(samples.shape, samples.dtype), pltpu.SemaphoreType.DMA((5,))],
    )
    gathered = lax.all_to_all(sent.reshape(devices, part_rows, DIN), RANKS, split_axis=0, concat_axis=0, tiled=True)
    own = call(
        runs_kernel,
        pltpu.VMEM((DIN + 2 * width + NORM_ROWS, runs), jnp.bfloat16),
        held,
        flops=2 * BLOCK * runs * DIN,
    )
    peer = lax.ppermute(own, "grp", [(i, i ^ 1) for i in range(grp)])
    sums = call(
        sums_kernel,
        pltpu.VMEM((rows, 2 * width), jnp.float32),
        (gathered, own, peer),
        flops=4 * rows * runs * (DIN + 4 * width),
        transcendentals=2 * rows * runs,
    )
    sums = sums.reshape(devices, part_rows, 2 * width)
    parts = lax.all_to_all(sums, RANKS, split_axis=0, concat_axis=0, tiled=True)
    return tuple(call(
        outputs_kernel,
        (pltpu.HBM((own_rows, width), jnp.float32),) * 2,
        (parts.reshape(slots + (part_rows, 2 * width)),),
        flops=parts.size,
        scratch=[pltpu.VMEM((own_rows, width), jnp.float32)] * 2 + [pltpu.SemaphoreType.DMA((2,))],
    ))


def solution(mesh):
    rows = P(AXES, None)
    return jax.shard_map(
        on_device,
        mesh=mesh,
        in_specs=(rows, rows, P(), rows, rows),
        out_specs=(rows, rows),
        check_vma=False,
    )
```

```python
import jax
import jax.numpy as jnp
from jax import lax
from jax.experimental import pallas as pl
from jax.experimental.pallas import tpu as pltpu
from jax.sharding import PartitionSpec as P

DIN = 512
AXES = ("wide", "grp")
RANKS = ("grp", "wide")
PAIR = 2
BLOCK = 128
NORM_ROWS = 16
VMEM_LIMIT = 40 * 1024 * 1024


def scaled(rows, inv_len):
    factor = inv_len * DIN ** (-0.5)
    return (rows.astype(jnp.float32) * factor).astype(jnp.bfloat16)


def send_kernel(
    samples_hbm, inv_len_hbm, archive_hbm, mean_hbm, var_hbm,
    sent_ref, inv_len_ref, archive_ref, mean_ref, var_ref, samples_ref, arrived,
):
    copies = [
        pltpu.make_async_copy(source, target, arrived.at[number])
        for number, (source, target) in enumerate((
            (archive_hbm, archive_ref),
            (mean_hbm, mean_ref),
            (var_hbm, var_ref),
            (samples_hbm, samples_ref),
            (inv_len_hbm, inv_len_ref),
        ))
    ]
    for copy in copies:
        copy.start()
    for copy in copies[3:]:
        copy.wait()
    samp_z = scaled(samples_ref[...], inv_len_ref[...])
    samp_z = samp_z.reshape((1, PAIR, 1) + sent_ref.shape[3:])
    sent_ref[...] = jnp.broadcast_to(samp_z, sent_ref.shape)
    for copy in copies[:3]:
        copy.wait()


def runs_kernel(inv_len_ref, archive_ref, mean_ref, var_ref, pack_ref):
    runs = archive_ref.shape[0]
    width = mean_ref.shape[0]
    coefs = jnp.concatenate([mean_ref[...], var_ref[...]], axis=0)
    for first in range(0, runs, 2 * width):
        block = slice(first, first + 2 * width)
        pack_ref[DIN : DIN + 2 * width, block] = coefs[:, block].T
    firsts = range(0, runs, BLOCK)
    arch_z = [scaled(archive_ref[first : first + BLOCK, :], inv_len_ref[...]) for first in firsts]
    turned = [rows.T for rows in arch_z]
    for first, columns in zip(firsts, turned):
        pack_ref[:DIN, first : first + BLOCK] = columns
    products = [
        jnp.dot(rows, columns, preferred_element_type=jnp.float32)
        for rows, columns in zip(arch_z, turned)
    ]
    row = lax.broadcasted_iota(jnp.int32, (BLOCK, BLOCK), 0)
    column = lax.broadcasted_iota(jnp.int32, (BLOCK, BLOCK), 1)
    norms = [
        jnp.sum(jnp.where(row == column, product, 0.0), axis=0, keepdims=True)
        for product in products
    ]
    rest = jnp.broadcast_to(0.5 * jnp.concatenate(norms, axis=1), (NORM_ROWS, runs))
    part_row = lax.broadcasted_iota(jnp.int32, rest.shape, 0)
    parts = jnp.zeros(rest.shape, jnp.float32)
    for number in range(3):
        part = rest.astype(jnp.bfloat16).astype(jnp.float32)
        parts = jnp.where(part_row == number, part, parts)
        rest = rest - part
    pack_ref[DIN + 2 * width :, :] = parts.astype(jnp.bfloat16)


def sums_kernel(slots_ref, own_ref, peer_ref, sums_ref):
    width = sums_ref.shape[1] // 2
    packs = (own_ref, peer_ref)
    slots, part_rows, _ = slots_ref.shape

    def block(first, count):
        samp_z = slots_ref[pl.ds(first, count)].reshape(count * part_rows, DIN)
        wide_copy = samp_z.astype(jnp.float32)
        samp_norm = 0.5 * jnp.sum(wide_copy * wide_copy, axis=-1, keepdims=True)
        arch_z = jnp.concatenate([pack_ref[:DIN, :] for pack_ref in packs], axis=1)
        inner_prod = jnp.dot(samp_z, arch_z, preferred_element_type=jnp.float32)
        norm_parts = jnp.concatenate([pack_ref[DIN + 2 * width :, :] for pack_ref in packs], axis=1)
        arch_norm = jnp.sum(norm_parts.astype(jnp.float32), axis=0, keepdims=True)
        kernel = jnp.exp(inner_prod - samp_norm - arch_norm)
        both = jnp.concatenate([kernel, kernel * kernel], axis=0).astype(jnp.bfloat16)
        coefs = jnp.concatenate(
            [
                pack_ref[DIN : DIN + 2 * width, first : first + 2 * width]
                for pack_ref in packs
                for first in range(0, pack_ref.shape[1], 2 * width)
            ],
            axis=0,
        )
        total = jnp.dot(both, coefs, preferred_element_type=jnp.float32)
        rows = count * part_rows
        lane = lax.broadcasted_iota(jnp.int32, (rows, 2 * width), 1)
        sums = jnp.where(lane < width, total[:rows], total[rows:])
        sums_ref[pl.ds(pl.multiple_of(first * part_rows, rows), rows), :] = sums

    step = min(slots, BLOCK // part_rows)
    if step == slots:
        block(0, slots)
    else:
        @pl.loop(0, slots // step)
        def _(number):
            block(number * step, step)


def outputs_kernel(parts_ref, mean_hbm, var_hbm, mean_ref, var_ref, written):
    width = mean_ref.shape[1]
    summed = jnp.sum(parts_ref[...], axis=(0, 2))
    summed = summed.reshape(mean_ref.shape[0], 2 * width)
    mean_ref[...] = summed[:, :width]
    mean_copy = pltpu.make_async_copy(mean_ref, mean_hbm, written.at[0])
    mean_copy.start()
    var_ref[...] = 1.0 - summed[:, width:]
    var_copy = pltpu.make_async_copy(var_ref, var_hbm, written.at[1])
    var_copy.start()
    mean_copy.wait()
    var_copy.wait()


def call(kernel, out_shape, inputs, flops, transcendentals=0, in_space=pltpu.VMEM, scratch=()):
    moved = sum(array.size * array.dtype.itemsize for array in inputs)
    return pl.pallas_call(
        kernel,
        out_shape=out_shape,
        in_specs=[pl.BlockSpec(memory_space=in_space)] * len(inputs),
        out_specs=jax.tree.map(lambda out: pl.BlockSpec(memory_space=out.memory_space), out_shape),
        scratch_shapes=scratch,
        cost_estimate=pl.CostEstimate(
            flops=flops, bytes_accessed=moved, transcendentals=transcendentals
        ),
        compiler_params=pltpu.CompilerParams(vmem_limit_bytes=VMEM_LIMIT),
    )(*inputs)


def on_device(samples, archive, inv_len, mean_coef, var_coef):
    devices = lax.axis_size(AXES)
    grp = lax.axis_size("grp")
    own_rows = samples.shape[0]
    part_rows = own_rows // PAIR
    rows = devices * part_rows
    slots = (grp // PAIR, PAIR, lax.axis_size("wide"))
    runs, width = mean_coef.shape

    arrays = (samples, inv_len.reshape(1, DIN), archive, mean_coef.T, var_coef.T)
    sent, *held = call(
        send_kernel,
        (pltpu.VMEM(slots + (part_rows, DIN), jnp.bfloat16),)
        + tuple(pltpu.VMEM(array.shape, array.dtype) for array in arrays[1:]),
        [pltpu.with_memory_space_constraint(array, pltpu.HBM) for array in arrays],
        flops=own_rows * DIN,
        in_space=pltpu.HBM,
        scratch=[pltpu.VMEM(samples.shape, samples.dtype), pltpu.SemaphoreType.DMA((5,))],
    )
    gathered = lax.all_to_all(sent.reshape(devices, part_rows, DIN), RANKS, split_axis=0, concat_axis=0, tiled=True)
    own = call(
        runs_kernel,
        pltpu.VMEM((DIN + 2 * width + NORM_ROWS, runs), jnp.bfloat16),
        held,
        flops=2 * BLOCK * runs * DIN,
    )
    peer = lax.ppermute(own, "grp", [(i, i ^ 1) for i in range(grp)])
    sums = call(
        sums_kernel,
        pltpu.VMEM((rows, 2 * width), jnp.float32),
        (gathered, own, peer),
        flops=4 * rows * runs * (DIN + 4 * width),
        transcendentals=2 * rows * runs,
    )
    sums = sums.reshape(devices, part_rows, 2 * width)
    parts = lax.all_to_all(sums, RANKS, split_axis=0, concat_axis=0, tiled=True)
    return tuple(call(
        outputs_kernel,
        (pltpu.HBM((own_rows, width), jnp.float32),) * 2,
        (parts.reshape(slots + (part_rows, 2 * width)),),
        flops=parts.size,
        scratch=[pltpu.VMEM((own_rows, width), jnp.float32)] * 2 + [pltpu.SemaphoreType.DMA((2,))],
    ))


def solution(mesh):
    rows = P(AXES, None)
    return jax.shard_map(
        on_device,
        mesh=mesh,
        in_specs=(rows, rows, P(), rows, rows),
        out_specs=(rows, rows),
        check_vma=False,
    )
```

```python
import jax
import jax.numpy as jnp
from jax import lax
from jax.experimental import pallas as pl
from jax.experimental.pallas import tpu as pltpu
from jax.sharding import PartitionSpec as P

DIN = 512
AXES = ("wide", "grp")
RANKS = ("grp", "wide")
PAIR = 2
BLOCK = 128
NORM_ROWS = 16
VMEM_LIMIT = 40 * 1024 * 1024


def scaled(rows, inv_len):
    factor = inv_len * DIN ** (-0.5)
    return (rows.astype(jnp.float32) * factor).astype(jnp.bfloat16)


def send_kernel(
    samples_hbm, inv_len_hbm, archive_hbm, mean_hbm, var_hbm,
    sent_ref, inv_len_ref, archive_ref, coefs_ref, samples_ref, arrived,
):
    width = mean_hbm.shape[0]
    copies = [
        pltpu.make_async_copy(source, target, arrived.at[number])
        for number, (source, target) in enumerate((
            (archive_hbm, archive_ref),
            (mean_hbm, coefs_ref.at[pl.ds(0, width)]),
            (var_hbm, coefs_ref.at[pl.ds(width, width)]),
            (samples_hbm, samples_ref),
            (inv_len_hbm, inv_len_ref),
        ))
    ]
    for copy in copies:
        copy.start()
    for copy in copies[3:]:
        copy.wait()
    samp_z = scaled(samples_ref[...], inv_len_ref[...])
    samp_z = samp_z.reshape((1, PAIR, 1) + sent_ref.shape[3:])
    sent_ref[...] = jnp.broadcast_to(samp_z, sent_ref.shape)
    for copy in copies[:3]:
        copy.wait()


def runs_kernel(inv_len_ref, archive_ref, coefs_ref, pack_ref):
    runs = archive_ref.shape[0]
    width = coefs_ref.shape[0] // 2
    row = lax.broadcasted_iota(jnp.int32, (BLOCK, BLOCK), 0)
    column = lax.broadcasted_iota(jnp.int32, (BLOCK, BLOCK), 1)
    norms = []
    for first in range(0, runs, BLOCK):
        arch_z = scaled(archive_ref[first : first + BLOCK, :], inv_len_ref[...])
        turned = arch_z.T
        pack_ref[:DIN, first : first + BLOCK] = turned
        products = jnp.dot(arch_z, turned, preferred_element_type=jnp.float32)
        norms.append(jnp.sum(jnp.where(row == column, products, 0.0), axis=0, keepdims=True))
    coefs = coefs_ref[...]
    for first in range(0, runs, 2 * width):
        block = slice(first, first + 2 * width)
        pack_ref[DIN : DIN + 2 * width, block] = coefs[:, block].T
    rest = jnp.broadcast_to(0.5 * jnp.concatenate(norms, axis=1), (NORM_ROWS, runs))
    part_row = lax.broadcasted_iota(jnp.int32, rest.shape, 0)
    parts = jnp.zeros(rest.shape, jnp.float32)
    for number in range(3):
        part = rest.astype(jnp.bfloat16).astype(jnp.float32)
        parts = jnp.where(part_row == number, part, parts)
        rest = rest - part
    pack_ref[DIN + 2 * width :, :] = parts.astype(jnp.bfloat16)


def sums_kernel(slots_ref, own_ref, peer_ref, sums_ref):
    width = sums_ref.shape[1] // 2
    packs = (own_ref, peer_ref)
    slots, part_rows, _ = slots_ref.shape

    def block(first, count):
        samp_z = slots_ref[pl.ds(first, count)].reshape(count * part_rows, DIN)
        wide_copy = samp_z.astype(jnp.float32)
        samp_norm = 0.5 * jnp.sum(wide_copy * wide_copy, axis=-1, keepdims=True)
        arch_z = jnp.concatenate([pack_ref[:DIN, :] for pack_ref in packs], axis=1)
        inner_prod = jnp.dot(samp_z, arch_z, preferred_element_type=jnp.float32)
        norm_parts = jnp.concatenate([pack_ref[DIN + 2 * width :, :] for pack_ref in packs], axis=1)
        arch_norm = jnp.sum(norm_parts.astype(jnp.float32), axis=0, keepdims=True)
        kernel = jnp.exp(inner_prod - samp_norm - arch_norm)
        both = jnp.concatenate([kernel, kernel * kernel], axis=0).astype(jnp.bfloat16)
        coefs = jnp.concatenate(
            [
                pack_ref[DIN : DIN + 2 * width, first : first + 2 * width]
                for pack_ref in packs
                for first in range(0, pack_ref.shape[1], 2 * width)
            ],
            axis=0,
        )
        total = jnp.dot(both, coefs, preferred_element_type=jnp.float32)
        rows = count * part_rows
        lane = lax.broadcasted_iota(jnp.int32, (rows, 2 * width), 1)
        sums = jnp.where(lane < width, total[:rows], total[rows:])
        sums_ref[pl.ds(pl.multiple_of(first * part_rows, rows), rows), :] = sums

    step = min(slots, BLOCK // part_rows)
    if step == slots:
        block(0, slots)
    else:
        @pl.loop(0, slots // step)
        def _(number):
            block(number * step, step)


def outputs_kernel(parts_ref, mean_hbm, var_hbm, mean_ref, var_ref, written):
    width = mean_ref.shape[1]
    summed = jnp.sum(parts_ref[...], axis=(0, 2))
    summed = summed.reshape(mean_ref.shape[0], 2 * width)
    mean_ref[...] = summed[:, :width]
    mean_copy = pltpu.make_async_copy(mean_ref, mean_hbm, written.at[0])
    mean_copy.start()
    var_ref[...] = 1.0 - summed[:, width:]
    var_copy = pltpu.make_async_copy(var_ref, var_hbm, written.at[1])
    var_copy.start()
    mean_copy.wait()
    var_copy.wait()


def call(kernel, out_shape, inputs, flops, transcendentals=0, in_space=pltpu.VMEM, scratch=()):
    moved = sum(array.size * array.dtype.itemsize for array in inputs)
    return pl.pallas_call(
        kernel,
        out_shape=out_shape,
        in_specs=[pl.BlockSpec(memory_space=in_space)] * len(inputs),
        out_specs=jax.tree.map(lambda out: pl.BlockSpec(memory_space=out.memory_space), out_shape),
        scratch_shapes=scratch,
        cost_estimate=pl.CostEstimate(
            flops=flops, bytes_accessed=moved, transcendentals=transcendentals
        ),
        compiler_params=pltpu.CompilerParams(vmem_limit_bytes=VMEM_LIMIT),
    )(*inputs)


def on_device(samples, archive, inv_len, mean_coef, var_coef):
    devices = lax.axis_size(AXES)
    grp = lax.axis_size("grp")
    own_rows = samples.shape[0]
    part_rows = own_rows // PAIR
    rows = devices * part_rows
    slots = (grp // PAIR, PAIR, lax.axis_size("wide"))
    runs, width = mean_coef.shape

    arrays = (samples, inv_len.reshape(1, DIN), archive, mean_coef.T, var_coef.T)
    sent, *held = call(
        send_kernel,
        (pltpu.VMEM(slots + (part_rows, DIN), jnp.bfloat16),)
        + tuple(pltpu.VMEM(array.shape, array.dtype) for array in arrays[1:3])
        + (pltpu.VMEM((2 * width, runs), mean_coef.dtype),),
        [pltpu.with_memory_space_constraint(array, pltpu.HBM) for array in arrays],
        flops=own_rows * DIN,
        in_space=pltpu.HBM,
        scratch=[pltpu.VMEM(samples.shape, samples.dtype), pltpu.SemaphoreType.DMA((5,))],
    )
    gathered = lax.all_to_all(sent.reshape(devices, part_rows, DIN), RANKS, split_axis=0, concat_axis=0, tiled=True)
    own = call(
        runs_kernel,
        pltpu.VMEM((DIN + 2 * width + NORM_ROWS, runs), jnp.bfloat16),
        held,
        flops=2 * BLOCK * runs * DIN,
    )
    peer = lax.ppermute(own, "grp", [(i, i ^ 1) for i in range(grp)])
    sums = call(
        sums_kernel,
        pltpu.VMEM((rows, 2 * width), jnp.float32),
        (gathered, own, peer),
        flops=4 * rows * runs * (DIN + 4 * width),
        transcendentals=2 * rows * runs,
    )
    sums = sums.reshape(devices, part_rows, 2 * width)
    parts = lax.all_to_all(sums, RANKS, split_axis=0, concat_axis=0, tiled=True)
    return tuple(call(
        outputs_kernel,
        (pltpu.HBM((own_rows, width), jnp.float32),) * 2,
        (parts.reshape(slots + (part_rows, 2 * width)),),
        flops=parts.size,
        scratch=[pltpu.VMEM((own_rows, width), jnp.float32)] * 2 + [pltpu.SemaphoreType.DMA((2,))],
    ))


def solution(mesh):
    rows = P(AXES, None)
    return jax.shard_map(
        on_device,
        mesh=mesh,
        in_specs=(rows, rows, P(), rows, rows),
        out_specs=(rows, rows),
        check_vma=False,
    )
```

```python
import jax
import jax.numpy as jnp
from jax import lax
from jax.experimental import pallas as pl
from jax.experimental.pallas import tpu as pltpu
from jax.sharding import PartitionSpec as P

DIN = 512
AXES = ("wide", "grp")
RANKS = ("grp", "wide")
PAIR = 2
BLOCK = 128
NORM_ROWS = 16
VMEM_LIMIT = 40 * 1024 * 1024


def scaled(rows, inv_len):
    factor = inv_len * DIN ** (-0.5)
    return (rows.astype(jnp.float32) * factor).astype(jnp.bfloat16)


def send_kernel(
    samples_hbm, inv_len_hbm, archive_hbm, mean_hbm, var_hbm,
    sent_ref, inv_len_ref, archive_ref, coefs_ref, samples_ref, arrived,
):
    width = mean_hbm.shape[0]
    copies = [
        pltpu.make_async_copy(source, target, arrived.at[number])
        for number, (source, target) in enumerate((
            (archive_hbm, archive_ref),
            (mean_hbm, coefs_ref.at[pl.ds(0, width)]),
            (var_hbm, coefs_ref.at[pl.ds(width, width)]),
            (samples_hbm, samples_ref),
            (inv_len_hbm, inv_len_ref),
        ))
    ]
    for copy in copies:
        copy.start()
    for copy in copies[3:]:
        copy.wait()
    samp_z = scaled(samples_ref[...], inv_len_ref[...])
    samp_z = samp_z.reshape((1, PAIR, 1) + sent_ref.shape[3:])
    sent_ref[...] = jnp.broadcast_to(samp_z, sent_ref.shape)
    for copy in copies[:3]:
        copy.wait()


def runs_kernel(inv_len_ref, archive_ref, coefs_ref, pack_ref):
    runs = archive_ref.shape[0]
    width = coefs_ref.shape[0] // 2
    coefs = coefs_ref[...]
    for first in range(0, runs, 2 * width):
        block = slice(first, first + 2 * width)
        pack_ref[DIN : DIN + 2 * width, block] = coefs[:, block].T
    row = lax.broadcasted_iota(jnp.int32, (BLOCK, BLOCK), 0)
    column = lax.broadcasted_iota(jnp.int32, (BLOCK, BLOCK), 1)
    norms = []
    for first in range(0, runs, BLOCK):
        arch_z = scaled(archive_ref[first : first + BLOCK, :], inv_len_ref[...])
        turned = arch_z.T
        pack_ref[:DIN, first : first + BLOCK] = turned
        products = jnp.dot(arch_z, turned, preferred_element_type=jnp.float32)
        norms.append(jnp.sum(jnp.where(row == column, products, 0.0), axis=0, keepdims=True))
    rest = jnp.broadcast_to(0.5 * jnp.concatenate(norms, axis=1), (NORM_ROWS, runs))
    part_row = lax.broadcasted_iota(jnp.int32, rest.shape, 0)
    parts = jnp.zeros(rest.shape, jnp.float32)
    for number in range(3):
        part = rest.astype(jnp.bfloat16).astype(jnp.float32)
        parts = jnp.where(part_row == number, part, parts)
        rest = rest - part
    pack_ref[DIN + 2 * width :, :] = parts.astype(jnp.bfloat16)


def sums_kernel(slots_ref, own_ref, peer_ref, sums_ref):
    width = sums_ref.shape[1] // 2
    packs = (own_ref, peer_ref)
    slots, part_rows, _ = slots_ref.shape

    def block(first, count):
        samp_z = slots_ref[pl.ds(first, count)].reshape(count * part_rows, DIN)
        wide_copy = samp_z.astype(jnp.float32)
        samp_norm = 0.5 * jnp.sum(wide_copy * wide_copy, axis=-1, keepdims=True)
        arch_z = jnp.concatenate([pack_ref[:DIN, :] for pack_ref in packs], axis=1)
        inner_prod = jnp.dot(samp_z, arch_z, preferred_element_type=jnp.float32)
        norm_parts = jnp.concatenate([pack_ref[DIN + 2 * width :, :] for pack_ref in packs], axis=1)
        arch_norm = jnp.sum(norm_parts.astype(jnp.float32), axis=0, keepdims=True)
        kernel = jnp.exp(inner_prod - samp_norm - arch_norm)
        both = jnp.concatenate([kernel, kernel * kernel], axis=0).astype(jnp.bfloat16)
        coefs = jnp.concatenate(
            [
                pack_ref[DIN : DIN + 2 * width, first : first + 2 * width]
                for pack_ref in packs
                for first in range(0, pack_ref.shape[1], 2 * width)
            ],
            axis=0,
        )
        total = jnp.dot(both, coefs, preferred_element_type=jnp.float32)
        rows = count * part_rows
        lane = lax.broadcasted_iota(jnp.int32, (rows, 2 * width), 1)
        sums = jnp.where(lane < width, total[:rows], total[rows:])
        sums_ref[pl.ds(pl.multiple_of(first * part_rows, rows), rows), :] = sums

    step = min(slots, BLOCK // part_rows)
    if step == slots:
        block(0, slots)
    else:
        @pl.loop(0, slots // step)
        def _(number):
            block(number * step, step)


def outputs_kernel(parts_ref, mean_hbm, var_hbm, mean_ref, var_ref, written):
    width = mean_ref.shape[1]
    summed = jnp.sum(parts_ref[...], axis=(0, 2))
    summed = summed.reshape(mean_ref.shape[0], 2 * width)
    mean_ref[...] = summed[:, :width]
    mean_copy = pltpu.make_async_copy(mean_ref, mean_hbm, written.at[0])
    mean_copy.start()
    var_ref[...] = 1.0 - summed[:, width:]
    var_copy = pltpu.make_async_copy(var_ref, var_hbm, written.at[1])
    var_copy.start()
    mean_copy.wait()
    var_copy.wait()


def call(kernel, out_shape, inputs, flops, transcendentals=0, in_space=pltpu.VMEM, scratch=()):
    moved = sum(array.size * array.dtype.itemsize for array in inputs)
    return pl.pallas_call(
        kernel,
        out_shape=out_shape,
        in_specs=[pl.BlockSpec(memory_space=in_space)] * len(inputs),
        out_specs=jax.tree.map(lambda out: pl.BlockSpec(memory_space=out.memory_space), out_shape),
        scratch_shapes=scratch,
        cost_estimate=pl.CostEstimate(
            flops=flops, bytes_accessed=moved, transcendentals=transcendentals
        ),
        compiler_params=pltpu.CompilerParams(vmem_limit_bytes=VMEM_LIMIT),
    )(*inputs)


def on_device(samples, archive, inv_len, mean_coef, var_coef):
    devices = lax.axis_size(AXES)
    grp = lax.axis_size("grp")
    own_rows = samples.shape[0]
    part_rows = own_rows // PAIR
    rows = devices * part_rows
    slots = (grp // PAIR, PAIR, lax.axis_size("wide"))
    runs, width = mean_coef.shape

    arrays = (samples, inv_len.reshape(1, DIN), archive, mean_coef.T, var_coef.T)
    sent, *held = call(
        send_kernel,
        (pltpu.VMEM(slots + (part_rows, DIN), jnp.bfloat16),)
        + tuple(pltpu.VMEM(array.shape, array.dtype) for array in arrays[1:3])
        + (pltpu.VMEM((2 * width, runs), mean_coef.dtype),),
        [pltpu.with_memory_space_constraint(array, pltpu.HBM) for array in arrays],
        flops=own_rows * DIN,
        in_space=pltpu.HBM,
        scratch=[pltpu.VMEM(samples.shape, samples.dtype), pltpu.SemaphoreType.DMA((5,))],
    )
    gathered = lax.all_to_all(sent.reshape(devices, part_rows, DIN), RANKS, split_axis=0, concat_axis=0, tiled=True)
    own = call(
        runs_kernel,
        pltpu.VMEM((DIN + 2 * width + NORM_ROWS, runs), jnp.bfloat16),
        held,
        flops=2 * BLOCK * runs * DIN,
    )
    peer = lax.ppermute(own, "grp", [(i, i ^ 1) for i in range(grp)])
    sums = call(
        sums_kernel,
        pltpu.VMEM((rows, 2 * width), jnp.float32),
        (gathered, own, peer),
        flops=4 * rows * runs * (DIN + 4 * width),
        transcendentals=2 * rows * runs,
    )
    sums = sums.reshape(devices, part_rows, 2 * width)
    parts = lax.all_to_all(sums, RANKS, split_axis=0, concat_axis=0, tiled=True)
    return tuple(call(
        outputs_kernel,
        (pltpu.HBM((own_rows, width), jnp.float32),) * 2,
        (parts.reshape(slots + (part_rows, 2 * width)),),
        flops=parts.size,
        scratch=[pltpu.VMEM((own_rows, width), jnp.float32)] * 2 + [pltpu.SemaphoreType.DMA((2,))],
    ))


def solution(mesh):
    rows = P(AXES, None)
    return jax.shard_map(
        on_device,
        mesh=mesh,
        in_specs=(rows, rows, P(), rows, rows),
        out_specs=(rows, rows),
        check_vma=False,
    )
```
